32 devices in a mesh: dp: 8 (over z, x), mp: 4 (over y, core).
Axes of the slice: x: 2, y: 2, z: 4, core: 2. Of those that a mesh axis runs over, the one named last changes fastest.
Arguments:
- images: bfloat16 [800, 198, 384], P(('dp', 'mp')), may hold values from -6 to 6
- keep_mask: int32 [800, 198], P(('dp', 'mp')), may hold values from 0 to 1, as said below
- kept_counts: int32 [800], P(('dp', 'mp')), may hold values from 20 to 198, as said below
- pack_offsets: int32 [800], P(('dp', 'mp')), may hold values from 0 to 2027, as said below
- segment_ids: int32 [65536], P(('dp', 'mp')), may hold values from 0 to 25, as said below
- cotangent: bfloat16 [65536, 384], P(('dp', 'mp')), may hold values from -6 to 6
- attn_weight: float32 [384, 1536], P(None, ('dp', 'mp'))
- ffn_weight: float32 [2, 384, 1536], P(None, None, ('dp', 'mp'))
- up_bias: float32 [1536], P(('dp', 'mp')), may hold values from -3 to 3
- vectors: float32 [8, 384], replicated
- attn_first: float32 [384, 1536], P(None, ('dp', 'mp')), may hold values from -80 to 80
- ffn_first: float32 [2, 384, 1536], P(None, None, ('dp', 'mp')), may hold values from -64 to 64
- bias_first: float32 [1536], P(('dp', 'mp')), may hold values from -48 to 48
- vec_first: float32 [8, 384], replicated, may hold values from -160 to 160
- attn_second: float32 [384, 1536], P(None, ('dp', 'mp')), may hold values from 8.192 to 131.072
- ffn_second: float32 [2, 384, 1536], P(None, None, ('dp', 'mp')), may hold values from 5.24288 to 83.88608
- bias_second: float32 [1536], P(('dp', 'mp')), may hold values from 2.94912 to 47.18592
- vec_second: float32 [8, 384], replicated, may hold values from 32.768 to 524.288
- attn_average: float32 [384, 1536], P(None, ('dp', 'mp')), may hold values from -0.3125 to 0.3125
- ffn_average: float32 [2, 384, 1536], P(None, None, ('dp', 'mp')), may hold values from -0.3125 to 0.3125
- bias_average: float32 [1536], P(('dp', 'mp')), may hold values from -3 to 3
- vec_average: float32 [8, 384], replicated, may hold values from -0.5 to 1.5
- step: int32 [1], replicated, may hold values from 1 to 20
Outputs:
- layer_out: bfloat16 [65536, 384], P(('dp', 'mp'))
- image_grads: float32 [800, 198, 384], P(('dp', 'mp'))
- attn_grad: float32 [384, 1536], P(None, ('dp', 'mp'))
- ffn_grad: float32 [2, 384, 1536], P(None, None, ('dp', 'mp'))
- bias_grad: float32 [1536], P(('dp', 'mp'))
- vec_grad: float32 [8, 384], replicated
- attn_new: float32 [384, 1536], P(None, ('dp', 'mp'))
- ffn_new: float32 [2, 384, 1536], P(None, None, ('dp', 'mp'))
- bias_new: float32 [1536], P(('dp', 'mp'))
- vec_new: float32 [8, 384], replicated
- attn_first_new: float32 [384, 1536], P(None, ('dp', 'mp'))
- ffn_first_new: float32 [2, 384, 1536], P(None, None, ('dp', 'mp'))
- bias_first_new: float32 [1536], P(('dp', 'mp'))
- vec_first_new: float32 [8, 384], replicated
- attn_second_new: float32 [384, 1536], P(None, ('dp', 'mp'))
- ffn_second_new: float32 [2, 384, 1536], P(None, None, ('dp', 'mp'))
- bias_second_new: float32 [1536], P(('dp', 'mp'))
- vec_second_new: float32 [8, 384], replicated
- attn_average_new: float32 [384, 1536], P(None, ('dp', 'mp'))
- ffn_average_new: float32 [2, 384, 1536], P(None, None, ('dp', 'mp'))
- bias_average_new: float32 [1536], P(('dp', 'mp'))
- vec_average_new: float32 [8, 384], replicated
The draws below stay inside these ranges and needn't reach their ends.
Inputs may be any that keep to these rules, and one draw needn't show every extreme that they name: `keep_mask`: each image keeps exactly kept_counts of its tokens, its first two among them. `kept_counts`: on every device the last image keeps 20 tokens and one of the others keeps all 198; the counts of a device's 25 images sum to 2047. `pack_offsets`: A device's images fill its pack in order from row 0 without gaps: an image's offset is the sum of the kept counts of the device's earlier images. `segment_ids`: each pack row carries the number of the image that fills it; 25 marks the last row of every pack, which is unused.
All inputs are finite; a program needn't handle non-finite values.
Results may differ from the reference program's by a relative error of at most 0.01.
The reference program's roundings to bfloat16 on the way count: a program that leaves them out, or rounds other values in their place, can miss the bound.
Values may be sent and summed in bfloat16 or wider, within the bound.
No kernel may reach another device: no remote copies, remote signals or barrier semaphores. Data moves between devices by JAX's collectives and lax.ppermute only.
A program may use at most 320 MiB of HBM per device.

```python
import math
import jax
import jax.numpy as jnp
from jax import lax

D = 384
HEADS = 6
HEAD = 64
FF = 1536
NTOK = 198
MIN_KEEP = 20
PACK = 2048
IMG_DEV = 25
TOKENS = 65536
IMAGES = 800
N_DP = 8
N_MP = 4


def count_table(key):
    groups = IMAGES // IMG_DEV
    middle = IMG_DEV - 2
    base = jax.random.fold_in(key, 7001)
    cube = jax.random.randint(base, (groups, middle), 0, 101).astype(jnp.int32)
    wanted = (MIN_KEEP + (NTOK - MIN_KEEP) * cube * cube * cube // 1000000).astype(jnp.int32)
    target = PACK - 1 - MIN_KEEP - NTOK
    after = jnp.broadcast_to((middle - 1 - jnp.arange(middle, dtype=jnp.int32))[:, None], (middle, groups)).astype(jnp.int32)

    def place(remain, column_data):
        want, later = column_data
        lower = jnp.maximum(MIN_KEEP, remain - NTOK * later)
        upper = jnp.minimum(NTOK, remain - MIN_KEEP * later)
        take = jnp.clip(want, lower, upper).astype(jnp.int32)
        return ((remain - take).astype(jnp.int32), take)
    start = jnp.full((groups,), target, jnp.int32)
    _, taken = lax.scan(place, start, (wanted.T, after))
    first = jnp.full((groups, 1), NTOK, jnp.int32)
    head = jnp.concatenate([first, taken.T.astype(jnp.int32)], axis=1).astype(jnp.int32)
    noise = jax.random.randint(jax.random.fold_in(key, 7006), (groups, IMG_DEV - 1), 0, 1048576).astype(jnp.int32)
    column = jnp.arange(IMG_DEV - 1, dtype=jnp.int32)[None, :]
    order = jnp.argsort(noise * IMG_DEV + column, axis=1).astype(jnp.int32)
    shuffled = jnp.take_along_axis(head, order, axis=1).astype(jnp.int32)
    last = jnp.full((groups, 1), MIN_KEEP, jnp.int32)
    return jnp.concatenate([shuffled, last], axis=1).astype(jnp.int32)


def draw_kept_counts(key, part):
    return count_table(key).reshape(IMAGES)


def draw_pack_offsets(key, part):
    counts = count_table(key)
    return (jnp.cumsum(counts, axis=1) - counts).astype(jnp.int32).reshape(IMAGES)


def draw_segment_ids(key, part):
    counts = count_table(key)
    ends = jnp.cumsum(counts, axis=1).astype(jnp.int32)
    row = jnp.arange(PACK, dtype=jnp.int32)[None, :, None]
    owner = jnp.sum((row >= ends[:, None, :]).astype(jnp.int32), axis=2)
    return owner.reshape(TOKENS).astype(jnp.int32)


def draw_keep_mask(key, part):
    counts = count_table(key).reshape(IMAGES)
    noise = jax.random.randint(jax.random.fold_in(key, 7002), (IMAGES, NTOK), 0, 1048576).astype(jnp.int32)
    position = jnp.arange(NTOK, dtype=jnp.int32)[None, :]
    order_key = jnp.where(position < 2, -1, noise) * NTOK + position
    order = jnp.argsort(order_key, axis=1)
    ranks = jnp.argsort(order, axis=1)
    return (ranks < counts[:, None]).astype(jnp.int32)


def draw_attn_weight(key, part):
    inner = jax.random.fold_in(key, 7003)
    column = jnp.arange(4 * D)[None, :]
    scale = jnp.where(column < 3 * D, 1.0, 4.0) / math.sqrt(D)
    base = jax.random.normal(inner, (D, 4 * D), jnp.float32)
    return (base * scale).astype(jnp.float32)


def draw_ffn_weight(key, part):
    inner = jax.random.fold_in(key, 7004)
    slab = jnp.arange(2)[:, None, None]
    scale = jnp.where(slab == 0, 1.0 / math.sqrt(D), 2.0 / math.sqrt(FF))
    base = jax.random.normal(inner, (2, D, FF), jnp.float32)
    return (base * scale).astype(jnp.float32)


def draw_vectors(key, part):
    inner = jax.random.fold_in(key, 7005)
    first, second = jax.random.split(inner)
    row = jnp.arange(8)[:, None]
    is_gain = (row == 0) | (row == 5)
    gains = jax.random.uniform(first, (8, D), jnp.float32, 0.6, 1.4)
    shifts = 0.3 * jax.random.normal(second, (8, D), jnp.float32)
    return jnp.where(is_gain, gains, shifts).astype(jnp.float32)


def block_levels(rng, dims, cuts, smallest, top_value):
    factor_of, own = 1.0, jax.random.fold_in(rng, 6)
    for dim, shards_of in cuts:
        heights = jnp.exp(jax.random.uniform(jax.random.fold_in(own, dim), (shards_of,), jnp.float32, smallest / len(cuts), top_value / len(cuts)))
        factor_of = factor_of * jnp.repeat(heights, dims[dim] // shards_of).reshape([-1 if axis == dim else 1 for axis in range(len(dims))])
    return factor_of


def normal_values(key, dims, deviation, limit, pieces=(), kind=jnp.bfloat16):
    entries = jax.random.normal(key, dims, jnp.float32) * deviation
    if len(pieces) > 0:
        entries = block_levels(key, dims, pieces, -0.22, 0.18) * entries
    return jnp.clip(entries, min=-limit, max=limit).astype(kind)


def setup_inputs(seed: int = 0) -> dict:
    splits = jax.random.split(jax.random.key(seed), 24)
    images = normal_values(splits[0], (IMAGES, NTOK, D), 1.0, 6.0, ((0, 32),))
    keep_mask = draw_keep_mask(jax.random.fold_in(splits[23], 71), 0)
    kept_counts = draw_kept_counts(jax.random.fold_in(splits[23], 71), 0)
    pack_offsets = draw_pack_offsets(jax.random.fold_in(splits[23], 71), 0)
    segment_ids = draw_segment_ids(jax.random.fold_in(splits[23], 71), 0)
    cotangent = normal_values(splits[5], (TOKENS, D), 1.0, 6.0, ((0, 32),))
    attn_weight = draw_attn_weight(jax.random.fold_in(splits[23], 71), 0)
    ffn_weight = draw_ffn_weight(jax.random.fold_in(splits[23], 71), 0)
    up_bias = normal_values(splits[8], (FF,), 0.5, 3.0, ((0, 32),), jnp.float32)
    vectors = draw_vectors(jax.random.fold_in(splits[23], 71), 0)
    attn_first = normal_values(splits[10], (D, 4 * D), (0.055 * TOKENS ** 0.5), 80.0, ((1, 32),), jnp.float32)
    ffn_first = normal_values(splits[11], (2, D, FF), (0.044 * TOKENS ** 0.5), 64.0, ((2, 32),), jnp.float32)
    bias_first = normal_values(splits[12], (FF,), (0.033 * TOKENS ** 0.5), 48.0, ((0, 32),), jnp.float32)
    vec_first = normal_values(splits[13], (8, D), (0.11 * TOKENS ** 0.5), 160.0, (), jnp.float32)
    attn_second = jnp.clip(jnp.exp(math.log(131.072) - 2.7725887 * jax.random.uniform(splits[14], (D, 4 * D), jnp.float32) ** block_levels(splits[14], (D, 4 * D), ((1, 32),), -0.2, 0.2)), 8.192, 131.072)
    ffn_second = jnp.clip(jnp.exp(math.log(83.88608) - 2.7725887 * jax.random.uniform(splits[15], (2, D, FF), jnp.float32) ** block_levels(splits[15], (2, D, FF), ((2, 32),), -0.2, 0.2)), 5.24288, 83.88608)
    bias_second = jnp.clip(jnp.exp(math.log(47.18592) - 2.7725887 * jax.random.uniform(splits[16], (FF,), jnp.float32) ** block_levels(splits[16], (FF,), ((0, 32),), -0.2, 0.2)), 2.94912, 47.18592)
    vec_second = jnp.clip(jnp.exp(jax.random.uniform(splits[17], (8, D), jnp.float32, math.log(32.768), math.log(524.288))), 32.768, 524.288)
    attn_average = normal_values(splits[18], (D, 4 * D), D ** -0.5, 0.3125, ((1, 32),), jnp.float32)
    ffn_average = normal_values(splits[19], (2, D, FF), D ** -0.5, 0.3125, ((2, 32),), jnp.float32)
    bias_average = normal_values(splits[20], (FF,), 0.5, 3.0, ((0, 32),), jnp.float32)
    vec_average = jnp.clip(jax.random.uniform(splits[21], (8, D), jnp.float32, -0.5, 1.5), -0.5, 1.5)
    step = jax.random.randint(splits[22], (1,), 1, 21).astype(jnp.int32)
    return dict(images=images, keep_mask=keep_mask, kept_counts=kept_counts, pack_offsets=pack_offsets, segment_ids=segment_ids, cotangent=cotangent, attn_weight=attn_weight, ffn_weight=ffn_weight, up_bias=up_bias, vectors=vectors, attn_first=attn_first, ffn_first=ffn_first, bias_first=bias_first, vec_first=vec_first, attn_second=attn_second, ffn_second=ffn_second, bias_second=bias_second, vec_second=vec_second, attn_average=attn_average, ffn_average=ffn_average, bias_average=bias_average, vec_average=vec_average, step=step)


HIGH = lax.Precision.HIGHEST
NORM_EPS = 1e-06
BETA_ONE = 0.9
BETA_TWO = 0.999
ADAM_EPS = 1e-08
MATRIX_RATE = 0.05
VECTOR_RATE = 0.2
WEIGHT_DECAY = 0.05
AVERAGE_DECAY = 0.8

@jax.custom_vjp
def low(v):
    return lax.optimization_barrier(v.astype(jnp.bfloat16)).astype(jnp.float32)

@jax.custom_vjp
def low_back(v):
    return v

def low_keep(v):
    return (low(v), None)

def low_pass(kept, grad):
    return (grad,)

def back_keep(v):
    return (v, None)

def back_low(kept, grad):
    return (low(grad),)
low.defvjp(low_keep, low_pass)
low_back.defvjp(back_keep, back_low)

def layer_norm(values, gain, shift):
    centre = lax.optimization_barrier(jnp.mean(values, axis=-1, keepdims=True))
    centred = values - centre
    spread = lax.optimization_barrier(jnp.mean(centred * centred, axis=-1, keepdims=True))
    return centred * lax.rsqrt(spread + NORM_EPS) * gain + shift

def pack_rows(keep_mask, kept_counts, pack_offsets, segment_ids):
    images_here = keep_mask.shape[0]
    length = keep_mask.shape[1]
    ranks = (jnp.cumsum(keep_mask, axis=1) - 1).astype(jnp.int32)
    slots = jnp.where(keep_mask > 0, ranks, length).astype(jnp.int32)
    image_row = jnp.broadcast_to(jnp.arange(images_here, dtype=jnp.int32)[:, None], keep_mask.shape)
    token_col = jnp.broadcast_to(jnp.arange(length, dtype=jnp.int32)[None, :], keep_mask.shape)
    position = jnp.zeros((images_here, length + 1), jnp.int32).at[image_row, slots].set(token_col)
    owner = jnp.minimum(segment_ids, images_here - 1).astype(jnp.int32)
    local = (jnp.arange(segment_ids.shape[0], dtype=jnp.int32) - pack_offsets[owner]).astype(jnp.int32)
    valid = (segment_ids < images_here) & (local >= 0) & (local < kept_counts[owner])
    local = jnp.clip(local, 0, length - 1).astype(jnp.int32)
    source = (owner * length + position[owner, local]).astype(jnp.int32)
    return (source, valid)

def gelu_exact(values):
    return jax.nn.gelu(values, approximate=False)

def pack_layer(images_here, keep_mask, kept_counts, pack_offsets, segment_ids, attn_weight, ffn_weight, up_bias, vectors):
    width = images_here.shape[2]
    source, valid = pack_rows(keep_mask, kept_counts, pack_offsets, segment_ids)
    inputs = jnp.where(valid[:, None], images_here.reshape(-1, width)[source], 0.0)
    normed = low(layer_norm(inputs, vectors[0], vectors[1]))
    weights = low(attn_weight)
    qkv_bias = jnp.concatenate([vectors[2], jnp.zeros_like(vectors[2]), vectors[3]])
    qkv = low(low_back(jnp.dot(normed, weights[:, :3 * width], precision=HIGH) + qkv_bias))
    rows = qkv.shape[0]
    query = qkv[:, :width].reshape(rows, HEADS, HEAD)
    key_rows = qkv[:, width:2 * width].reshape(rows, HEADS, HEAD)
    value = qkv[:, 2 * width:].reshape(rows, HEADS, HEAD)
    raw = low_back(jnp.einsum('qhd,khd->hqk', query, key_rows, precision=HIGH))
    same = segment_ids[:, None] == segment_ids[None, :]
    scores = jnp.where(same[None], raw * (1.0 / math.sqrt(HEAD)), -1000000000.0)
    top = lax.optimization_barrier(jnp.max(scores, axis=-1, keepdims=True))
    expo = jnp.exp(scores - top)
    probs = expo / lax.optimization_barrier(jnp.sum(expo, axis=-1, keepdims=True))
    mixed = jnp.einsum('hqk,khd->qhd', low(probs), value, precision=HIGH)
    mixed = low(low_back(mixed.reshape(rows, width)))
    branch = low_back(jnp.dot(mixed, weights[:, 3 * width:], precision=HIGH)) + vectors[4]
    middle = inputs + branch
    normed_two = low(layer_norm(middle, vectors[5], vectors[6]))
    ffn = low(ffn_weight)
    hidden_in = low_back(jnp.dot(normed_two, ffn[0], precision=HIGH)) + low(up_bias)
    hidden = low(gelu_exact(hidden_in))
    down = low_back(jnp.dot(hidden, ffn[1].T, precision=HIGH)) + vectors[7]
    return jnp.where(valid[:, None], middle + down, 0.0)

def forward(images, attn_weight, ffn_weight, up_bias, vectors, keep_mask, kept_counts, pack_offsets, segment_ids):
    groups = N_DP * N_MP
    layer = jax.checkpoint(pack_layer)

    def one_pack(carry, slabs):
        result = layer(slabs[0], slabs[1], slabs[2], slabs[3], slabs[4], attn_weight, ffn_weight, up_bias, vectors)
        return (carry, result)
    slabs = (images.reshape(groups, IMG_DEV, NTOK, D), keep_mask.reshape(groups, IMG_DEV, NTOK), kept_counts.reshape(groups, IMG_DEV), pack_offsets.reshape(groups, IMG_DEV), segment_ids.reshape(groups, PACK))
    _, outputs = lax.scan(one_pack, jnp.zeros((), jnp.float32), slabs)
    return outputs.reshape(TOKENS, D)

def adamw(weight, grad, first, second, average, count, rate, decay):
    first_new = BETA_ONE * first + (1.0 - BETA_ONE) * grad
    second_new = BETA_TWO * second + (1.0 - BETA_TWO) * grad * grad
    first_hat = first_new / (1.0 - jnp.power(BETA_ONE, count))
    second_hat = second_new / (1.0 - jnp.power(BETA_TWO, count))
    weight_new = weight - rate * (first_hat / (jnp.sqrt(second_hat) + ADAM_EPS) + decay * weight)
    average_new = AVERAGE_DECAY * average + (1.0 - AVERAGE_DECAY) * weight_new
    return (weight_new, first_new, second_new, average_new)

def reference(images, keep_mask, kept_counts, pack_offsets, segment_ids, cotangent, attn_weight, ffn_weight, up_bias, vectors, attn_first, ffn_first, bias_first, vec_first, attn_second, ffn_second, bias_second, vec_second, attn_average, ffn_average, bias_average, vec_average, step):

    def run(image_values, attn_values, ffn_values, bias_values, vector_values):
        return forward(image_values, attn_values, ffn_values, bias_values, vector_values, keep_mask, kept_counts, pack_offsets, segment_ids)
    layer_out, pull = jax.vjp(run, images.astype(jnp.float32), attn_weight, ffn_weight, up_bias, vectors)
    image_grads, attn_grad, ffn_grad, bias_grad, vec_grad = pull(cotangent.astype(jnp.float32))
    count = step[0].astype(jnp.float32)
    attn_up = adamw(attn_weight, attn_grad, attn_first, attn_second, attn_average, count, MATRIX_RATE, WEIGHT_DECAY)
    ffn_up = adamw(ffn_weight, ffn_grad, ffn_first, ffn_second, ffn_average, count, MATRIX_RATE, WEIGHT_DECAY)
    bias_up = adamw(up_bias, bias_grad, bias_first, bias_second, bias_average, count, VECTOR_RATE, 0.0)
    vec_up = adamw(vectors, vec_grad, vec_first, vec_second, vec_average, count, VECTOR_RATE, 0.0)
    return (layer_out.astype(jnp.bfloat16), image_grads, attn_grad, ffn_grad, bias_grad, vec_grad, attn_up[0], ffn_up[0], bias_up[0], vec_up[0], attn_up[1], ffn_up[1], bias_up[1], vec_up[1], attn_up[2], ffn_up[2], bias_up[2], vec_up[2], attn_up[3], ffn_up[3], bias_up[3], vec_up[3])
```

```python
import functools
import math

import jax
import jax.numpy as jnp
from jax import lax
from jax.experimental import pallas as pl
from jax.experimental.pallas import tpu as pltpu
from jax.sharding import PartitionSpec as P

HEADS = 6
HEAD = 64
PAIR = 2 * HEAD
PAIRS = HEADS // 2
BLK = 128
REACH = 5
EXCLUDED = -8.0e9
INCLUDED = 3.0e38

NORM_EPS = 1e-06
BETA_ONE = 0.9
BETA_TWO = 0.999
ADAM_EPS = 1e-08
MATRIX_RATE = 0.05
VECTOR_RATE = 0.2
WEIGHT_DECAY = 0.05
AVERAGE_DECAY = 0.8

LOG2E = 1.4426950408889634
SCORE_LOG2 = LOG2E / math.sqrt(HEAD)
SCALE = 1.0 / math.sqrt(HEAD)

f32 = jnp.float32
bf16 = jnp.bfloat16
NN = (((1,), (0,)), ((), ()))
NT = (((1,), (1,)), ((), ()))
TN = (((0,), (0,)), ((), ()))
VM = pl.BlockSpec(memory_space=pltpu.VMEM)
SM = pl.BlockSpec(memory_space=pltpu.SMEM)
S = jax.ShapeDtypeStruct


def dot(left, right, dims=NN):
    return lax.dot_general(left, right, dims, preferred_element_type=f32)


def kernel_call(body, ins, outs, scratch=(), flops=0, moved=0, name=None):
    return pl.pallas_call(
        body,
        out_shape=outs,
        in_specs=ins,
        out_specs=tuple(VM for _ in outs),
        scratch_shapes=list(scratch),
        compiler_params=pltpu.CompilerParams(vmem_limit_bytes=58 * 2**20),
        cost_estimate=pl.CostEstimate(flops=flops, bytes_accessed=moved, transcendentals=0),
        name=name,
    )


def row_sums(values):
    rows, width = values.shape
    return jnp.sum(values.reshape(rows // 8, 8, width), axis=0)


def norm_parts(values):
    scale = 1.0 / values.shape[-1]
    centre = jnp.sum(values, axis=-1, keepdims=True) * scale
    centred = values - centre
    spread = jnp.sum(centred * centred, axis=-1, keepdims=True) * scale
    inverse = lax.rsqrt(spread + NORM_EPS)
    return centred * inverse, inverse


def norm_back(unit, inverse, gain, grad):
    scale = 1.0 / unit.shape[-1]
    scaled = grad * gain
    mean = jnp.sum(scaled, axis=-1, keepdims=True) * scale
    along = jnp.sum(scaled * unit, axis=-1, keepdims=True) * scale
    return inverse * (scaled - mean - unit * along)


def tile_rows(count, size):
    return pl.ds(pl.multiple_of(count * size, size), size)


def pack_body(win, offs, images, keep, seg_rows, vec, packed, normed, normed_t, seg_cols, acc, slots):
    images_here, length = keep.shape
    rows, width = packed.shape
    before = lax.broadcasted_iota(jnp.int32, (length, length), 0)
    after = lax.broadcasted_iota(jnp.int32, (length, length), 1)
    tri = jnp.where(before <= after, 1.0, 0.0).astype(bf16)
    kept = keep[...]
    ranks = dot(kept.astype(f32).astype(bf16), tri).astype(jnp.int32) - 1
    slots[...] = jnp.where(kept > 0, ranks, -4 * win)
    acc[0:8, :] = jnp.zeros((8, width), f32)
    place = lax.broadcasted_iota(jnp.int32, (win, length), 0)

    def one_image(i, carry):
        base = pl.multiple_of((offs[i] // 8) * 8, 8)
        shift = offs[i] - base
        chosen = jnp.where(place == slots[pl.ds(i, 1), :] + shift, 1.0, 0.0).astype(bf16)
        moved = dot(chosen, images[i])
        acc[pl.ds(base, 8), :] += moved[0:8]
        acc[pl.ds(base + 8, win - 8), :] = moved[8:]
        return carry

    lax.fori_loop(0, images_here, one_image, 0)

    def one_tile(i, carry):
        sl = tile_rows(i, 256)
        values = acc[sl, :]
        packed[sl, :] = values.astype(bf16)
        unit, _ = norm_parts(values)
        low = (unit * vec[0:1, :] + vec[1:2, :]).astype(bf16)
        normed[sl, :] = low
        normed_t[:, sl] = low.T
        return carry

    lax.fori_loop(0, rows // 256, one_tile, 0)

    def one_block(j, carry):
        line = seg_rows[pl.ds(j, 1), :]
        seg_cols[tile_rows(j, BLK), :] = jnp.broadcast_to(line, (BLK, BLK)).T
        return carry

    lax.fori_loop(0, rows // BLK, one_block, 0)


def pack_call(images, keep, offs, seg_rows, vec, rows):
    images_here, length, width = images.shape
    win = (length + 7 + 7) // 8 * 8
    return kernel_call(
        functools.partial(pack_body, win),
        [SM, VM, VM, VM, VM],
        (S((rows, width), bf16), S((rows, width), bf16), S((width, rows), bf16), S((rows, BLK), jnp.int32)),
        [pltpu.VMEM((rows + win, width), f32), pltpu.VMEM((images_here, length), jnp.int32)],
        flops=2 * images_here * win * length * width,
        moved=images.size * 2 + rows * width * 6,
        name="pack",
    )(offs, images, keep, seg_rows, vec)


def window(seg, offs, counts, j, images_here, rows):
    first = seg[j * BLK]
    last = seg[j * BLK + BLK - 1]
    used = last < images_here
    last_here = jnp.where(used, last, 0)
    low = offs[first] // BLK
    end = jnp.where(used, offs[last_here] + counts[last_here], rows)
    return low, (end + BLK - 1) // BLK - low


def masked_pair(pair):
    lane = lax.broadcasted_iota(jnp.int32, pair.shape, 1)
    none = jnp.zeros_like(pair)
    return jnp.concatenate([jnp.where(lane < HEAD, pair, none), jnp.where(lane >= HEAD, pair, none)], axis=0)


def limits(seg_rows, seg_cols, j, keys):
    same = seg_cols[keys, :] == seg_rows[pl.ds(j, 1), :]
    lim = jnp.where(same, INCLUDED, EXCLUDED)
    return jnp.concatenate([lim, lim], axis=1)


def over_windows(seg, offs, counts, images_here, rows, block):
    def one(j, carry):
        low, size = window(seg, offs, counts, j, images_here, rows)
        for n in range(1, REACH + 1):

            @pl.when(size == n)
            def _():
                block(j, pl.ds(pl.multiple_of(low * BLK, BLK), n * BLK))

        return carry

    lax.fori_loop(0, rows // BLK, one, 0)


def attend_body(seg, offs, counts, normed, w_t, bias, seg_rows, seg_cols, qkv, mixed_t, stats, value_t):
    rows, width = normed.shape
    images_here = offs.shape[0]

    def project(i, carry):
        sl = tile_rows(i, 512)
        low = (dot(normed[sl, :], w_t[...], NT) + bias[...]).astype(bf16)
        qkv[sl, :] = low
        value_t[:, sl] = low[:, 2 * width :].T
        return carry

    lax.fori_loop(0, rows // 512, project, 0)

    def block(j, keys):
        here = tile_rows(j, BLK)
        lim = limits(seg_rows, seg_cols, j, keys)
        for p in range(PAIRS):
            at = slice(p * PAIR, (p + 1) * PAIR)
            queries = masked_pair(qkv[here, at])
            scores = dot(qkv[keys, width + p * PAIR : width + (p + 1) * PAIR], queries, NT)
            scores = jnp.minimum(scores, lim)
            top = jnp.max(scores, axis=0, keepdims=True)
            expo = jnp.exp2((scores - top) * SCORE_LOG2)
            total = jnp.sum(expo, axis=0, keepdims=True)
            probs_low = (expo * (1.0 / total)).astype(bf16)
            out = dot(value_t[at, keys], probs_low)
            mixed_t[p * PAIR : p * PAIR + HEAD, here] = out[:HEAD, :BLK].astype(bf16)
            mixed_t[p * PAIR + HEAD : (p + 1) * PAIR, here] = out[HEAD:, BLK:].astype(bf16)
            level = top * SCORE_LOG2 + jnp.log2(total)
            stats[pl.ds(j, 1), p * 2 * BLK : (p + 1) * 2 * BLK] = level

    over_windows(seg, offs, counts, images_here, rows, block)


def attend_call(seg, offs, counts, normed, w_t, bias, seg_rows, seg_cols):
    rows, width = normed.shape
    return kernel_call(
        attend_body,
        [SM, SM, SM, VM, VM, VM, VM, VM],
        (S((rows, 3 * width), bf16), S((width, rows), bf16), S((rows // BLK, HEADS * BLK), f32)),
        [pltpu.VMEM((width, rows), bf16)],
        flops=2 * rows * width * 3 * width + 4 * rows * 384 * width,
        moved=rows * width * 12,
        name="attend",
    )(seg, offs, counts, normed, w_t, bias, seg_rows, seg_cols)


def attend_back_body(seg, offs, counts, qkv, mixed_grad, stats, seg_rows, seg_cols, qkv_grad, key_t, key_grad, value_grad):
    rows, width = mixed_grad.shape
    images_here = offs.shape[0]

    def prepare(i, carry):
        sl = tile_rows(i, 512)
        key_t[:, sl] = qkv[sl, width : 2 * width].T
        key_grad[sl, :] = jnp.zeros((512, width), f32)
        value_grad[sl, :] = jnp.zeros((512, width), f32)
        return carry

    lax.fori_loop(0, rows // 512, prepare, 0)

    def block(j, keys):
        here = tile_rows(j, BLK)
        lim = limits(seg_rows, seg_cols, j, keys)
        for p in range(PAIRS):
            at = slice(p * PAIR, (p + 1) * PAIR)
            queries = masked_pair(qkv[here, at])
            outs = masked_pair(mixed_grad[here, at])
            level = stats[pl.ds(j, 1), p * 2 * BLK : (p + 1) * 2 * BLK]
            scores = dot(qkv[keys, width + p * PAIR : width + (p + 1) * PAIR], queries, NT)
            probs = jnp.exp2(jnp.minimum(scores, lim) * SCORE_LOG2 - level)
            prob_grad = dot(qkv[keys, 2 * width + p * PAIR : 2 * width + (p + 1) * PAIR], outs, NT)
            inner = jnp.sum(probs * prob_grad, axis=0, keepdims=True)
            score_grad = (probs * (prob_grad - inner)).astype(bf16)
            key_grad[keys, at] += dot(score_grad, queries)
            value_grad[keys, at] += dot(probs.astype(bf16), outs)
            query_t = dot(key_t[at, keys], score_grad) * SCALE
            joined = jnp.concatenate([query_t[:HEAD, :BLK], query_t[HEAD:, BLK:]], axis=0)
            qkv_grad[here, at] = joined.T.astype(bf16)

    over_windows(seg, offs, counts, images_here, rows, block)

    def finish(i, carry):
        sl = tile_rows(i, 256)
        qkv_grad[sl, width : 2 * width] = (key_grad[sl, :] * SCALE).astype(bf16)
        qkv_grad[sl, 2 * width :] = value_grad[sl, :].astype(bf16)
        return carry

    lax.fori_loop(0, rows // 256, finish, 0)


def attend_back_call(seg, offs, counts, qkv, mixed_grad, stats, seg_rows, seg_cols):
    rows, width = mixed_grad.shape
    return kernel_call(
        attend_back_body,
        [SM, SM, SM, VM, VM, VM, VM, VM],
        (S((rows, 3 * width), bf16),),
        [pltpu.VMEM((width, rows), bf16), pltpu.VMEM((rows, width), f32), pltpu.VMEM((rows, width), f32)],
        flops=10 * rows * 384 * width,
        moved=rows * width * 16,
        name="attend_back",
    )(seg, offs, counts, qkv, mixed_grad, stats, seg_rows, seg_cols)[0]


def feed_body(
    packed, mixed_t, cot, vec, up_bias, w_out_t, w_up_t, w_down,
    layer_out, middle_grad, mixed_grad, out_grad, ffn_grad, bias_grad, sums,
    hid_s, gi_s, n2t_s, glt_s, mlow_s,
):
    rows, width = packed.shape
    size = 512
    bias_grad[...] = jnp.zeros_like(bias_grad)
    sums[...] = jnp.zeros_like(sums)

    def one(i, carry):
        sl = tile_rows(i, size)
        middle = packed[sl, :].astype(f32) + dot(mixed_t[:, sl].T, w_out_t[...], NT) + vec[4:5, :]
        unit, inverse = norm_parts(middle)
        low = (unit * vec[5:6, :] + vec[6:7, :]).astype(bf16)
        n2t_s[:, sl] = low.T
        valid = lax.broadcasted_iota(jnp.int32, (size, 1), 0) + i * size < rows - 1
        grad_out = jnp.where(valid, cot[sl, :].astype(f32), 0.0)
        grad_low = grad_out.astype(bf16)
        glt_s[:, sl] = grad_low.T
        sums[24:32, :] += row_sums(grad_out)
        u = dot(low, w_up_t[...], NT) + up_bias[...]
        phi = 0.5 + 0.5 * lax.erf(u * (1.0 / math.sqrt(2.0)))
        hidden = (u * phi).astype(bf16)
        hid_s[sl, :] = hidden
        slope = phi + u * jnp.exp2(u * u * (-0.5 * LOG2E)) * (1.0 / math.sqrt(2.0 * math.pi))
        grad_in = dot(grad_low, w_down[...], NT) * slope
        bias_grad[...] += row_sums(grad_in)
        grad_in_low = grad_in.astype(bf16)
        gi_s[sl, :] = grad_in_low
        down = dot(hidden, w_down[...])
        layer_out[sl, :] = jnp.where(valid, middle + down + vec[7:8, :], 0.0).astype(bf16)
        n2_grad = dot(grad_in_low, w_up_t[...])
        sums[8:16, :] += row_sums(n2_grad * unit)
        sums[16:24, :] += row_sums(n2_grad)
        total = grad_out + norm_back(unit, inverse, vec[5:6, :], n2_grad)
        middle_grad[sl, :] = total
        sums[0:8, :] += row_sums(total)
        total_low = total.astype(bf16)
        mlow_s[sl, :] = total_low
        mixed_grad[sl, :] = dot(total_low, w_out_t[...]).astype(bf16)
        return carry

    lax.fori_loop(0, rows // size, one, 0)
    units = w_up_t.shape[0]
    for lower in range(0, units, 256):
        hs = slice(lower, lower + 256)
        ffn_grad[0, hs, :] = dot(n2t_s[...], gi_s[:, hs]).T
        ffn_grad[1, hs, :] = dot(glt_s[...], hid_s[:, hs]).T
    out_grad[...] = dot(mixed_t[...], mlow_s[...]).T


def feed_call(packed, mixed_t, cot, vec, up_bias, w_out_t, w_up_t, w_down):
    rows, width = packed.shape
    units = w_up_t.shape[0]
    return kernel_call(
        feed_body,
        [VM] * 8,
        (
            S((rows, width), bf16),
            S((rows, width), f32),
            S((rows, width), bf16),
            S((width, width), f32),
            S((2, units, width), f32),
            S((8, units), f32),
            S((32, width), f32),
        ),
        [
            pltpu.VMEM((rows, units), bf16),
            pltpu.VMEM((rows, units), bf16),
            pltpu.VMEM((width, rows), bf16),
            pltpu.VMEM((width, rows), bf16),
            pltpu.VMEM((rows, width), bf16),
        ],
        flops=12 * rows * width * units + 6 * rows * width * width,
        moved=rows * width * 16 + units * width * 12,
        name="feed",
    )(packed, mixed_t, cot, vec, up_bias, w_out_t, w_up_t, w_down)


def input_body(qkv_grad, w_t, packed, normed_t, middle_grad, vec, input_grad, weight_grad, sums):
    rows, width = packed.shape
    size = 512
    sums[...] = jnp.zeros_like(sums)

    def one(i, carry):
        sl = tile_rows(i, size)
        grads = qkv_grad[sl, :]
        normed_grad = dot(grads, w_t[...])
        unit, inverse = norm_parts(packed[sl, :].astype(f32))
        sums[0:8, :] += row_sums(normed_grad * unit)
        sums[8:16, :] += row_sums(normed_grad)
        sums[16:24, :] += row_sums(grads[:, :width].astype(f32))
        sums[24:32, :] += row_sums(grads[:, 2 * width :].astype(f32))
        input_grad[sl, :] = middle_grad[sl, :] + norm_back(unit, inverse, vec[0:1, :], normed_grad)
        return carry

    lax.fori_loop(0, rows // size, one, 0)
    for lower in range(0, 3 * width, 128):
        hs = slice(lower, lower + 128)
        weight_grad[hs, :] = dot(normed_t[...], qkv_grad[:, hs]).T


def input_call(qkv_grad, w_t, packed, normed_t, middle_grad, vec):
    rows, width = packed.shape
    return kernel_call(
        input_body,
        [VM] * 6,
        (S((rows, width), f32), S((3 * width, width), f32), S((32, width), f32)),
        flops=12 * rows * width * width,
        moved=rows * width * 20,
        name="input_back",
    )(qkv_grad, w_t, packed, normed_t, middle_grad, vec)


def unpack_body(win, offs, keep, input_grad, image_grads, slots):
    images_here, length = keep.shape
    rows, width = input_grad.shape
    before = lax.broadcasted_iota(jnp.int32, (length, length), 0)
    after = lax.broadcasted_iota(jnp.int32, (length, length), 1)
    tri = jnp.where(before <= after, 1.0, 0.0).astype(bf16)
    kept = keep[...]
    ranks = dot(kept.astype(f32).astype(bf16), tri).astype(jnp.int32) - 1
    slots[...] = jnp.where(kept > 0, ranks, -4 * win)
    place = lax.broadcasted_iota(jnp.int32, (win, length), 0)

    def one_image(i, carry):
        base = pl.multiple_of(jnp.minimum((offs[i] // 8) * 8, rows - win), 8)
        shift = offs[i] - base
        chosen = jnp.where(place == slots[pl.ds(i, 1), :] + shift, 1.0, 0.0).astype(bf16)
        values = input_grad[pl.ds(base, win), :]
        high = values.astype(bf16)
        rest = (values - high.astype(f32)).astype(bf16)
        image_grads[i] = dot(chosen, high, TN) + dot(chosen, rest, TN)
        return carry

    lax.fori_loop(0, images_here, one_image, 0)


def unpack_call(offs, keep, input_grad):
    images_here, length = keep.shape
    rows, width = input_grad.shape
    win = (length + 7 + 7) // 8 * 8
    return kernel_call(
        functools.partial(unpack_body, win),
        [SM, VM, VM],
        (S((images_here, length, width), f32),),
        [pltpu.VMEM((images_here, length), jnp.int32)],
        flops=4 * images_here * win * length * width,
        moved=images_here * length * width * 4 + rows * width * 4,
        name="unpack",
    )(offs, keep, input_grad)[0]


def adamw(weight, grad, first, second, average, count, rate, decay):
    first_new = BETA_ONE * first + (1.0 - BETA_ONE) * grad
    second_new = BETA_TWO * second + (1.0 - BETA_TWO) * grad * grad
    first_hat = first_new / (1.0 - jnp.power(BETA_ONE, count))
    second_hat = second_new / (1.0 - jnp.power(BETA_TWO, count))
    weight_new = weight - rate * (first_hat / (jnp.sqrt(second_hat) + ADAM_EPS) + decay * weight)
    average_new = AVERAGE_DECAY * average + (1.0 - AVERAGE_DECAY) * weight_new
    return (weight_new, first_new, second_new, average_new)


def body(
    images, keep_mask, kept_counts, pack_offsets, segment_ids, cotangent,
    attn_weight, ffn_weight, up_bias, vectors,
    attn_first, ffn_first, bias_first, vec_first,
    attn_second, ffn_second, bias_second, vec_second,
    attn_average, ffn_average, bias_average, vec_average, step,
):
    width = images.shape[2]
    rows = segment_ids.shape[0]
    both = ("dp", "mp")
    attn_t = lax.all_gather(attn_weight.astype(bf16).T, both, axis=0, tiled=True)
    ffn_t = lax.all_gather(jnp.swapaxes(ffn_weight.astype(bf16), 1, 2), both, axis=1, tiled=True)
    bias_full = lax.all_gather(up_bias.astype(bf16), both, axis=0, tiled=True).astype(f32)[None, :]
    seg_rows = segment_ids.reshape(rows // BLK, BLK)
    packed, normed, normed_t, seg_cols = pack_call(images, keep_mask, pack_offsets, seg_rows, vectors, rows)
    w_qkv_t = attn_t[: 3 * width]
    w_out_t = attn_t[3 * width :]
    qkv_bias = jnp.concatenate([vectors[2], jnp.zeros_like(vectors[2]), vectors[3]])[None, :]
    qkv, mixed_t, stats = attend_call(
        segment_ids, pack_offsets, kept_counts, normed, w_qkv_t, qkv_bias, seg_rows, seg_cols
    )
    layer_out, middle_grad, mixed_grad, out_grad, ffn_part, bias_part, sums_two = feed_call(
        packed, mixed_t, cotangent, vectors, bias_full, w_out_t, ffn_t[0], ffn_t[1]
    )
    qkv_grad = attend_back_call(
        segment_ids, pack_offsets, kept_counts, qkv, mixed_grad, stats, seg_rows, seg_cols
    )
    input_grad, qkv_weight_grad, sums_one = input_call(qkv_grad, w_qkv_t, packed, normed_t, middle_grad, vectors)
    image_grads = unpack_call(pack_offsets, keep_mask, input_grad)
    sums_one = sums_one.reshape(4, 8, width).sum(axis=1)
    sums_two = sums_two.reshape(4, 8, width).sum(axis=1)
    vec_terms = jnp.concatenate([sums_one, sums_two], axis=0)
    attn_terms = jnp.concatenate([qkv_weight_grad, out_grad], axis=0)
    attn_grad = lax.psum_scatter(attn_terms.astype(bf16), both, scatter_dimension=0, tiled=True).astype(f32).T
    ffn_grad = jnp.swapaxes(
        lax.psum_scatter(ffn_part.astype(bf16), both, scatter_dimension=1, tiled=True).astype(f32), 1, 2
    )
    bias_grad = lax.psum_scatter(bias_part.sum(axis=0), both, scatter_dimension=0, tiled=True)
    vec_grad = lax.psum(vec_terms, both)
    count = step[0].astype(f32)
    attn_up = adamw(
        attn_weight, attn_grad, attn_first, attn_second, attn_average, count, MATRIX_RATE, WEIGHT_DECAY
    )
    ffn_up = adamw(ffn_weight, ffn_grad, ffn_first, ffn_second, ffn_average, count, MATRIX_RATE, WEIGHT_DECAY)
    bias_up = adamw(up_bias, bias_grad, bias_first, bias_second, bias_average, count, VECTOR_RATE, 0.0)
    vec_up = adamw(vectors, vec_grad, vec_first, vec_second, vec_average, count, VECTOR_RATE, 0.0)
    news = [part[k] for k in range(4) for part in (attn_up, ffn_up, bias_up, vec_up)]
    return (layer_out, image_grads, attn_grad, ffn_grad, bias_grad, vec_grad, *news)


def solution(mesh):
    both = ("dp", "mp")
    matrix, slab, line = P(None, both), P(None, None, both), P(both)
    states = (matrix, slab, line, P())
    return jax.shard_map(
        body,
        mesh=mesh,
        in_specs=(P(both, None, None), P(both, None), line, line, line, P(both, None), *states * 4, P()),
        out_specs=(P(both, None), P(both, None, None), *states, *states * 4),
        check_vma=False,
    )
```

```python
import functools
import math

import jax
import jax.numpy as jnp
from jax import lax
from jax.experimental import pallas as pl
from jax.experimental.pallas import tpu as pltpu
from jax.sharding import PartitionSpec as P

HEADS = 6
HEAD = 64
PAIR = 2 * HEAD
PAIRS = HEADS // 2
BLK = 128
REACH = 5
CHUNKS = 32
HALF = CHUNKS // 2
EXTRA = 16
EXCLUDED = -8.0e9
INCLUDED = 3.0e38

NORM_EPS = 1e-06
BETA_ONE = 0.9
BETA_TWO = 0.999
ADAM_EPS = 1e-08
MATRIX_RATE = 0.05
VECTOR_RATE = 0.2
WEIGHT_DECAY = 0.05
AVERAGE_DECAY = 0.8

LOG2E = 1.4426950408889634
SCORE_LOG2 = LOG2E / math.sqrt(HEAD)
SCALE = 1.0 / math.sqrt(HEAD)

f32 = jnp.float32
bf16 = jnp.bfloat16
NN = (((1,), (0,)), ((), ()))
NT = (((1,), (1,)), ((), ()))
TN = (((0,), (0,)), ((), ()))
VM = pl.BlockSpec(memory_space=pltpu.VMEM)
SM = pl.BlockSpec(memory_space=pltpu.SMEM)
S = jax.ShapeDtypeStruct


def dot(left, right, dims=NN):
    return lax.dot_general(left, right, dims, preferred_element_type=f32)


def kernel_call(body, ins, outs, scratch=(), flops=0, micros=1, name=None):
    return pl.pallas_call(
        body,
        out_shape=outs,
        in_specs=ins,
        out_specs=tuple(VM for _ in outs),
        scratch_shapes=list(scratch),
        compiler_params=pltpu.CompilerParams(vmem_limit_bytes=58 * 2**20),
        cost_estimate=pl.CostEstimate(flops=flops, bytes_accessed=micros * 3_500_000, transcendentals=0),
        name=name,
    )


def row_sums(values):
    rows, width = values.shape
    return jnp.sum(values.reshape(rows // 8, 8, width), axis=0)


def norm_parts(values):
    scale = 1.0 / values.shape[-1]
    centre = jnp.sum(values, axis=-1, keepdims=True) * scale
    centred = values - centre
    spread = jnp.sum(centred * centred, axis=-1, keepdims=True) * scale
    inverse = lax.rsqrt(spread + NORM_EPS)
    return centred * inverse, inverse


def norm_back(unit, inverse, gain, grad):
    scale = 1.0 / unit.shape[-1]
    scaled = grad * gain
    mean = jnp.sum(scaled, axis=-1, keepdims=True) * scale
    along = jnp.sum(scaled * unit, axis=-1, keepdims=True) * scale
    return inverse * (scaled - mean - unit * along)


def tile_rows(count, size):
    return pl.ds(pl.multiple_of(count * size, size), size)


def place_of(own, other):
    apart = lax.shift_right_logical(own, 1) ^ (other // 2)
    return (apart & 3) * 4 + lax.shift_right_logical(apart, 2)


def spread_pieces(own, halves, out):
    for near in range(2):
        for slot in range(HALF):
            apart = near + 2 * ((slot // 4) + 4 * (slot % 4))
            out[own ^ apart] = halves[near][slot * out.shape[1] : (slot + 1) * out.shape[1], :]


def store_pieces(own, start, pieces, keep, send, at, step):
    count, size, _ = pieces.shape
    odd = (own & 1) == 1
    for e in range(0, count, 2):
        row = pl.multiple_of(place_of(own, start + e) * step + at, 16)
        even_piece, odd_piece = pieces[e], pieces[e + 1]
        keep[pl.ds(row, size), :] = jnp.where(odd, odd_piece, even_piece)
        send[pl.ds(row, size), :] = jnp.where(odd, even_piece, odd_piece)


def split_low(values):
    high = values.astype(bf16)
    return high, (values - high.astype(f32)).astype(bf16)


def combine_body(parts, size, extra, count, *refs):
    own, received, outs = refs[0], refs[1 : 1 + count], refs[1 + count :]
    base = parts * size
    for part in range(parts):
        rows = slice(part * size, (part + 1) * size)
        total = own[rows, :].astype(f32)
        for other in received:
            total = total + other[rows, :].astype(f32)
        if part == 0:
            outs[0][:size, :] = total
        else:
            outs[part][:size, :] = total.astype(bf16)
    if extra:
        if own.dtype == bf16:
            sums = [own[base : base + extra, :].astype(f32) + own[base + extra :, :].astype(f32)]
        else:
            sums = [own[base:, :]]
        sums += [r[base : base + extra, :].astype(f32) + r[base + extra :, :].astype(f32) for r in received]
        while len(sums) > 1:
            sums = [sums[i] + sums[i + 1] for i in range(0, len(sums), 2)]
        high, low = split_low(sums[0])
        outs[0][size:, :] = high.astype(f32) + low.astype(f32) if parts > 1 else sums[0]
        for out in outs[1:]:
            out[size : size + extra, :] = high
            out[size + extra :, :] = low


def combine_call(own, received, parts, extra):
    size = (received[0].shape[0] - 2 * extra) // parts
    width = own.shape[1]
    outs = (S((size + extra, width), f32),) + (S((size + 2 * extra, width), bf16),) * (parts - 1)
    return kernel_call(
        functools.partial(combine_body, parts, size, extra, len(received)),
        [VM] * (1 + len(received)),
        outs,
        flops=own.size * len(received),
        micros=2,
        name="combine",
    )(own, *received)


def over_core(values):
    return lax.ppermute(values, "mp", [(i, i ^ 1) for i in range(lax.axis_size("mp"))])


def over_plane(values, apart):
    devices = lax.axis_size("dp") * lax.axis_size("mp")
    return lax.ppermute(values, ("dp", "mp"), [(i, i ^ (2 * apart)) for i in range(devices)])


def over_line(values, apart):
    return lax.ppermute(values, "dp", [(i, i ^ (2 * apart)) for i in range(lax.axis_size("dp"))])


def tie(*values):
    return lax.optimization_barrier(values)


def gather_line(piece):
    return jnp.concatenate([piece] + [over_line(piece, k) for k in (1, 2, 3)], axis=0)


def gather_plane(pieces):
    return jnp.concatenate([pieces] + [over_plane(pieces, k) for k in (1, 2, 3)], axis=0)


def place_body(win, offs, images, keep, packed, acc, slots):
    images_here, length = keep.shape
    rows, width = packed.shape
    before = lax.broadcasted_iota(jnp.int32, (length, length), 0)
    after = lax.broadcasted_iota(jnp.int32, (length, length), 1)
    tri = jnp.where(before <= after, 1.0, 0.0).astype(bf16)
    kept = keep[...]
    ranks = dot(kept.astype(f32).astype(bf16), tri).astype(jnp.int32) - 1
    slots[...] = jnp.where(kept > 0, ranks, -4 * win)
    acc[0:8, :] = jnp.zeros((8, width), f32)
    place = lax.broadcasted_iota(jnp.int32, (win, length), 0)

    def one_image(i, carry):
        base = pl.multiple_of((offs[i] // 8) * 8, 8)
        shift = offs[i] - base
        chosen = jnp.where(place == slots[pl.ds(i, 1), :] + shift, 1.0, 0.0).astype(bf16)
        moved = dot(chosen, images[i])
        acc[pl.ds(base, 8), :] += moved[0:8]
        acc[pl.ds(base + 8, win - 8), :] = moved[8:]
        return carry

    lax.fori_loop(0, images_here, one_image, 0)
    packed[...] = acc[:rows, :].astype(bf16)


def place_call(images, keep, offs, rows):
    images_here, length, width = images.shape
    win = (length + 7 + 7) // 8 * 8
    return kernel_call(
        functools.partial(place_body, win),
        [SM, VM, VM],
        (S((rows, width), bf16),),
        [pltpu.VMEM((rows + win, width), f32), pltpu.VMEM((images_here, length), jnp.int32)],
        flops=2 * images_here * win * length * width,
        micros=9,
        name="place",
    )(offs, images, keep)[0]


def norm_body(packed, seg_rows, vec, normed, normed_t, seg_cols):
    rows, width = packed.shape

    def one_tile(i, carry):
        sl = tile_rows(i, 256)
        unit, _ = norm_parts(packed[sl, :].astype(f32))
        low = (unit * vec[0:1, :] + vec[1:2, :]).astype(bf16)
        normed[sl, :] = low
        normed_t[:, sl] = low.T
        return carry

    lax.fori_loop(0, rows // 256, one_tile, 0)

    def one_block(j, carry):
        line = seg_rows[pl.ds(j, 1), :]
        seg_cols[tile_rows(j, BLK), :] = jnp.broadcast_to(line, (BLK, BLK)).T
        return carry

    lax.fori_loop(0, rows // BLK, one_block, 0)


def norm_call(packed, seg_rows, vec):
    rows, width = packed.shape
    return kernel_call(
        norm_body,
        [VM, VM, VM],
        (S((rows, width), bf16), S((width, rows), bf16), S((rows, BLK), jnp.int32)),
        flops=rows * width * 12,
        micros=6,
        name="norm",
    )(packed, seg_rows, vec)


def window(seg, offs, counts, j, images_here, rows):
    first = seg[j * BLK]
    last = seg[j * BLK + BLK - 1]
    used = last < images_here
    last_here = jnp.where(used, last, 0)
    low = offs[first] // BLK
    end = jnp.where(used, offs[last_here] + counts[last_here], rows)
    return low, (end + BLK - 1) // BLK - low


def masked_pair(pair):
    lane = lax.broadcasted_iota(jnp.int32, pair.shape, 1)
    none = jnp.zeros_like(pair)
    return jnp.concatenate([jnp.where(lane < HEAD, pair, none), jnp.where(lane >= HEAD, pair, none)], axis=0)


def limits(seg_rows, seg_cols, j, keys):
    same = seg_cols[keys, :] == seg_rows[pl.ds(j, 1), :]
    lim = jnp.where(same, INCLUDED, EXCLUDED)
    return jnp.concatenate([lim, lim], axis=1)


def over_windows(seg, offs, counts, images_here, rows, first, blocks, block):
    def one(j, carry):
        low, size = window(seg, offs, counts, j, images_here, rows)
        for n in range(1, REACH + 1):

            @pl.when(size == n)
            def _():
                block(j, pl.ds(pl.multiple_of(low * BLK, BLK), n * BLK))

        return carry

    lax.fori_loop(first, first + blocks, one, 0)


def project_body(own, normed, mine, other, bias, qkv, value_t, w_t):
    rows, width = normed.shape
    spread_pieces(own[0], (mine, other), w_t)
    units = w_t.shape[0] * w_t.shape[1]
    weights = w_t[...].reshape(units, width)[: 3 * width]

    def project(i, carry):
        sl = tile_rows(i, 512)
        low = (dot(normed[sl, :], weights, NT) + bias[...]).astype(bf16)
        qkv[sl, :] = low
        value_t[:, sl] = low[:, 2 * width :].T
        return carry

    lax.fori_loop(0, rows // 512, project, 0)


def project_call(own, normed, mine, other, bias):
    rows, width = normed.shape
    piece = mine.shape[0] // HALF
    return kernel_call(
        project_body,
        [SM, VM, VM, VM, VM],
        (S((rows, 3 * width), bf16), S((width, rows), bf16), S((CHUNKS, piece, width), bf16)),
        flops=2 * rows * width * 3 * width,
        micros=8,
        name="project",
    )(own, normed, mine, other, bias)


def attend_body(first, seg, offs, counts, qkv, value_t, seg_rows, seg_cols, mixed_t, stats):
    width, rows = value_t.shape
    images_here = offs.shape[0]

    def block(j, keys):
        here = tile_rows(j, BLK)
        there = tile_rows(j - first, BLK)
        lim = limits(seg_rows, seg_cols, j, keys)
        for p in range(PAIRS):
            at = slice(p * PAIR, (p + 1) * PAIR)
            queries = masked_pair(qkv[here, at])
            scores = dot(qkv[keys, width + p * PAIR : width + (p + 1) * PAIR], queries, NT)
            scores = jnp.minimum(scores, lim)
            top = jnp.max(scores, axis=0, keepdims=True)
            expo = jnp.exp2((scores - top) * SCORE_LOG2)
            total = jnp.sum(expo, axis=0, keepdims=True)
            probs_low = (expo * (1.0 / total)).astype(bf16)
            out = dot(value_t[at, keys], probs_low)
            mixed_t[p * PAIR : p * PAIR + HEAD, there] = out[:HEAD, :BLK].astype(bf16)
            mixed_t[p * PAIR + HEAD : (p + 1) * PAIR, there] = out[HEAD:, BLK:].astype(bf16)
            level = top * SCORE_LOG2 + jnp.log2(total)
            stats[pl.ds(j - first, 1), p * 2 * BLK : (p + 1) * 2 * BLK] = level

    over_windows(seg, offs, counts, images_here, rows, first, mixed_t.shape[1] // BLK, block)


def attend_call(first, blocks, seg, offs, counts, qkv, value_t, seg_rows, seg_cols):
    width, rows = value_t.shape
    return kernel_call(
        functools.partial(attend_body, first),
        [SM, SM, SM, VM, VM, VM, VM],
        (S((width, blocks * BLK), bf16), S((blocks, HEADS * BLK), f32)),
        flops=4 * blocks * BLK * 1024 * width,
        micros=15,
        name="attend",
    )(seg, offs, counts, qkv, value_t, seg_rows, seg_cols)


def attend_back_body(seg, offs, counts, qkv, key_t, mixed_grad, stats, seg_rows, seg_cols, qkv_grad, key_grad, value_grad):
    rows, width = mixed_grad.shape
    images_here = offs.shape[0]

    def prepare(i, carry):
        sl = tile_rows(i, 512)
        key_grad[sl, :] = jnp.zeros((512, width), f32)
        value_grad[sl, :] = jnp.zeros((512, width), f32)
        return carry

    lax.fori_loop(0, rows // 512, prepare, 0)

    def block(j, keys):
        here = tile_rows(j, BLK)
        lim = limits(seg_rows, seg_cols, j, keys)
        for p in range(PAIRS):
            at = slice(p * PAIR, (p + 1) * PAIR)
            queries = masked_pair(qkv[here, at])
            outs = masked_pair(mixed_grad[here, at])
            level = stats[pl.ds(j, 1), p * 2 * BLK : (p + 1) * 2 * BLK]
            scores = dot(qkv[keys, width + p * PAIR : width + (p + 1) * PAIR], queries, NT)
            probs = jnp.exp2(jnp.minimum(scores, lim) * SCORE_LOG2 - level)
            prob_grad = dot(qkv[keys, 2 * width + p * PAIR : 2 * width + (p + 1) * PAIR], outs, NT)
            inner = jnp.sum(probs * prob_grad, axis=0, keepdims=True)
            score_grad = (probs * (prob_grad - inner)).astype(bf16)
            key_grad[keys, at] += dot(score_grad, queries)
            value_grad[keys, at] += dot(probs.astype(bf16), outs)
            query_t = dot(key_t[at, keys], score_grad) * SCALE
            joined = jnp.concatenate([query_t[:HEAD, :BLK], query_t[HEAD:, BLK:]], axis=0)
            qkv_grad[here, at] = joined.T.astype(bf16)

    over_windows(seg, offs, counts, images_here, rows, 0, rows // BLK, block)

    def finish(i, carry):
        sl = tile_rows(i, 256)
        qkv_grad[sl, width : 2 * width] = (key_grad[sl, :] * SCALE).astype(bf16)
        qkv_grad[sl, 2 * width :] = value_grad[sl, :].astype(bf16)
        return carry

    lax.fori_loop(0, rows // 256, finish, 0)


def attend_back_call(seg, offs, counts, qkv, key_t, mixed_grad, stats, seg_rows, seg_cols):
    rows, width = mixed_grad.shape
    return kernel_call(
        attend_back_body,
        [SM, SM, SM, VM, VM, VM, VM, VM, VM],
        (S((rows, 3 * width), bf16),),
        [pltpu.VMEM((rows, width), f32), pltpu.VMEM((rows, width), f32)],
        flops=10 * rows * 384 * width,
        micros=32,
        name="attend_back",
    )(seg, offs, counts, qkv, key_t, mixed_grad, stats, seg_rows, seg_cols)[0]


def bias_line(rows_of, units):
    chunks, size = rows_of.shape
    column = lax.broadcasted_iota(jnp.int32, (size, units), 1)
    within = lax.broadcasted_iota(jnp.int32, (size, units), 0)
    repeat = jnp.where(column % size == within, 1.0, 0.0).astype(bf16)
    wide = dot(rows_of, repeat)
    owner = lax.broadcasted_iota(jnp.int32, (chunks, units), 1) // size
    mine = owner == lax.broadcasted_iota(jnp.int32, (chunks, units), 0)
    return jnp.sum(jnp.where(mine, wide, 0.0), axis=0, keepdims=True)


def feed_body(
    own, packed, mixed_a, mixed_b, cot, vec, w_t, mine, other,
    layer_out, middle_grad, mixed_grad, keep, send, sums_out,
    all_s, up_s, down_s, hid_s, gi_s, n2t_s, glt_s, bias_s, sums, bias_sum,
):
    rows, width = packed.shape
    size = 512
    half = mixed_a.shape[1] // size
    me = own[0]
    units = up_s.shape[0]
    piece = units // CHUNKS
    spread_pieces(me, (mine, other), all_s)
    up_s[...] = all_s[:, :piece, :].reshape(units, width)
    down_s[...] = all_s[:, piece : 2 * piece, :].reshape(units, width)
    bias_s[...] = bias_line(all_s[:, 2 * piece, :piece], units)
    bias_sum[...] = jnp.zeros_like(bias_sum)
    sums[...] = jnp.zeros_like(sums)

    def one(mixed, base, i, carry):
        sl = tile_rows(i + base, size)
        at = tile_rows(i, size)
        middle = packed[sl, :].astype(f32) + dot(mixed[:, at].T, w_t[3 * HALF // 2 :].reshape(width, width), NT) + vec[4:5, :]
        unit, inverse = norm_parts(middle)
        low = (unit * vec[5:6, :] + vec[6:7, :]).astype(bf16)
        n2t_s[:, sl] = low.T
        valid = lax.broadcasted_iota(jnp.int32, (size, 1), 0) + (i + base) * size < rows - 1
        grad_out = jnp.where(valid, cot[sl, :].astype(f32), 0.0)
        grad_low = grad_out.astype(bf16)
        glt_s[:, sl] = grad_low.T
        sums[24:32, :] += row_sums(grad_out)
        u = dot(low, up_s[...], NT) + bias_s[...]
        phi = 0.5 + 0.5 * lax.erf(u * (1.0 / math.sqrt(2.0)))
        hidden = (u * phi).astype(bf16)
        hid_s[sl, :] = hidden
        slope = phi + u * jnp.exp2(u * u * (-0.5 * LOG2E)) * (1.0 / math.sqrt(2.0 * math.pi))
        grad_in = dot(grad_low, down_s[...], NT) * slope
        bias_sum[...] += row_sums(grad_in)
        grad_in_low = grad_in.astype(bf16)
        gi_s[sl, :] = grad_in_low
        down = dot(hidden, down_s[...])
        layer_out[sl, :] = jnp.where(valid, middle + down + vec[7:8, :], 0.0).astype(bf16)
        n2_grad = dot(grad_in_low, up_s[...])
        sums[8:16, :] += row_sums(n2_grad * unit)
        sums[16:24, :] += row_sums(n2_grad)
        total = grad_out + norm_back(unit, inverse, vec[5:6, :], n2_grad)
        middle_grad[sl, :] = total
        sums[0:8, :] += row_sums(total)
        total_low = total.astype(bf16)
        mixed_grad[sl, :] = dot(total_low, w_t[3 * HALF // 2 :].reshape(width, width)).astype(bf16)
        return carry

    lax.fori_loop(0, half, functools.partial(one, mixed_a, 0), 0)
    lax.fori_loop(0, half, functools.partial(one, mixed_b, half), 0)
    for lower in range(0, units, width):
        hs = slice(lower, lower + width)
        for index, (left, right) in enumerate(((n2t_s, gi_s), (glt_s, hid_s))):
            pieces = dot(left[...], right[:, hs]).T.astype(bf16).reshape(width // piece, piece, width)
            store_pieces(me, lower // piece, pieces, keep, send, index * piece, 2 * piece)
    for row in range(4):
        sums_out[row : row + 1, :] = jnp.sum(sums[8 * row : 8 * row + 8, :], axis=0, keepdims=True)
    line = jnp.sum(bias_sum[...], axis=0, keepdims=True)
    for row in range(units // width):
        sums_out[4 + row : 5 + row, :] = line[:, row * width : (row + 1) * width]


def feed_call(own, packed, mixed_a, mixed_b, cot, vec, w_t, mine, other):
    rows, width = packed.shape
    units = 4 * width
    piece = units // CHUNKS
    return kernel_call(
        feed_body,
        [SM] + [VM] * 8,
        (
            S((rows, width), bf16),
            S((rows, width), f32),
            S((rows, width), bf16),
            S((units, width), bf16),
            S((units, width), bf16),
            S((8, width), f32),
        ),
        [
            pltpu.VMEM((CHUNKS, mine.shape[0] // HALF, width), bf16),
            pltpu.VMEM((units, width), bf16),
            pltpu.VMEM((units, width), bf16),
            pltpu.VMEM((rows, units), bf16),
            pltpu.VMEM((rows, units), bf16),
            pltpu.VMEM((width, rows), bf16),
            pltpu.VMEM((width, rows), bf16),
            pltpu.VMEM((1, units), f32),
            pltpu.VMEM((32, width), f32),
            pltpu.VMEM((8, units), f32),
        ],
        flops=12 * rows * width * units + 6 * rows * width * width,
        micros=36,
        name="feed",
    )(own, packed, mixed_a, mixed_b, cot, vec, w_t, mine, other)


def side_body(mixed_a, mixed_b, middle_grad, qkv, out_grad, key_t):
    rows, width = middle_grad.shape
    size = 512

    def one(i, carry):
        sl = tile_rows(i, size)
        key_t[:, sl] = qkv[sl, width : 2 * width].T
        return carry

    lax.fori_loop(0, rows // size, one, 0)
    first = rows // 2
    total = dot(mixed_a[...], middle_grad[:first, :].astype(bf16))
    total += dot(mixed_b[...], middle_grad[first:, :].astype(bf16))
    out_grad[...] = total.T.astype(bf16)


def side_call(mixed_a, mixed_b, middle_grad, qkv):
    rows, width = middle_grad.shape
    return kernel_call(
        side_body,
        [VM] * 4,
        (S((width, width), bf16), S((width, rows), bf16)),
        flops=2 * rows * width * width,
        micros=6,
        name="side",
    )(mixed_a, mixed_b, middle_grad, qkv)


def input_body(own, qkv_grad, w_t, packed, normed_t, middle_grad, out_grad, feed_sums, vec, input_grad, keep, send, sums):
    rows, width = packed.shape
    me = own[0]
    piece = w_t.shape[1]
    weights = w_t[: 3 * HALF // 2].reshape(3 * width, width)
    size = 512
    sums[...] = jnp.zeros_like(sums)

    def one(i, carry):
        sl = tile_rows(i, size)
        grads = qkv_grad[sl, :]
        normed_grad = dot(grads, weights)
        unit, inverse = norm_parts(packed[sl, :].astype(f32))
        sums[0:8, :] += row_sums(normed_grad * unit)
        sums[8:16, :] += row_sums(normed_grad)
        sums[16:24, :] += row_sums(grads[:, :width].astype(f32))
        sums[24:32, :] += row_sums(grads[:, 2 * width :].astype(f32))
        input_grad[sl, :] = middle_grad[sl, :] + norm_back(unit, inverse, vec[0:1, :], normed_grad)
        return carry

    lax.fori_loop(0, rows // size, one, 0)
    for lower in range(0, 3 * width, width):
        pieces = dot(normed_t[...], qkv_grad[:, lower : lower + width]).T.astype(bf16)
        store_pieces(me, lower // piece, pieces.reshape(width // piece, piece, width), keep, send, 0, piece)
    store_pieces(me, 3 * width // piece, out_grad[...].reshape(width // piece, piece, width), keep, send, 0, piece)
    lines = [jnp.sum(sums[8 * row : 8 * row + 8, :], axis=0, keepdims=True) for row in range(4)]
    lines = jnp.concatenate(lines + [feed_sums[...], jnp.zeros((4, width), f32)], axis=0)
    high, low = split_low(lines)
    base = HALF * piece
    for out in (keep, send):
        out[base : base + EXTRA, :] = high
        out[base + EXTRA :, :] = low


def input_call(own, qkv_grad, w_t, packed, normed_t, middle_grad, out_grad, feed_sums, vec):
    rows, width = packed.shape
    sent = S((HALF * w_t.shape[1] + 2 * EXTRA, width), bf16)
    return kernel_call(
        input_body,
        [SM] + [VM] * 8,
        (S((rows, width), f32), sent, sent),
        [pltpu.VMEM((32, width), f32)],
        flops=12 * rows * width * width,
        micros=14,
        name="input_back",
    )(own, qkv_grad, w_t, packed, normed_t, middle_grad, out_grad, feed_sums, vec)


def unpack_body(win, offs, keep, input_grad, image_grads, slots):
    images_here, length = keep.shape
    rows, width = input_grad.shape
    before = lax.broadcasted_iota(jnp.int32, (length, length), 0)
    after = lax.broadcasted_iota(jnp.int32, (length, length), 1)
    tri = jnp.where(before <= after, 1.0, 0.0).astype(bf16)
    kept = keep[...]
    ranks = dot(kept.astype(f32).astype(bf16), tri).astype(jnp.int32) - 1
    slots[...] = jnp.where(kept > 0, ranks, -4 * win)
    place = lax.broadcasted_iota(jnp.int32, (win, length), 0)

    def one_image(i, carry):
        base = pl.multiple_of(jnp.minimum((offs[i] // 8) * 8, rows - win), 8)
        shift = offs[i] - base
        chosen = jnp.where(place == slots[pl.ds(i, 1), :] + shift, 1.0, 0.0).astype(bf16)
        values = input_grad[pl.ds(base, win), :]
        high = values.astype(bf16)
        rest = (values - high.astype(f32)).astype(bf16)
        image_grads[i] = dot(chosen, high, TN) + dot(chosen, rest, TN)
        return carry

    lax.fori_loop(0, images_here, one_image, 0)


def unpack_call(offs, keep, input_grad):
    images_here, length = keep.shape
    rows, width = input_grad.shape
    win = (length + 7 + 7) // 8 * 8
    return kernel_call(
        functools.partial(unpack_body, win),
        [SM, VM, VM],
        (S((images_here, length, width), f32),),
        [pltpu.VMEM((images_here, length), jnp.int32)],
        flops=4 * images_here * win * length * width,
        micros=13,
        name="unpack",
    )(offs, keep, input_grad)[0]


def to_halves(chunks):
    _, size, width = chunks.shape
    ordered = chunks.reshape(4, 4, 2, size, width).transpose(2, 1, 0, 3, 4).reshape(2, HALF * size, width)
    return ordered[0], ordered[1]


def from_halves(keep, send, parts, width):
    size = keep.shape[0] // HALF // parts
    both = jnp.stack([keep, send]).reshape(2, 4, 4, parts, size, width)
    return both.transpose(2, 1, 0, 3, 4, 5).reshape(CHUNKS, parts, size, width)


def adamw(weight, grad, first, second, average, count, rate, decay):
    first_new = BETA_ONE * first + (1.0 - BETA_ONE) * grad
    second_new = BETA_TWO * second + (1.0 - BETA_TWO) * grad * grad
    first_hat = first_new / (1.0 - jnp.power(BETA_ONE, count))
    second_hat = second_new / (1.0 - jnp.power(BETA_TWO, count))
    weight_new = weight - rate * (first_hat / (jnp.sqrt(second_hat) + ADAM_EPS) + decay * weight)
    average_new = AVERAGE_DECAY * average + (1.0 - AVERAGE_DECAY) * weight_new
    return (weight_new, first_new, second_new, average_new)


def body(
    images, keep_mask, kept_counts, pack_offsets, segment_ids, cotangent,
    attn_weight, ffn_weight, up_bias, vectors,
    attn_first, ffn_first, bias_first, vec_first,
    attn_second, ffn_second, bias_second, vec_second,
    attn_average, ffn_average, bias_average, vec_average, step,
):
    width = images.shape[2]
    rows = segment_ids.shape[0]
    both = ("dp", "mp")
    piece = attn_weight.shape[1]
    tree = lax.axis_size("dp") == 8 and lax.axis_size("mp") == 4
    bias_row = jnp.pad(up_bias.astype(bf16)[None, :], ((0, 15), (0, width - piece)))
    seg_rows = segment_ids.reshape(rows // BLK, BLK)
    placed = place_call(images, keep_mask, pack_offsets, rows)
    if tree:
        own = (lax.axis_index("dp") * 4 + lax.axis_index("mp")).astype(jnp.int32)[None]
        attn_piece = attn_weight.astype(bf16).T
        ffn_piece = jnp.concatenate([ffn_weight[0].astype(bf16).T, ffn_weight[1].astype(bf16).T, bias_row], axis=0)
        attn_line = gather_line(attn_piece)
        attn_line, placed, ffn_piece = tie(attn_line, placed, ffn_piece)
        ffn_line = gather_line(ffn_piece)
        attn_mine = gather_plane(attn_line)
        normed, normed_t, seg_cols = norm_call(placed, seg_rows, vectors)
        attn_mine, normed, ffn_line = tie(attn_mine, normed, ffn_line)
        attn_other = over_core(attn_mine)
    else:
        own = jnp.zeros((1,), jnp.int32)
        attn_all = lax.all_gather(attn_weight.astype(bf16).T, both, axis=0, tiled=True)
        ffn_all = lax.all_gather(jnp.swapaxes(ffn_weight.astype(bf16), 1, 2), both, axis=1, tiled=True)
        bias_all = lax.all_gather(up_bias.astype(bf16), both, axis=0, tiled=True)
        size = 4 * width // CHUNKS
        ffn_all = jnp.concatenate(
            [
                ffn_all[0].reshape(CHUNKS, size, width),
                ffn_all[1].reshape(CHUNKS, size, width),
                jnp.pad(bias_all.reshape(CHUNKS, 1, size), ((0, 0), (0, 15), (0, width - size))),
            ],
            axis=1,
        )
        attn_mine, attn_other = to_halves(attn_all.reshape(CHUNKS, size, width))
        ffn_mine, ffn_other = to_halves(ffn_all)
        normed, normed_t, seg_cols = norm_call(placed, seg_rows, vectors)
    qkv_bias = jnp.concatenate([vectors[2], jnp.zeros_like(vectors[2]), vectors[3]])[None, :]
    qkv, value_t, w_t = project_call(own, normed, attn_mine, attn_other, qkv_bias)
    if tree:
        qkv, ffn_line = tie(qkv, ffn_line)
        ffn_mine = gather_plane(ffn_line)
    where = (segment_ids, pack_offsets, kept_counts)
    half = rows // BLK // 2
    mixed_a, stats_a = attend_call(0, half, *where, qkv, value_t, seg_rows, seg_cols)
    if tree:
        qkv, ffn_mine, mixed_a = tie(qkv, ffn_mine, mixed_a)
        ffn_other = over_core(ffn_mine)
    mixed_b, stats_b = attend_call(half, half, *where, qkv, value_t, seg_rows, seg_cols)
    layer_out, middle_grad, mixed_grad, ffn_keep, ffn_send, feed_sums = feed_call(
        own, placed, mixed_a, mixed_b, cotangent, vectors, w_t, ffn_mine, ffn_other
    )
    stats = jnp.concatenate([stats_a, stats_b], axis=0)
    if tree:
        ffn_in = over_core(ffn_send)
    out_grad, key_t = side_call(mixed_a, mixed_b, middle_grad, qkv)
    if tree:
        key_t, ffn_in = tie(key_t, ffn_in)
        ffn_own, *ffn_out = combine_call(ffn_keep, [ffn_in], 4, 0)
        key_t, ffn_own, *ffn_out = tie(key_t, ffn_own, *ffn_out)
        ffn_in = [over_plane(p, k + 1) for k, p in enumerate(ffn_out)]
    qkv_grad = attend_back_call(*where, qkv, key_t, mixed_grad, stats, seg_rows, seg_cols)
    if tree:
        qkv_grad, *ffn_in = tie(qkv_grad, *ffn_in)
        ffn_own, *ffn_out = combine_call(ffn_own, ffn_in, 4, 0)
        qkv_grad, ffn_own, *ffn_out = tie(qkv_grad, ffn_own, *ffn_out)
        ffn_in = [over_line(p, k + 1) for k, p in enumerate(ffn_out)]
    input_grad, attn_keep, attn_send = input_call(
        own, qkv_grad, w_t, placed, normed_t, middle_grad, out_grad, feed_sums, vectors
    )
    if tree:
        input_grad, attn_send, *ffn_in = tie(input_grad, attn_send, *ffn_in)
        attn_in = over_core(attn_send)
        attn_own, *attn_out = combine_call(attn_keep, [attn_in], 4, EXTRA)
        attn_in = [over_plane(p, k + 1) for k, p in enumerate(attn_out)]
        image_grads = unpack_call(pack_offsets, keep_mask, input_grad)
        image_grads, *attn_in = tie(image_grads, *attn_in)
        attn_own, *attn_out = combine_call(attn_own, attn_in, 4, EXTRA)
        attn_in = [over_line(p, k + 1) for k, p in enumerate(attn_out)]
        ffn_t = combine_call(ffn_own, ffn_in, 1, 0)[0]
        ffn_grad = jnp.swapaxes(ffn_t.reshape(2, piece, width), 1, 2)
        attn_t = combine_call(attn_own, attn_in, 1, EXTRA)[0]
        attn_grad = attn_t[:piece].T
        sums = attn_t[piece:]
    else:
        image_grads = unpack_call(pack_offsets, keep_mask, input_grad)
        ffn_t = jnp.swapaxes(from_halves(ffn_keep, ffn_send, 2, width), 0, 1).reshape(2, 4 * width, width)
        ffn_t = lax.psum_scatter(ffn_t.astype(f32), both, scatter_dimension=1, tiled=True)
        ffn_grad = jnp.swapaxes(ffn_t, 1, 2)
        base = attn_keep.shape[0] - 2 * EXTRA
        attn_t = from_halves(attn_keep[:base], attn_send[:base], 1, width).reshape(4 * width, width)
        attn_grad = lax.psum_scatter(attn_t.astype(f32), both, scatter_dimension=0, tiled=True).T
        sums = attn_keep[base : base + EXTRA].astype(f32) + attn_keep[base + EXTRA :].astype(f32)
        sums = lax.psum(sums, both)
    vec_grad = sums[:8]
    index = lax.axis_index("dp") * lax.axis_size("mp") + lax.axis_index("mp")
    bias_grad = lax.dynamic_slice_in_dim(sums[8:12].reshape(4 * width), index * piece, piece, 0)
    count = step[0].astype(f32)
    attn_up = adamw(
        attn_weight, attn_grad, attn_first, attn_second, attn_average, count, MATRIX_RATE, WEIGHT_DECAY
    )
    ffn_up = adamw(ffn_weight, ffn_grad, ffn_first, ffn_second, ffn_average, count, MATRIX_RATE, WEIGHT_DECAY)
    bias_up = adamw(up_bias, bias_grad, bias_first, bias_second, bias_average, count, VECTOR_RATE, 0.0)
    vec_up = adamw(vectors, vec_grad, vec_first, vec_second, vec_average, count, VECTOR_RATE, 0.0)
    news = [part[k] for k in range(4) for part in (attn_up, ffn_up, bias_up, vec_up)]
    return (layer_out, image_grads, attn_grad, ffn_grad, bias_grad, vec_grad, *news)


def solution(mesh):
    both = ("dp", "mp")
    matrix, slab, line = P(None, both), P(None, None, both), P(both)
    states = (matrix, slab, line, P())
    return jax.shard_map(
        body,
        mesh=mesh,
        in_specs=(P(both, None, None), P(both, None), line, line, line, P(both, None), *states * 4, P()),
        out_specs=(P(both, None), P(both, None, None), *states, *states * 4),
        check_vma=False,
    )
```

```python
import functools
import math

import jax
import jax.numpy as jnp
from jax import lax
from jax.experimental import pallas as pl
from jax.experimental.pallas import tpu as pltpu
from jax.sharding import PartitionSpec as P

HEADS = 6
HEAD = 64
PAIR = 2 * HEAD
PAIRS = HEADS // 2
BLK = 128
REACH = 5
CHUNKS = 32
HALF = CHUNKS // 2
EXTRA = 16
EXCLUDED = -8.0e9
INCLUDED = 3.0e38

NORM_EPS = 1e-06
BETA_ONE = 0.9
BETA_TWO = 0.999
ADAM_EPS = 1e-08
MATRIX_RATE = 0.05
VECTOR_RATE = 0.2
WEIGHT_DECAY = 0.05
AVERAGE_DECAY = 0.8

LOG2E = 1.4426950408889634
SCORE_LOG2 = LOG2E / math.sqrt(HEAD)
SCALE = 1.0 / math.sqrt(HEAD)

f32 = jnp.float32
bf16 = jnp.bfloat16
NN = (((1,), (0,)), ((), ()))
NT = (((1,), (1,)), ((), ()))
TN = (((0,), (0,)), ((), ()))
VM = pl.BlockSpec(memory_space=pltpu.VMEM)
SM = pl.BlockSpec(memory_space=pltpu.SMEM)
S = jax.ShapeDtypeStruct


def dot(left, right, dims=NN):
    return lax.dot_general(left, right, dims, preferred_element_type=f32)


def kernel_call(body, ins, outs, scratch=(), flops=0, micros=1, name=None, grid=(), out_specs=None):
    return pl.pallas_call(
        body,
        grid=grid,
        out_shape=outs,
        in_specs=ins,
        out_specs=out_specs or tuple(VM for _ in outs),
        scratch_shapes=list(scratch),
        compiler_params=pltpu.CompilerParams(vmem_limit_bytes=58 * 2**20),
        cost_estimate=pl.CostEstimate(flops=flops, bytes_accessed=micros * 3_500_000, transcendentals=0),
        name=name,
    )


def whole(shape):
    return pl.BlockSpec(shape, lambda i: (0,) * len(shape))


def row_sums(values):
    rows, width = values.shape
    return jnp.sum(values.reshape(rows // 8, 8, width), axis=0)


def norm_parts(values):
    scale = 1.0 / values.shape[-1]
    centre = jnp.sum(values, axis=-1, keepdims=True) * scale
    centred = values - centre
    spread = jnp.sum(centred * centred, axis=-1, keepdims=True) * scale
    inverse = lax.rsqrt(spread + NORM_EPS)
    return centred * inverse, inverse


def norm_back(unit, inverse, gain, grad):
    scale = 1.0 / unit.shape[-1]
    scaled = grad * gain
    mean = jnp.sum(scaled, axis=-1, keepdims=True) * scale
    along = jnp.sum(scaled * unit, axis=-1, keepdims=True) * scale
    return inverse * (scaled - mean - unit * along)


def tile_rows(count, size):
    return pl.ds(pl.multiple_of(count * size, size), size)


def place_of(own, other):
    apart = lax.shift_right_logical(own, 1) ^ (other // 2)
    return (apart & 3) * 4 + lax.shift_right_logical(apart, 2)


def spread_pieces(own, halves, out):
    for near in range(2):
        for slot in range(HALF):
            apart = near + 2 * ((slot // 4) + 4 * (slot % 4))
            out[own ^ apart] = halves[near][slot * out.shape[1] : (slot + 1) * out.shape[1], :]


def store_pieces(own, start, pieces, keep, send, at, step):
    count, size, _ = pieces.shape
    odd = (own & 1) == 1
    for e in range(0, count, 2):
        row = pl.multiple_of(place_of(own, start + e) * step + at, 16)
        even_piece, odd_piece = pieces[e], pieces[e + 1]
        keep[pl.ds(row, size), :] = jnp.where(odd, odd_piece, even_piece)
        send[pl.ds(row, size), :] = jnp.where(odd, even_piece, odd_piece)


def split_low(values):
    high = values.astype(bf16)
    return high, (values - high.astype(f32)).astype(bf16)


def combine_body(parts, size, extra, count, *refs):
    own, received, outs = refs[0], refs[1 : 1 + count], refs[1 + count :]
    base = parts * size
    for part in range(parts):
        rows = slice(part * size, (part + 1) * size)
        total = own[rows, :].astype(f32)
        for other in received:
            total = total + other[rows, :].astype(f32)
        if part == 0:
            outs[0][:size, :] = total
        else:
            outs[part][:size, :] = total.astype(bf16)
    if extra:
        if own.dtype == bf16:
            sums = [own[base : base + extra, :].astype(f32) + own[base + extra :, :].astype(f32)]
        else:
            sums = [own[base:, :]]
        sums += [r[base : base + extra, :].astype(f32) + r[base + extra :, :].astype(f32) for r in received]
        while len(sums) > 1:
            sums = [sums[i] + sums[i + 1] for i in range(0, len(sums), 2)]
        high, low = split_low(sums[0])
        outs[0][size:, :] = high.astype(f32) + low.astype(f32) if parts > 1 else sums[0]
        for out in outs[1:]:
            out[size : size + extra, :] = high
            out[size + extra :, :] = low


def combine_call(own, received, parts, extra):
    size = (received[0].shape[0] - 2 * extra) // parts
    width = own.shape[1]
    outs = (S((size + extra, width), f32),) + (S((size + 2 * extra, width), bf16),) * (parts - 1)
    return kernel_call(
        functools.partial(combine_body, parts, size, extra, len(received)),
        [VM] * (1 + len(received)),
        outs,
        flops=own.size * len(received),
        micros=2,
        name="combine",
    )(own, *received)


def over_core(values):
    return lax.ppermute(values, "mp", [(i, i ^ 1) for i in range(lax.axis_size("mp"))])


def over_plane(values, apart):
    devices = lax.axis_size("dp") * lax.axis_size("mp")
    return lax.ppermute(values, ("dp", "mp"), [(i, i ^ (2 * apart)) for i in range(devices)])


def over_line(values, apart):
    return lax.ppermute(values, "dp", [(i, i ^ (2 * apart)) for i in range(lax.axis_size("dp"))])


def tie(*values):
    return lax.optimization_barrier(values)


def gather_plane(pieces):
    return jnp.concatenate([pieces] + [over_plane(pieces, k) for k in (1, 2, 3)], axis=0)


def place_body(win, offs, images, keep, packed, acc, slots):
    images_here, length = keep.shape
    rows, width = packed.shape
    before = lax.broadcasted_iota(jnp.int32, (length, length), 0)
    after = lax.broadcasted_iota(jnp.int32, (length, length), 1)
    tri = jnp.where(before <= after, 1.0, 0.0).astype(bf16)
    kept = keep[...]
    ranks = dot(kept.astype(f32).astype(bf16), tri).astype(jnp.int32) - 1
    slots[...] = jnp.where(kept > 0, ranks, -4 * win)
    acc[0:8, :] = jnp.zeros((8, width), f32)
    place = lax.broadcasted_iota(jnp.int32, (win, length), 0)

    def one_image(i, carry):
        base = pl.multiple_of((offs[i] // 8) * 8, 8)
        shift = offs[i] - base
        chosen = jnp.where(place == slots[pl.ds(i, 1), :] + shift, 1.0, 0.0).astype(bf16)
        moved = dot(chosen, images[i])
        acc[pl.ds(base, 8), :] += moved[0:8]
        acc[pl.ds(base + 8, win - 8), :] = moved[8:]
        return carry

    lax.fori_loop(0, images_here, one_image, 0)
    packed[...] = acc[:rows, :].astype(bf16)


def place_call(images, keep, offs, rows):
    images_here, length, width = images.shape
    win = (length + 7 + 7) // 8 * 8
    return kernel_call(
        functools.partial(place_body, win),
        [SM, VM, VM],
        (S((rows, width), bf16),),
        [pltpu.VMEM((rows + win, width), f32), pltpu.VMEM((images_here, length), jnp.int32)],
        flops=2 * images_here * win * length * width,
        micros=9,
        name="place",
    )(offs, images, keep)[0]


def norm_body(packed, seg_rows, vec, normed, normed_t, seg_cols):
    rows, width = packed.shape

    def one_tile(i, carry):
        sl = tile_rows(i, 256)
        unit, _ = norm_parts(packed[sl, :].astype(f32))
        low = (unit * vec[0:1, :] + vec[1:2, :]).astype(bf16)
        normed[sl, :] = low
        normed_t[:, sl] = low.T
        return carry

    lax.fori_loop(0, rows // 256, one_tile, 0)

    def one_block(j, carry):
        line = seg_rows[pl.ds(j, 1), :]
        seg_cols[tile_rows(j, BLK), :] = jnp.broadcast_to(line, (BLK, BLK)).T
        return carry

    lax.fori_loop(0, rows // BLK, one_block, 0)


def norm_call(packed, seg_rows, vec):
    rows, width = packed.shape
    return kernel_call(
        norm_body,
        [VM, VM, VM],
        (S((rows, width), bf16), S((width, rows), bf16), S((rows, BLK), jnp.int32)),
        flops=rows * width * 12,
        micros=6,
        name="norm",
    )(packed, seg_rows, vec)


def window(seg, offs, counts, j, images_here, tiles):
    first = seg[j * BLK]
    last = seg[j * BLK + BLK - 1]
    used = last < images_here
    last_here = jnp.where(used, last, 0)
    end = jnp.where(used, offs[last_here] + counts[last_here], tiles * BLK)
    low = offs[first] // BLK
    size = jnp.maximum((end + BLK - 1) // BLK - low, 2)
    return jnp.minimum(low, tiles - size), size


def masked_pair(pair):
    lane = lax.broadcasted_iota(jnp.int32, pair.shape, 1)
    none = jnp.zeros_like(pair)
    return jnp.concatenate([jnp.where(lane < HEAD, pair, none), jnp.where(lane >= HEAD, pair, none)], axis=0)


def limits(seg_rows, seg_cols, j, keys):
    same = seg_cols[keys, :] == seg_rows[pl.ds(j, 1), :]
    lim = jnp.where(same, INCLUDED, EXCLUDED)
    return jnp.concatenate([lim, lim], axis=1)


def over_windows(seg, offs, counts, tiles, base, first, blocks, block):
    def one(j, carry):
        low, size = window(seg, offs, counts, j, offs.shape[0], tiles)
        for n in range(2, REACH + 1):

            @pl.when(size == n)
            def _():
                block(j, pl.ds(pl.multiple_of((low - base) * BLK, BLK), n * BLK))

        return carry

    lax.fori_loop(first, first + blocks, one, 0)


def attend_blocks(base, first, blocks, seg, offs, counts, qkv, value_t, seg_rows, seg_cols, mixed_t, stats):
    width = value_t.shape[0]
    tiles = seg.shape[0] // BLK

    def block(j, keys):
        here = tile_rows(j - base, BLK)
        there = tile_rows(j - first, BLK)
        lim = limits(seg_rows, seg_cols, j, keys)
        ats = [slice(p * PAIR, (p + 1) * PAIR) for p in range(PAIRS)]
        raws = [
            dot(qkv[keys, width + p * PAIR : width + (p + 1) * PAIR], masked_pair(qkv[here, ats[p]]), NT)
            for p in range(PAIRS)
        ]
        raws = [jnp.minimum(raw, lim) for raw in raws]
        tops = [jnp.max(raw, axis=0, keepdims=True) for raw in raws]
        expos = [jnp.exp2((raw - top) * SCORE_LOG2) for raw, top in zip(raws, tops)]
        totals = [jnp.sum(expo, axis=0, keepdims=True) for expo in expos]
        lows = [(expo * (1.0 / total)).astype(bf16) for expo, total in zip(expos, totals)]
        outs = [dot(value_t[at, keys], low) for at, low in zip(ats, lows)]
        for p in range(PAIRS):
            out = outs[p]
            mixed_t[p * PAIR : p * PAIR + HEAD, there] = out[:HEAD, :BLK].astype(bf16)
            mixed_t[p * PAIR + HEAD : (p + 1) * PAIR, there] = out[HEAD:, BLK:].astype(bf16)
            level = tops[p] * SCORE_LOG2 + jnp.log2(totals[p])
            stats[pl.ds(j - first, 1), p * 2 * BLK : (p + 1) * 2 * BLK] = level

    over_windows(seg, offs, counts, tiles, base, first, blocks, block)


def attend_first_body(
    own, seg, offs, counts, normed, mine, other, bias, seg_rows, seg_cols,
    qkv, key_t, value_t, w_t, mixed_t, stats,
):
    rows, width = normed.shape
    spread_pieces(own[0], (mine, other), w_t)
    units = w_t.shape[0] * w_t.shape[1]
    weights = w_t[...].reshape(units, width)[: 3 * width]

    def project(i, carry):
        sl = tile_rows(i, 512)
        low = (dot(normed[sl, :], weights, NT) + bias[...]).astype(bf16)
        qkv[sl, :] = low
        key_t[:, sl] = low[:, width : 2 * width].T
        value_t[:, sl] = low[:, 2 * width :].T
        return carry

    lax.fori_loop(0, rows // 512, project, 0)
    attend_blocks(
        0, 0, mixed_t.shape[1] // BLK, seg, offs, counts, qkv, value_t, seg_rows, seg_cols, mixed_t, stats
    )


def attend_first_call(blocks, own, seg, offs, counts, normed, mine, other, bias, seg_rows, seg_cols):
    rows, width = normed.shape
    piece = mine.shape[0] // HALF
    return kernel_call(
        attend_first_body,
        [SM, SM, SM, SM, VM, VM, VM, VM, VM, VM],
        (
            S((rows, 3 * width), bf16),
            S((width, rows), bf16),
            S((width, rows), bf16),
            S((CHUNKS, piece, width), bf16),
            S((width, blocks * BLK), bf16),
            S((blocks, HEADS * BLK), f32),
        ),
        flops=2 * rows * width * 3 * width,
        micros=20,
        name="attend_first",
    )(own, seg, offs, counts, normed, mine, other, bias, seg_rows, seg_cols)


def attend_last_call(blocks, seg, offs, counts, qkv, value_t, seg_rows, seg_cols):
    width, rows = value_t.shape
    part = (blocks + REACH - 1) * BLK
    while rows % part:
        part += BLK
    at = rows // part - 1
    tiles = rows // BLK
    return kernel_call(
        functools.partial(attend_blocks, tiles - part // BLK, tiles - blocks, blocks),
        [
            SM,
            SM,
            SM,
            pl.BlockSpec((part, 3 * width), lambda i: (at, 0)),
            pl.BlockSpec((width, part), lambda i: (0, at)),
            whole(seg_rows.shape),
            pl.BlockSpec((part, BLK), lambda i: (at, 0)),
        ],
        (S((width, blocks * BLK), bf16), S((blocks, HEADS * BLK), f32)),
        grid=(1,),
        out_specs=(whole((width, blocks * BLK)), whole((blocks, HEADS * BLK))),
        flops=4 * blocks * BLK * 512 * width,
        micros=5,
        name="attend_last",
    )(seg, offs, counts, qkv, value_t, seg_rows, seg_cols)


def attend_back(seg, offs, counts, qkv, key_t, mixed_grad, stats, seg_rows, seg_cols, qkv_grad, key_grad, value_grad):
    rows, width = mixed_grad.shape
    key_grad[...] = jnp.zeros_like(key_grad)
    value_grad[...] = jnp.zeros_like(value_grad)

    def block(j, keys):
        here = tile_rows(j, BLK)
        lim = limits(seg_rows, seg_cols, j, keys)
        ats = [slice(p * PAIR, (p + 1) * PAIR) for p in range(PAIRS)]
        levels = stats[pl.ds(j, 1), :]
        levels = [levels[:, p * 2 * BLK : (p + 1) * 2 * BLK] for p in range(PAIRS)]
        queries = [masked_pair(qkv[here, at]) for at in ats]
        outs = [masked_pair(mixed_grad[here, at]) for at in ats]
        raws = [
            dot(qkv[keys, width + p * PAIR : width + (p + 1) * PAIR], queries[p], NT) for p in range(PAIRS)
        ]
        grads = [
            dot(qkv[keys, 2 * width + p * PAIR : 2 * width + (p + 1) * PAIR], outs[p], NT) for p in range(PAIRS)
        ]
        probs = [jnp.exp2(jnp.minimum(raw, lim) * SCORE_LOG2 - level) for raw, level in zip(raws, levels)]
        inners = [jnp.sum(prob * grad, axis=0, keepdims=True) for prob, grad in zip(probs, grads)]
        lows = [prob.astype(bf16) for prob in probs]
        score_grads = [
            (prob * (grad - inner)).astype(bf16) for prob, grad, inner in zip(probs, grads, inners)
        ]
        for p in range(PAIRS):
            value_grad[keys, ats[p]] += dot(lows[p], outs[p])
        for p in range(PAIRS):
            key_grad[keys, ats[p]] += dot(score_grads[p], queries[p])
        for p in range(PAIRS):
            query_t = dot(key_t[ats[p], keys], score_grads[p]) * SCALE
            joined = jnp.concatenate([query_t[:HEAD, :BLK], query_t[HEAD:, BLK:]], axis=0)
            qkv_grad[here, ats[p]] = joined.T.astype(bf16)

    over_windows(seg, offs, counts, rows // BLK, 0, 0, rows // BLK, block)


def bias_line(rows_of, units):
    chunks, size = rows_of.shape
    column = lax.broadcasted_iota(jnp.int32, (size, units), 1)
    within = lax.broadcasted_iota(jnp.int32, (size, units), 0)
    repeat = jnp.where(column % size == within, 1.0, 0.0).astype(bf16)
    wide = dot(rows_of, repeat)
    owner = lax.broadcasted_iota(jnp.int32, (chunks, units), 1) // size
    mine = owner == lax.broadcasted_iota(jnp.int32, (chunks, units), 0)
    return jnp.sum(jnp.where(mine, wide, 0.0), axis=0, keepdims=True)


def feed_body(
    sub, own, packed, mixed_a, mixed_b, cot, vec, w_t, mine, other,
    layer_out, middle_grad, mixed_grad, keep, send,
    all_s, up_s, down_s, hid_s, gi_s, n2t_s, glt_s, bias_s, sums, bias_sum, mixed,
):
    size, width = packed.shape
    step, steps = pl.program_id(0), pl.num_programs(0)
    me = own[0]
    units = up_s.shape[0]
    piece = units // CHUNKS

    @pl.when(step == 0)
    def _():
        spread_pieces(me, (mine, other), all_s)
        up_s[...] = all_s[:, :piece, :].reshape(units, width)
        down_s[...] = all_s[:, piece : 2 * piece, :].reshape(units, width)
        bias_s[...] = bias_line(all_s[:, 2 * piece, :piece], units)
        bias_sum[...] = jnp.zeros_like(bias_sum)
        sums[...] = jnp.zeros_like(sums)

    @pl.when(step < steps - 1)
    def _():
        mixed[...] = mixed_a[...]

    @pl.when(step == steps - 1)
    def _():
        mixed[...] = mixed_b[...]

    w_out_t = w_t[...].reshape(width, width)
    parts = [slice(k * sub, (k + 1) * sub) for k in range(size // sub)]
    rows = [pl.ds(pl.multiple_of(step * size + k * sub, sub), sub) for k in range(size // sub)]
    mids = [packed[at, :].astype(f32) + dot(mixed[:, at].T, w_out_t, NT) + vec[4:5, :] for at in parts]
    units_of = [norm_parts(middle) for middle in mids]
    lows = [(unit * vec[5:6, :] + vec[6:7, :]).astype(bf16) for unit, _ in units_of]
    valids = [
        lax.broadcasted_iota(jnp.int32, (sub, 1), 0) + step * size + k * sub < steps * size - 1
        for k in range(size // sub)
    ]
    outs = [jnp.where(valid, cot[at, :].astype(f32), 0.0) for valid, at in zip(valids, parts)]
    out_lows = [out.astype(bf16) for out in outs]
    us = [dot(low, up_s[...], NT) + bias_s[...] for low in lows]
    grads = [dot(out_low, down_s[...], NT) for out_low in out_lows]
    downs, backs = [], []
    for k in range(size // sub):
        n2t_s[:, rows[k]] = lows[k].T
        glt_s[:, rows[k]] = out_lows[k].T
        u = us[k]
        phi = 0.5 + 0.5 * lax.erf(u * (1.0 / math.sqrt(2.0)))
        hidden = (u * phi).astype(bf16)
        hid_s[rows[k], :] = hidden
        slope = phi + u * jnp.exp2(u * u * (-0.5 * LOG2E)) * (1.0 / math.sqrt(2.0 * math.pi))
        grad_in = grads[k] * slope
        bias_sum[...] += row_sums(grad_in)
        grad_in_low = grad_in.astype(bf16)
        gi_s[rows[k], :] = grad_in_low
        downs.append(dot(hidden, down_s[...]))
        backs.append(dot(grad_in_low, up_s[...]))
    totals = []
    for k, at in enumerate(parts):
        unit, inverse = units_of[k]
        layer_out[at, :] = jnp.where(valids[k], mids[k] + downs[k] + vec[7:8, :], 0.0).astype(bf16)
        n2_grad = backs[k]
        sums[8:16, :] += row_sums(n2_grad * unit)
        sums[16:24, :] += row_sums(n2_grad)
        total = outs[k] + norm_back(unit, inverse, vec[5:6, :], n2_grad)
        middle_grad[at, :] = total
        sums[0:8, :] += row_sums(total)
        sums[24:32, :] += row_sums(outs[k])
        totals.append(total.astype(bf16))
    for k, at in enumerate(parts):
        mixed_grad[at, :] = dot(totals[k], w_out_t).astype(bf16)

    @pl.when(step == steps - 1)
    def _():
        wide = 2 * width
        for lower in range(0, units, wide):
            hs = slice(lower, lower + wide)
            for index, (left, right) in enumerate(((n2t_s, gi_s), (glt_s, hid_s))):
                pieces = dot(left[...], right[:, hs]).T.astype(bf16).reshape(wide // piece, piece, width)
                store_pieces(me, lower // piece, pieces, keep, send, index * piece, 2 * piece)
        line = jnp.sum(bias_sum[...], axis=0, keepdims=True)
        lines = [jnp.sum(sums[8 * row : 8 * row + 8, :], axis=0, keepdims=True) for row in range(4)]
        lines += [line[:, row * width : (row + 1) * width] for row in range(units // width)]
        store_extra(lines, keep, send)


def store_extra(lines, keep, send):
    width = keep.shape[1]
    lines = jnp.concatenate(lines + [jnp.zeros((EXTRA - len(lines), width), f32)], axis=0)
    high, low = split_low(lines)
    base = keep.shape[0] - 2 * EXTRA
    for out in (keep, send):
        out[base : base + EXTRA, :] = high
        out[base + EXTRA :, :] = low


def feed_call(own, packed, mixed_a, mixed_b, cot, vec, w_t, mine, other):
    rows, width = packed.shape
    units = 4 * width
    size = mixed_b.shape[1]
    steps = rows // size
    row_block = pl.BlockSpec((size, width), lambda i: (i, 0))
    sent = (units + 2 * EXTRA, width)
    return kernel_call(
        functools.partial(feed_body, size),
        [
            SM,
            row_block,
            pl.BlockSpec((width, size), lambda i: (0, jnp.minimum(i, steps - 2))),
            whole(mixed_b.shape),
            row_block,
            whole((8, width)),
            pl.BlockSpec((CHUNKS // 4, units // CHUNKS, width), lambda i: (3, 0, 0)),
            whole(mine.shape),
            whole(other.shape),
        ],
        (S((rows, width), bf16), S((rows, width), f32), S((rows, width), bf16), S(sent, bf16), S(sent, bf16)),
        [
            pltpu.VMEM((CHUNKS, mine.shape[0] // HALF, width), bf16),
            pltpu.VMEM((units, width), bf16),
            pltpu.VMEM((units, width), bf16),
            pltpu.VMEM((rows, units), bf16),
            pltpu.VMEM((rows, units), bf16),
            pltpu.VMEM((width, rows), bf16),
            pltpu.VMEM((width, rows), bf16),
            pltpu.VMEM((1, units), f32),
            pltpu.VMEM((32, width), f32),
            pltpu.VMEM((8, units), f32),
            pltpu.VMEM((width, size), bf16),
        ],
        grid=(steps,),
        out_specs=(row_block, row_block, row_block, whole(sent), whole(sent)),
        flops=12 * rows * width * units + 6 * rows * width * width,
        micros=30,
        name="feed",
    )(own, packed, mixed_a, mixed_b, cot, vec, w_t, mine, other)


def side_body(mixed_a, mixed_b, middle_grad, out_grad):
    first = mixed_a.shape[1]
    total = dot(mixed_a[...], middle_grad[:first, :].astype(bf16))
    total += dot(mixed_b[...], middle_grad[first:, :].astype(bf16))
    out_grad[...] = total.T.astype(bf16)


def side_call(mixed_a, mixed_b, middle_grad):
    rows, width = middle_grad.shape
    return kernel_call(
        side_body,
        [VM] * 3,
        (S((width, width), bf16),),
        flops=2 * rows * width * width,
        micros=4,
        name="side",
    )(mixed_a, mixed_b, middle_grad)[0]


def back_body(
    own, seg, offs, counts, qkv, key_t, mixed_grad, stats, seg_rows, seg_cols,
    w_t, packed, normed_t, middle_grad, out_grad, vec,
    input_grad, keep, send, qkv_grad, key_grad, value_grad, sums,
):
    rows, width = packed.shape
    me = own[0]
    piece = w_t.shape[1]
    size = 512
    attend_back(seg, offs, counts, qkv, key_t, mixed_grad, stats, seg_rows, seg_cols, qkv_grad, key_grad, value_grad)
    weights = w_t[: 3 * HALF // 2].reshape(3 * width, width)
    sums[...] = jnp.zeros_like(sums)

    def one(i, carry):
        sl = tile_rows(i, size)
        qkv_grad[sl, width : 2 * width] = (key_grad[sl, :] * SCALE).astype(bf16)
        qkv_grad[sl, 2 * width :] = value_grad[sl, :].astype(bf16)
        grads = qkv_grad[sl, :]
        normed_grad = dot(grads, weights)
        unit, inverse = norm_parts(packed[sl, :].astype(f32))
        sums[0:8, :] += row_sums(normed_grad * unit)
        sums[8:16, :] += row_sums(normed_grad)
        sums[16:24, :] += row_sums(grads[:, :width].astype(f32))
        sums[24:32, :] += row_sums(grads[:, 2 * width :].astype(f32))
        input_grad[sl, :] = middle_grad[sl, :] + norm_back(unit, inverse, vec[0:1, :], normed_grad)
        return carry

    lax.fori_loop(0, rows // size, one, 0)
    for lower in range(0, 3 * width, width):
        pieces = dot(normed_t[...], qkv_grad[:, lower : lower + width]).T.astype(bf16)
        store_pieces(me, lower // piece, pieces.reshape(width // piece, piece, width), keep, send, 0, piece)
    store_pieces(me, 3 * width // piece, out_grad[...].reshape(width // piece, piece, width), keep, send, 0, piece)
    lines = [jnp.sum(sums[8 * row : 8 * row + 8, :], axis=0, keepdims=True) for row in range(4)]
    store_extra(lines, keep, send)


def back_call(
    own, seg, offs, counts, qkv, key_t, mixed_grad, stats, seg_rows, seg_cols,
    w_t, packed, normed_t, middle_grad, out_grad, vec,
):
    rows, width = packed.shape
    sent = S((HALF * w_t.shape[1] + 2 * EXTRA, width), bf16)
    return kernel_call(
        back_body,
        [SM] * 4 + [VM] * 12,
        (S((rows, width), f32), sent, sent),
        [
            pltpu.VMEM((rows, 3 * width), bf16),
            pltpu.VMEM((rows, width), f32),
            pltpu.VMEM((rows, width), f32),
            pltpu.VMEM((32, width), f32),
        ],
        flops=22 * rows * width * width,
        micros=34,
        name="back",
    )(
        own, seg, offs, counts, qkv, key_t, mixed_grad, stats, seg_rows, seg_cols,
        w_t, packed, normed_t, middle_grad, out_grad, vec,
    )


def unpack_body(win, first, count, offs, keep, input_grad, *refs):
    image_grads, slots = refs[-2], refs[-1]
    images_here, length = keep.shape
    rows, width = input_grad.shape
    before = lax.broadcasted_iota(jnp.int32, (length, length), 0)
    after = lax.broadcasted_iota(jnp.int32, (length, length), 1)
    tri = jnp.where(before <= after, 1.0, 0.0).astype(bf16)
    place = lax.broadcasted_iota(jnp.int32, (win, length), 0)

    @pl.when(pl.program_id(0) == 0)
    def _():
        kept = keep[...]
        ranks = dot(kept.astype(f32).astype(bf16), tri).astype(jnp.int32) - 1
        slots[...] = jnp.where(kept > 0, ranks, -4 * win)

    chosen, values = [], []
    for k in range(image_grads.shape[0]):
        i = first + pl.program_id(0) * image_grads.shape[0] + k
        base = pl.multiple_of(jnp.minimum((offs[i] // 8) * 8, rows - win), 8)
        shift = offs[i] - base
        chosen.append(jnp.where(place == slots[pl.ds(i, 1), :] + shift, 1.0, 0.0).astype(bf16))
        values.append(input_grad[pl.ds(base, win), :])
    highs = [value.astype(bf16) for value in values]
    rests = [(value - high.astype(f32)).astype(bf16) for value, high in zip(values, highs)]
    for k in range(image_grads.shape[0]):
        image_grads[k] = dot(chosen[k], highs[k], TN) + dot(chosen[k], rests[k], TN)


def unpack_call(first, count, offs, keep, input_grad, filled=None):
    images_here, length = keep.shape
    rows, width = input_grad.shape
    win = (length + 7 + 7) // 8 * 8
    size = 5
    out = pl.BlockSpec((size, length, width), lambda i: (first // size + i, 0, 0))
    extra_in = [] if filled is None else [pl.BlockSpec(memory_space=pl.ANY)]
    extra = [] if filled is None else [filled]
    return pl.pallas_call(
        functools.partial(unpack_body, win, first, count),
        grid=(count // size,),
        out_shape=S((images_here, length, width), f32),
        in_specs=[SM, whole(keep.shape), whole(input_grad.shape)] + extra_in,
        out_specs=out,
        scratch_shapes=[pltpu.VMEM((images_here, length), jnp.int32)],
        input_output_aliases={} if filled is None else {3: 0},
        compiler_params=pltpu.CompilerParams(vmem_limit_bytes=58 * 2**20),
        cost_estimate=pl.CostEstimate(flops=0, bytes_accessed=7 * 3_500_000, transcendentals=0),
        name="unpack",
    )(offs, keep, input_grad, *extra)


def to_halves(chunks):
    _, size, width = chunks.shape
    ordered = chunks.reshape(4, 4, 2, size, width).transpose(2, 1, 0, 3, 4).reshape(2, HALF * size, width)
    return ordered[0], ordered[1]


def from_halves(keep, send, parts, width):
    size = keep.shape[0] // HALF // parts
    both = jnp.stack([keep, send]).reshape(2, 4, 4, parts, size, width)
    return both.transpose(2, 1, 0, 3, 4, 5).reshape(CHUNKS, parts, size, width)


def adamw(weight, grad, first, second, average, count, rate, decay):
    first_new = BETA_ONE * first + (1.0 - BETA_ONE) * grad
    second_new = BETA_TWO * second + (1.0 - BETA_TWO) * grad * grad
    first_hat = first_new / (1.0 - jnp.power(BETA_ONE, count))
    second_hat = second_new / (1.0 - jnp.power(BETA_TWO, count))
    weight_new = weight - rate * (first_hat / (jnp.sqrt(second_hat) + ADAM_EPS) + decay * weight)
    average_new = AVERAGE_DECAY * average + (1.0 - AVERAGE_DECAY) * weight_new
    return (weight_new, first_new, second_new, average_new)


def adamw_with(weight, grad, first, second, average, one, two, rate, decay):
    first_new = BETA_ONE * first + (1.0 - BETA_ONE) * grad
    second_new = BETA_TWO * second + (1.0 - BETA_TWO) * grad * grad
    weight_new = weight - rate * ((first_new / one) / (jnp.sqrt(second_new / two) + ADAM_EPS) + decay * weight)
    average_new = AVERAGE_DECAY * average + (1.0 - AVERAGE_DECAY) * weight_new
    return (weight_new, first_new, second_new, average_new)


def finish_body(powers, own, in_a, in_b, in_c, known, *refs):
    states, outs = refs[:8], refs[8:]
    size = states[0].shape[0]
    received = (in_a, in_b, in_c)
    grad = own[:size, :]
    for other in received:
        grad = grad + other[:size, :].astype(f32)
    sums = [own[size:, :]]
    sums += [r[size : size + EXTRA, :].astype(f32) + r[size + EXTRA :, :].astype(f32) for r in received]
    sums = (sums[0] + sums[1]) + (sums[2] + sums[3])
    vec_grad = jnp.concatenate([sums[:4], known[:4, :]], axis=0)
    news = adamw_with(states[0][...], grad, *(r[...] for r in states[1:4]), powers[0], powers[1], MATRIX_RATE, WEIGHT_DECAY)
    vec_news = adamw_with(states[4][...], vec_grad, *(r[...] for r in states[5:8]), powers[0], powers[1], VECTOR_RATE, 0.0)
    for ref, value in zip(outs, (grad, *news, vec_grad, *vec_news)):
        ref[...] = value


def finish_call(powers, own, received, known, states):
    main, vec = S(states[0].shape, f32), S(states[4].shape, f32)
    return kernel_call(
        finish_body,
        [SM] + [VM] * 13,
        (main,) * 5 + (vec,) * 5,
        micros=2,
        name="finish",
    )(powers, own, *received, known, *states)


def body(
    images, keep_mask, kept_counts, pack_offsets, segment_ids, cotangent,
    attn_weight, ffn_weight, up_bias, vectors,
    attn_first, ffn_first, bias_first, vec_first,
    attn_second, ffn_second, bias_second, vec_second,
    attn_average, ffn_average, bias_average, vec_average, step,
):
    width = images.shape[2]
    rows = segment_ids.shape[0]
    both = ("dp", "mp")
    piece = attn_weight.shape[1]
    tree = lax.axis_size("dp") == 8 and lax.axis_size("mp") == 4
    bias_row = jnp.pad(up_bias.astype(bf16)[None, :], ((0, 15), (0, width - piece)))
    seg_rows = segment_ids.reshape(rows // BLK, BLK)
    placed = place_call(images, keep_mask, pack_offsets, rows)
    count = step[0].astype(f32)
    powers = jnp.stack([1.0 - jnp.power(BETA_ONE, count), 1.0 - jnp.power(BETA_TWO, count)])
    if tree:
        own = (lax.axis_index("dp") * 4 + lax.axis_index("mp")).astype(jnp.int32)[None]
        pieces = jnp.concatenate(
            [attn_weight.astype(bf16).T, ffn_weight[0].astype(bf16).T, ffn_weight[1].astype(bf16).T, bias_row], axis=0
        )
        lines = [pieces] + [over_line(pieces, k) for k in (1, 2, 3)]
        placed, *lines = tie(placed, *lines)
        attn_line = jnp.concatenate([line[:piece] for line in lines], axis=0)
        ffn_line = jnp.concatenate([line[piece:] for line in lines], axis=0)
        attn_mine = gather_plane(attn_line)
        normed, normed_t, seg_cols = norm_call(placed, seg_rows, vectors)
        attn_mine, normed, ffn_line = tie(attn_mine, normed, ffn_line)
        attn_other = over_core(attn_mine)
        attn_other, ffn_line = tie(attn_other, ffn_line)
        ffn_lines = [ffn_line] + [over_plane(ffn_line, k) for k in (1, 2, 3)]
    else:
        own = jnp.zeros((1,), jnp.int32)
        attn_all = lax.all_gather(attn_weight.astype(bf16).T, both, axis=0, tiled=True)
        ffn_all = lax.all_gather(jnp.swapaxes(ffn_weight.astype(bf16), 1, 2), both, axis=1, tiled=True)
        bias_all = lax.all_gather(up_bias.astype(bf16), both, axis=0, tiled=True)
        size = 4 * width // CHUNKS
        ffn_all = jnp.concatenate(
            [
                ffn_all[0].reshape(CHUNKS, size, width),
                ffn_all[1].reshape(CHUNKS, size, width),
                jnp.pad(bias_all.reshape(CHUNKS, 1, size), ((0, 0), (0, 15), (0, width - size))),
            ],
            axis=1,
        )
        attn_mine, attn_other = to_halves(attn_all.reshape(CHUNKS, size, width))
        ffn_mine, ffn_other = to_halves(ffn_all)
        normed, normed_t, seg_cols = norm_call(placed, seg_rows, vectors)
    qkv_bias = jnp.concatenate([vectors[2], jnp.zeros_like(vectors[2]), vectors[3]])[None, :]
    where = (segment_ids, pack_offsets, kept_counts)
    blocks = rows // BLK
    late = blocks // 4
    qkv, key_t, value_t, w_t, mixed_a, stats_a = attend_first_call(
        blocks - late, own, *where, normed, attn_mine, attn_other, qkv_bias, seg_rows, seg_cols
    )
    if tree:
        qkv, mixed_a, *ffn_lines = tie(qkv, mixed_a, *ffn_lines)
        ffn_mine = jnp.concatenate(ffn_lines, axis=0)
        ffn_other = over_core(ffn_mine)
    mixed_b, stats_b = attend_last_call(late, *where, qkv, value_t, seg_rows, seg_cols)
    if tree:
        mixed_b, ffn_mine, ffn_other = tie(mixed_b, ffn_mine, ffn_other)
    layer_out, middle_grad, mixed_grad, ffn_keep, ffn_send = feed_call(
        own, placed, mixed_a, mixed_b, cotangent, vectors, w_t, ffn_mine, ffn_other
    )
    stats = jnp.concatenate([stats_a, stats_b], axis=0)
    if tree:
        ffn_in = over_core(ffn_send)
    out_grad = side_call(mixed_a, mixed_b, middle_grad)
    if tree:
        out_grad, ffn_in = tie(out_grad, ffn_in)
        ffn_own, *ffn_out = combine_call(ffn_keep, [ffn_in], 4, EXTRA)
        out_grad, ffn_own, *ffn_out = tie(out_grad, ffn_own, *ffn_out)
        ffn_in = [over_plane(p, k + 1) for k, p in enumerate(ffn_out)]
    input_grad, attn_keep, attn_send = back_call(
        own, *where, qkv, key_t, mixed_grad, stats, seg_rows, seg_cols,
        w_t, placed, normed_t, middle_grad, out_grad, vectors,
    )
    attn_states = (attn_weight, attn_first, attn_second, attn_average)
    vec_states = (vectors, vec_first, vec_second, vec_average)
    early = images.shape[0] * 2 // 5
    if tree:
        input_grad, attn_send, *ffn_in = tie(input_grad, attn_send, *ffn_in)
        attn_in = over_core(attn_send)
        ffn_own, *ffn_out = combine_call(ffn_own, ffn_in, 4, EXTRA)
        ffn_own, attn_in, *ffn_out = tie(ffn_own, attn_in, *ffn_out)
        attn_own, *attn_out = combine_call(attn_keep, [attn_in], 4, EXTRA)
        attn_in = [over_plane(p, k + 1) for k, p in enumerate(attn_out)]
        ffn_in = [over_line(p, k + 1) for k, p in enumerate(ffn_out)]
        image_grads = unpack_call(0, early, pack_offsets, keep_mask, input_grad)
        image_grads, *attn_in = tie(image_grads, *attn_in)
        attn_own, *attn_out = combine_call(attn_own, attn_in, 4, EXTRA)
        attn_in = [over_line(p, k + 1) for k, p in enumerate(attn_out)]
        image_grads = unpack_call(early, images.shape[0] - early, pack_offsets, keep_mask, input_grad, image_grads)
        ffn_t = combine_call(ffn_own, ffn_in, 1, EXTRA)[0]
        image_grads, *attn_in = tie(image_grads, *attn_in)
        ffn_grad = jnp.swapaxes(ffn_t[: 2 * piece].reshape(2, piece, width), 1, 2)
        known = ffn_t[2 * piece :]
        finished = finish_call(powers, attn_own, attn_in, known, [v.T for v in attn_states] + list(vec_states))
        attn_grad, *attn_up = [v.T for v in finished[:5]]
        vec_grad, *vec_up = finished[5:]
        bias_sums = known[4:8]
    else:
        image_grads = unpack_call(0, images.shape[0], pack_offsets, keep_mask, input_grad)
        base = ffn_keep.shape[0] - 2 * EXTRA
        ffn_t = from_halves(ffn_keep[:base], ffn_send[:base], 2, width)
        ffn_t = jnp.swapaxes(ffn_t, 0, 1).reshape(2, 4 * width, width)
        ffn_t = lax.psum_scatter(ffn_t.astype(f32), both, scatter_dimension=1, tiled=True)
        ffn_grad = jnp.swapaxes(ffn_t, 1, 2)
        known = ffn_keep[base : base + EXTRA].astype(f32) + ffn_keep[base + EXTRA :].astype(f32)
        base = attn_keep.shape[0] - 2 * EXTRA
        attn_t = from_halves(attn_keep[:base], attn_send[:base], 1, width).reshape(4 * width, width)
        attn_grad = lax.psum_scatter(attn_t.astype(f32), both, scatter_dimension=0, tiled=True).T
        sums = attn_keep[base : base + EXTRA].astype(f32) + attn_keep[base + EXTRA :].astype(f32)
        sums = lax.psum(jnp.concatenate([sums[:4], known[:8]], axis=0), both)
        vec_grad, bias_sums = sums[:8], sums[8:]
        attn_up = adamw(attn_weight, attn_grad, *attn_states[1:], count, MATRIX_RATE, WEIGHT_DECAY)
        vec_up = adamw(vectors, vec_grad, *vec_states[1:], count, VECTOR_RATE, 0.0)
    index = lax.axis_index("dp") * lax.axis_size("mp") + lax.axis_index("mp")
    bias_grad = lax.dynamic_slice_in_dim(bias_sums.reshape(4 * width), index * piece, piece, 0)
    ffn_up = adamw(ffn_weight, ffn_grad, ffn_first, ffn_second, ffn_average, count, MATRIX_RATE, WEIGHT_DECAY)
    bias_up = adamw(up_bias, bias_grad, bias_first, bias_second, bias_average, count, VECTOR_RATE, 0.0)
    news = [part[k] for k in range(4) for part in (attn_up, ffn_up, bias_up, vec_up)]
    return (layer_out, image_grads, attn_grad, ffn_grad, bias_grad, vec_grad, *news)


def solution(mesh):
    both = ("dp", "mp")
    matrix, slab, line = P(None, both), P(None, None, both), P(both)
    states = (matrix, slab, line, P())
    return jax.shard_map(
        body,
        mesh=mesh,
        in_specs=(P(both, None, None), P(both, None), line, line, line, P(both, None), *states * 4, P()),
        out_specs=(P(both, None), P(both, None, None), *states, *states * 4),
        check_vma=False,
    )
```

```python
import functools
import math

import jax
import jax.numpy as jnp
from jax import lax
from jax.experimental import pallas as pl
from jax.experimental.pallas import tpu as pltpu
from jax.sharding import PartitionSpec as P

HEADS = 6
HEAD = 64
PAIR = 2 * HEAD
PAIRS = HEADS // 2
BLK = 128
REACH = 5
CHUNKS = 32
HALF = CHUNKS // 2
EXTRA = 16
EXCLUDED = -8.0e9
INCLUDED = 3.0e38

NORM_EPS = 1e-06
BETA_ONE = 0.9
BETA_TWO = 0.999
ADAM_EPS = 1e-08
MATRIX_RATE = 0.05
VECTOR_RATE = 0.2
WEIGHT_DECAY = 0.05
AVERAGE_DECAY = 0.8

LOG2E = 1.4426950408889634
SCORE_LOG2 = LOG2E / math.sqrt(HEAD)
SCALE = 1.0 / math.sqrt(HEAD)

f32 = jnp.float32
bf16 = jnp.bfloat16
NN = (((1,), (0,)), ((), ()))
NT = (((1,), (1,)), ((), ()))
TN = (((0,), (0,)), ((), ()))
VM = pl.BlockSpec(memory_space=pltpu.VMEM)
SM = pl.BlockSpec(memory_space=pltpu.SMEM)
HB = pl.BlockSpec(memory_space=pl.ANY)
S = jax.ShapeDtypeStruct


def dot(left, right, dims=NN):
    return lax.dot_general(left, right, dims, preferred_element_type=f32)


def kernel_call(body, ins, outs, scratch=(), flops=0, micros=1, name=None, grid=(), out_specs=None):
    return pl.pallas_call(
        body,
        grid=grid,
        out_shape=outs,
        in_specs=ins,
        out_specs=out_specs or tuple(VM for _ in outs),
        scratch_shapes=list(scratch),
        compiler_params=pltpu.CompilerParams(vmem_limit_bytes=58 * 2**20),
        cost_estimate=pl.CostEstimate(flops=flops, bytes_accessed=micros * 3_500_000, transcendentals=0),
        name=name,
    )


def whole(shape):
    return pl.BlockSpec(shape, lambda i: (0,) * len(shape))


def row_sums(values):
    rows, width = values.shape
    return jnp.sum(values.reshape(rows // 8, 8, width), axis=0)


def norm_parts(values):
    scale = 1.0 / values.shape[-1]
    centre = jnp.sum(values, axis=-1, keepdims=True) * scale
    centred = values - centre
    spread = jnp.sum(centred * centred, axis=-1, keepdims=True) * scale
    inverse = lax.rsqrt(spread + NORM_EPS)
    return centred * inverse, inverse


def norm_back(unit, inverse, gain, grad):
    scale = 1.0 / unit.shape[-1]
    scaled = grad * gain
    mean = jnp.sum(scaled, axis=-1, keepdims=True) * scale
    along = jnp.sum(scaled * unit, axis=-1, keepdims=True) * scale
    return inverse * (scaled - mean - unit * along)


def tile_rows(count, size):
    return pl.ds(pl.multiple_of(count * size, size), size)


def plane_first(apart):
    return (apart & 3) * 4 + lax.shift_right_logical(apart, 2)


def line_first(apart):
    return apart


def spread_pieces(own, halves, out):
    for near in range(2):
        for slot in range(HALF):
            apart = near + 2 * ((slot // 4) + 4 * (slot % 4))
            out[own ^ apart] = halves[near][slot * out.shape[1] : (slot + 1) * out.shape[1], :]


def store_pieces(own, start, pieces, keep, send, at, step, order):
    count, size, _ = pieces.shape
    odd = (own & 1) == 1
    for e in range(0, count, 2):
        apart = lax.shift_right_logical(own, 1) ^ ((start + e) // 2)
        row = pl.multiple_of(order(apart) * step + at, 16)
        even_piece, odd_piece = pieces[e], pieces[e + 1]
        keep[pl.ds(row, size), :] = jnp.where(odd, odd_piece, even_piece)
        send[pl.ds(row, size), :] = jnp.where(odd, even_piece, odd_piece)


def split_low(values):
    high = values.astype(bf16)
    return high, (values - high.astype(f32)).astype(bf16)


def combine_body(parts, size, extra, count, *refs):
    own, received, outs = refs[0], refs[1 : 1 + count], refs[1 + count :]
    base = parts * size
    for part in range(parts):
        rows = slice(part * size, (part + 1) * size)
        total = own[rows, :].astype(f32)
        for other in received:
            total = total + other[rows, :].astype(f32)
        if part == 0:
            outs[0][:size, :] = total
        else:
            outs[part][:size, :] = total.astype(bf16)
    if extra:
        if own.dtype == bf16:
            sums = [own[base : base + extra, :].astype(f32) + own[base + extra :, :].astype(f32)]
        else:
            sums = [own[base:, :]]
        sums += [r[base : base + extra, :].astype(f32) + r[base + extra :, :].astype(f32) for r in received]
        while len(sums) > 1:
            sums = [sums[i] + sums[i + 1] for i in range(0, len(sums), 2)]
        high, low = split_low(sums[0])
        outs[0][size:, :] = high.astype(f32) + low.astype(f32) if parts > 1 else sums[0]
        for out in outs[1:]:
            out[size : size + extra, :] = high
            out[size + extra :, :] = low


def combine_call(own, received, parts, extra):
    size = (received[0].shape[0] - 2 * extra) // parts
    width = own.shape[1]
    outs = (S((size + extra, width), f32),) + (S((size + 2 * extra, width), bf16),) * (parts - 1)
    return kernel_call(
        functools.partial(combine_body, parts, size, extra, len(received)),
        [VM] * (1 + len(received)),
        outs,
        flops=own.size * len(received),
        micros=2,
        name="combine",
    )(own, *received)


def over_core(values):
    return lax.ppermute(values, "mp", [(i, i ^ 1) for i in range(lax.axis_size("mp"))])


def over_plane(values, apart):
    devices = lax.axis_size("dp") * lax.axis_size("mp")
    return lax.ppermute(values, ("dp", "mp"), [(i, i ^ (2 * apart)) for i in range(devices)])


def over_line(values, apart):
    return lax.ppermute(values, "dp", [(i, i ^ (2 * apart)) for i in range(lax.axis_size("dp"))])


def tie(*values):
    return lax.optimization_barrier(values)


def gather_plane(pieces):
    return jnp.concatenate([pieces] + [over_plane(pieces, k) for k in (1, 2, 3)], axis=0)


def place_body(win, offs, images, keep, packed, acc, slots):
    images_here, length = keep.shape
    rows, width = packed.shape
    before = lax.broadcasted_iota(jnp.int32, (length, length), 0)
    after = lax.broadcasted_iota(jnp.int32, (length, length), 1)
    tri = jnp.where(before <= after, 1.0, 0.0).astype(bf16)
    kept = keep[...]
    ranks = dot(kept.astype(f32).astype(bf16), tri).astype(jnp.int32) - 1
    slots[...] = jnp.where(kept > 0, ranks, -4 * win)
    acc[0:8, :] = jnp.zeros((8, width), f32)
    place = lax.broadcasted_iota(jnp.int32, (win, length), 0)

    def one_image(i, carry):
        base = pl.multiple_of((offs[i] // 8) * 8, 8)
        shift = offs[i] - base
        chosen = jnp.where(place == slots[pl.ds(i, 1), :] + shift, 1.0, 0.0).astype(bf16)
        moved = dot(chosen, images[i])
        acc[pl.ds(base, 8), :] += moved[0:8]
        acc[pl.ds(base + 8, win - 8), :] = moved[8:]
        return carry

    lax.fori_loop(0, images_here, one_image, 0)
    packed[...] = acc[:rows, :].astype(bf16)


def place_call(images, keep, offs, rows):
    images_here, length, width = images.shape
    win = (length + 7 + 7) // 8 * 8
    return kernel_call(
        functools.partial(place_body, win),
        [SM, VM, VM],
        (S((rows, width), bf16),),
        [pltpu.VMEM((rows + win, width), f32), pltpu.VMEM((images_here, length), jnp.int32)],
        flops=2 * images_here * win * length * width,
        micros=9,
        name="place",
    )(offs, images, keep)[0]


def norm_body(packed, seg_rows, vec, normed, normed_t, seg_cols):
    rows, width = packed.shape

    def one_tile(i, carry):
        sl = tile_rows(i, 256)
        unit, _ = norm_parts(packed[sl, :].astype(f32))
        low = (unit * vec[0:1, :] + vec[1:2, :]).astype(bf16)
        normed[sl, :] = low
        normed_t[:, sl] = low.T
        return carry

    lax.fori_loop(0, rows // 256, one_tile, 0)

    def one_block(j, carry):
        line = seg_rows[pl.ds(j, 1), :]
        seg_cols[tile_rows(j, BLK), :] = jnp.broadcast_to(line, (BLK, BLK)).T
        return carry

    lax.fori_loop(0, rows // BLK, one_block, 0)


def norm_call(packed, seg_rows, vec):
    rows, width = packed.shape
    return kernel_call(
        norm_body,
        [VM, VM, VM],
        (S((rows, width), bf16), S((width, rows), bf16), S((rows, BLK), jnp.int32)),
        flops=rows * width * 12,
        micros=6,
        name="norm",
    )(packed, seg_rows, vec)


def window(seg, offs, counts, j, images_here, tiles):
    first = seg[j * BLK]
    last = seg[j * BLK + BLK - 1]
    used = last < images_here
    last_here = jnp.where(used, last, 0)
    end = jnp.where(used, offs[last_here] + counts[last_here], tiles * BLK)
    low = offs[first] // BLK
    size = jnp.maximum((end + BLK - 1) // BLK - low, 2)
    return jnp.minimum(low, tiles - size), size


def masked_pair(pair):
    lane = lax.broadcasted_iota(jnp.int32, pair.shape, 1)
    none = jnp.zeros_like(pair)
    return jnp.concatenate([jnp.where(lane < HEAD, pair, none), jnp.where(lane >= HEAD, pair, none)], axis=0)


def limits(seg_rows, seg_cols, j, keys):
    same = seg_cols[keys, :] == seg_rows[pl.ds(j, 1), :]
    lim = jnp.where(same, INCLUDED, EXCLUDED)
    return jnp.concatenate([lim, lim], axis=1)


def over_windows(seg, offs, counts, tiles, base, first, blocks, block, before=None):
    def one(j, carry):
        if before is not None:
            before(j)
        low, size = window(seg, offs, counts, j, offs.shape[0], tiles)
        for n in range(2, REACH + 1):

            @pl.when(size == n)
            def _():
                block(j, pl.ds(pl.multiple_of((low - base) * BLK, BLK), n * BLK))

        return carry

    lax.fori_loop(first, first + blocks, one, 0)


def attend_blocks(base, first, blocks, seg, offs, counts, qkv, value_t, seg_rows, seg_cols, mixed_t, stats):
    width = value_t.shape[0]
    tiles = seg.shape[0] // BLK

    def block(j, keys):
        here = tile_rows(j - base, BLK)
        there = tile_rows(j - first, BLK)
        lim = limits(seg_rows, seg_cols, j, keys)
        ats = [slice(p * PAIR, (p + 1) * PAIR) for p in range(PAIRS)]
        raws = [
            dot(qkv[keys, width + p * PAIR : width + (p + 1) * PAIR], masked_pair(qkv[here, ats[p]]), NT)
            for p in range(PAIRS)
        ]
        raws = [jnp.minimum(raw, lim) for raw in raws]
        tops = [jnp.max(raw, axis=0, keepdims=True) for raw in raws]
        expos = [jnp.exp2((raw - top) * SCORE_LOG2) for raw, top in zip(raws, tops)]
        totals = [jnp.sum(expo, axis=0, keepdims=True) for expo in expos]
        lows = [(expo * (1.0 / total)).astype(bf16) for expo, total in zip(expos, totals)]
        outs = [dot(value_t[at, keys], low) for at, low in zip(ats, lows)]
        for p in range(PAIRS):
            out = outs[p]
            mixed_t[p * PAIR : p * PAIR + HEAD, there] = out[:HEAD, :BLK].astype(bf16)
            mixed_t[p * PAIR + HEAD : (p + 1) * PAIR, there] = out[HEAD:, BLK:].astype(bf16)
            level = tops[p] * SCORE_LOG2 + jnp.log2(totals[p])
            stats[pl.ds(j - first, 1), p * 2 * BLK : (p + 1) * 2 * BLK] = level

    over_windows(seg, offs, counts, tiles, base, first, blocks, block)


def attend_first_body(
    own, seg, offs, counts, normed, mine, other, vec, seg_rows, seg_cols,
    qkv_out, key_out, value_out, w_out, mixed_t, stats,
    qkv, key_t, value_t, w_t, sems,
):
    rows, width = normed.shape
    size = 512
    spread_pieces(own[0], (mine, other), w_t)
    units = w_t.shape[0] * w_t.shape[1]
    weights = w_t[...].reshape(units, width)[: 3 * width]
    bias = jnp.concatenate([vec[2:3, :], jnp.zeros((1, width), f32), vec[3:4, :]], axis=1)
    last = pltpu.make_async_copy(w_t, w_out, sems.at[3, 0])
    last.start()

    def copies(i):
        sl = tile_rows(i, size)
        return [
            pltpu.make_async_copy(qkv.at[sl, :], qkv_out.at[sl, :], sems.at[0, i]),
            pltpu.make_async_copy(key_t.at[:, sl], key_out.at[:, sl], sems.at[1, i]),
            pltpu.make_async_copy(value_t.at[:, sl], value_out.at[:, sl], sems.at[2, i]),
        ]

    def project(i, carry):
        sl = tile_rows(i, size)
        low = (dot(normed[sl, :], weights, NT) + bias).astype(bf16)
        qkv[sl, :] = low
        key_t[:, sl] = low[:, width : 2 * width].T
        value_t[:, sl] = low[:, 2 * width :].T
        for copy in copies(i):
            copy.start()
        return carry

    lax.fori_loop(0, rows // size, project, 0)
    attend_blocks(
        0, 0, mixed_t.shape[1] // BLK, seg, offs, counts, qkv, value_t, seg_rows, seg_cols, mixed_t, stats
    )
    for i in range(rows // size):
        for copy in copies(i):
            copy.wait()
    last.wait()


def attend_first_call(blocks, own, seg, offs, counts, normed, mine, other, vec, seg_rows, seg_cols):
    rows, width = normed.shape
    piece = mine.shape[0] // HALF
    kept = ((rows, 3 * width), (width, rows), (width, rows), (CHUNKS, piece, width))
    return kernel_call(
        attend_first_body,
        [SM, SM, SM, SM, VM, VM, VM, VM, VM, VM],
        tuple(S(shape, bf16) for shape in kept)
        + (S((width, blocks * BLK), bf16), S((blocks, HEADS * BLK), f32)),
        [pltpu.VMEM(shape, bf16) for shape in kept] + [pltpu.SemaphoreType.DMA((4, rows // 512))],
        flops=2 * rows * width * 3 * width,
        micros=20,
        name="attend_first",
        out_specs=(HB, HB, HB, HB, VM, VM),
    )(own, seg, offs, counts, normed, mine, other, vec, seg_rows, seg_cols)


def attend_last_call(blocks, seg, offs, counts, qkv, value_t, seg_rows, seg_cols):
    width, rows = value_t.shape
    part = (blocks + REACH - 1) * BLK
    while rows % part:
        part += BLK
    at = rows // part - 1
    tiles = rows // BLK
    return kernel_call(
        functools.partial(attend_blocks, tiles - part // BLK, tiles - blocks, blocks),
        [
            SM,
            SM,
            SM,
            pl.BlockSpec((part, 3 * width), lambda i: (at, 0)),
            pl.BlockSpec((width, part), lambda i: (0, at)),
            whole(seg_rows.shape),
            pl.BlockSpec((part, BLK), lambda i: (at, 0)),
        ],
        (S((width, blocks * BLK), bf16), S((blocks, HEADS * BLK), f32)),
        grid=(1,),
        out_specs=(whole((width, blocks * BLK)), whole((blocks, HEADS * BLK))),
        flops=4 * blocks * BLK * 512 * width,
        micros=5,
        name="attend_last",
    )(seg, offs, counts, qkv, value_t, seg_rows, seg_cols)


def attend_back(
    seg, offs, counts, qkv, key_t, mixed_grad, stats_a, stats_b, seg_rows, seg_cols, qkv_grad, key_grad, value_grad, stats, before
):
    rows, width = mixed_grad.shape
    key_grad[...] = jnp.zeros_like(key_grad)
    value_grad[...] = jnp.zeros_like(value_grad)
    stats[: stats_a.shape[0], :] = stats_a[...]
    stats[stats_a.shape[0] :, :] = stats_b[...]

    def block(j, keys):
        here = tile_rows(j, BLK)
        lim = limits(seg_rows, seg_cols, j, keys)
        ats = [slice(p * PAIR, (p + 1) * PAIR) for p in range(PAIRS)]
        levels = stats[pl.ds(j, 1), :]
        levels = [levels[:, p * 2 * BLK : (p + 1) * 2 * BLK] for p in range(PAIRS)]
        queries = [masked_pair(qkv[here, at]) for at in ats]
        outs = [masked_pair(mixed_grad[here, at]) for at in ats]
        raws = [
            dot(qkv[keys, width + p * PAIR : width + (p + 1) * PAIR], queries[p], NT) for p in range(PAIRS)
        ]
        grads = [
            dot(qkv[keys, 2 * width + p * PAIR : 2 * width + (p + 1) * PAIR], outs[p], NT) for p in range(PAIRS)
        ]
        probs = [jnp.exp2(jnp.minimum(raw, lim) * SCORE_LOG2 - level) for raw, level in zip(raws, levels)]
        inners = [jnp.sum(prob * grad, axis=0, keepdims=True) for prob, grad in zip(probs, grads)]
        lows = [prob.astype(bf16) for prob in probs]
        score_grads = [
            (prob * (grad - inner)).astype(bf16) for prob, grad, inner in zip(probs, grads, inners)
        ]
        for p in range(PAIRS):
            value_grad[keys, ats[p]] += dot(lows[p], outs[p])
        for p in range(PAIRS):
            key_grad[keys, ats[p]] += dot(score_grads[p], queries[p])
        for p in range(PAIRS):
            query_t = dot(key_t[ats[p], keys], score_grads[p]) * SCALE
            joined = jnp.concatenate([query_t[:HEAD, :BLK], query_t[HEAD:, BLK:]], axis=0)
            qkv_grad[here, ats[p]] = joined.T.astype(bf16)

    over_windows(seg, offs, counts, rows // BLK, 0, 0, rows // BLK, block, before)


def bias_line(rows_of, units):
    chunks, size = rows_of.shape
    column = lax.broadcasted_iota(jnp.int32, (size, units), 1)
    within = lax.broadcasted_iota(jnp.int32, (size, units), 0)
    repeat = jnp.where(column % size == within, 1.0, 0.0).astype(bf16)
    wide = dot(rows_of, repeat)
    owner = lax.broadcasted_iota(jnp.int32, (chunks, units), 1) // size
    mine = owner == lax.broadcasted_iota(jnp.int32, (chunks, units), 0)
    return jnp.sum(jnp.where(mine, wide, 0.0), axis=0, keepdims=True)


def feed_body(
    sub, own, packed, mixed_a, mixed_b, cot, vec, w_t, mine, other,
    layer_out, middle_grad, mixed_grad, keep, send,
    all_s, up_s, down_s, hid_s, gi_s, n2t_s, glt_s, bias_s, sums, bias_sum, mixed,
):
    size, width = packed.shape
    step, steps = pl.program_id(0), pl.num_programs(0)
    me = own[0]
    units = up_s.shape[0]
    piece = units // CHUNKS

    @pl.when(step == 0)
    def _():
        spread_pieces(me, (mine, other), all_s)
        up_s[...] = all_s[:, :piece, :].reshape(units, width)
        down_s[...] = all_s[:, piece : 2 * piece, :].reshape(units, width)
        bias_s[...] = bias_line(all_s[:, 2 * piece, :piece], units)
        bias_sum[...] = jnp.zeros_like(bias_sum)
        sums[...] = jnp.zeros_like(sums)

    @pl.when(step < steps - 1)
    def _():
        mixed[...] = mixed_a[...]

    @pl.when(step == steps - 1)
    def _():
        mixed[...] = mixed_b[...]

    w_out_t = w_t[...].reshape(width, width)
    parts = [slice(k * sub, (k + 1) * sub) for k in range(size // sub)]
    rows = [pl.ds(pl.multiple_of(step * size + k * sub, sub), sub) for k in range(size // sub)]
    mids = [packed[at, :].astype(f32) + dot(mixed[:, at].T, w_out_t, NT) + vec[4:5, :] for at in parts]
    units_of = [norm_parts(middle) for middle in mids]
    lows = [(unit * vec[5:6, :] + vec[6:7, :]).astype(bf16) for unit, _ in units_of]
    valids = [
        lax.broadcasted_iota(jnp.int32, (sub, 1), 0) + step * size + k * sub < steps * size - 1
        for k in range(size // sub)
    ]
    outs = [jnp.where(valid, cot[at, :].astype(f32), 0.0) for valid, at in zip(valids, parts)]
    out_lows = [out.astype(bf16) for out in outs]
    us = [dot(low, up_s[...], NT) + bias_s[...] for low in lows]
    grads = [dot(out_low, down_s[...], NT) for out_low in out_lows]
    downs, backs = [], []
    for k in range(size // sub):
        n2t_s[:, rows[k]] = lows[k].T
        glt_s[:, rows[k]] = out_lows[k].T
        u = us[k]
        phi = 0.5 + 0.5 * lax.erf(u * (1.0 / math.sqrt(2.0)))
        hidden = (u * phi).astype(bf16)
        hid_s[rows[k], :] = hidden
        slope = phi + u * jnp.exp2(u * u * (-0.5 * LOG2E)) * (1.0 / math.sqrt(2.0 * math.pi))
        grad_in = grads[k] * slope
        bias_sum[...] += row_sums(grad_in)
        grad_in_low = grad_in.astype(bf16)
        gi_s[rows[k], :] = grad_in_low
        downs.append(dot(hidden, down_s[...]))
        backs.append(dot(grad_in_low, up_s[...]))
    totals = []
    for k, at in enumerate(parts):
        unit, inverse = units_of[k]
        layer_out[at, :] = jnp.where(valids[k], mids[k] + downs[k] + vec[7:8, :], 0.0).astype(bf16)
        n2_grad = backs[k]
        sums[8:16, :] += row_sums(n2_grad * unit)
        sums[16:24, :] += row_sums(n2_grad)
        total = outs[k] + norm_back(unit, inverse, vec[5:6, :], n2_grad)
        middle_grad[at, :] = total
        sums[0:8, :] += row_sums(total)
        sums[24:32, :] += row_sums(outs[k])
        totals.append(total.astype(bf16))
    for k, at in enumerate(parts):
        mixed_grad[at, :] = dot(totals[k], w_out_t).astype(bf16)

    @pl.when(step == steps - 1)
    def _():
        wide = 2 * width
        for lower in range(0, units, wide):
            hs = slice(lower, lower + wide)
            for index, (left, right) in enumerate(((n2t_s, gi_s), (glt_s, hid_s))):
                pieces = dot(left[...], right[:, hs]).T.astype(bf16).reshape(wide // piece, piece, width)
                store_pieces(me, lower // piece, pieces, keep, send, index * piece, 2 * piece, line_first)
        line = jnp.sum(bias_sum[...], axis=0, keepdims=True)
        lines = [jnp.sum(sums[8 * row : 8 * row + 8, :], axis=0, keepdims=True) for row in range(4)]
        lines += [line[:, row * width : (row + 1) * width] for row in range(units // width)]
        store_extra(lines, keep, send)


def store_extra(lines, keep, send):
    width = keep.shape[1]
    lines = jnp.concatenate(lines + [jnp.zeros((EXTRA - len(lines), width), f32)], axis=0)
    high, low = split_low(lines)
    base = keep.shape[0] - 2 * EXTRA
    for out in (keep, send):
        out[base : base + EXTRA, :] = high
        out[base + EXTRA :, :] = low


def feed_call(own, packed, mixed_a, mixed_b, cot, vec, w_t, mine, other):
    rows, width = packed.shape
    units = 4 * width
    size = mixed_b.shape[1]
    steps = rows // size
    row_block = pl.BlockSpec((size, width), lambda i: (i, 0))
    sent = (units + 2 * EXTRA, width)
    return kernel_call(
        functools.partial(feed_body, size),
        [
            SM,
            row_block,
            pl.BlockSpec((width, size), lambda i: (0, jnp.minimum(i, steps - 2))),
            whole(mixed_b.shape),
            row_block,
            whole((8, width)),
            pl.BlockSpec((CHUNKS // 4, units // CHUNKS, width), lambda i: (3, 0, 0)),
            whole(mine.shape),
            whole(other.shape),
        ],
        (S((rows, width), bf16), S((rows, width), f32), S((rows, width), bf16), S(sent, bf16), S(sent, bf16)),
        [
            pltpu.VMEM((CHUNKS, mine.shape[0] // HALF, width), bf16),
            pltpu.VMEM((units, width), bf16),
            pltpu.VMEM((units, width), bf16),
            pltpu.VMEM((rows, units), bf16),
            pltpu.VMEM((rows, units), bf16),
            pltpu.VMEM((width, rows), bf16),
            pltpu.VMEM((width, rows), bf16),
            pltpu.VMEM((1, units), f32),
            pltpu.VMEM((32, width), f32),
            pltpu.VMEM((8, units), f32),
            pltpu.VMEM((width, size), bf16),
        ],
        grid=(steps,),
        out_specs=(row_block, row_block, row_block, whole(sent), whole(sent)),
        flops=12 * rows * width * units + 6 * rows * width * width,
        micros=30,
        name="feed",
    )(own, packed, mixed_a, mixed_b, cot, vec, w_t, mine, other)


def side_body(mixed_a, mixed_b, middle_grad, out_grad):
    first = mixed_a.shape[1]
    total = dot(mixed_a[...], middle_grad[:first, :].astype(bf16))
    total += dot(mixed_b[...], middle_grad[first:, :].astype(bf16))
    out_grad[...] = total.T.astype(bf16)


def side_call(mixed_a, mixed_b, middle_grad):
    rows, width = middle_grad.shape
    return kernel_call(
        side_body,
        [VM] * 3,
        (S((width, width), bf16),),
        flops=2 * rows * width * width,
        micros=4,
        name="side",
    )(mixed_a, mixed_b, middle_grad)[0]


def back_body(
    own, seg, offs, counts, qkv_in, key_in, mixed_in, stats_a, stats_b, seg_rows, seg_cols,
    w_in, packed_in, normed_in, middle_in, out_grad, vec,
    input_out, keep, send,
    qkv, key_t, mixed_grad, w_t, packed, normed_t, middle_grad, input_grad,
    qkv_grad, key_grad, value_grad, stats, sums, sems, late_sems, out_sems,
):
    rows, width = packed.shape
    me = own[0]
    piece = w_t.shape[1]
    size = 512

    def early(i):
        sl = tile_rows(i, size)
        return [
            pltpu.make_async_copy(qkv_in.at[sl, :], qkv.at[sl, :], sems.at[0, i]),
            pltpu.make_async_copy(key_in.at[:, sl], key_t.at[:, sl], sems.at[1, i]),
            pltpu.make_async_copy(mixed_in.at[sl, :], mixed_grad.at[sl, :], sems.at[2, i]),
        ]

    late = [
        pltpu.make_async_copy(source, target, late_sems.at[k])
        for k, (source, target) in enumerate(
            ((w_in, w_t), (packed_in, packed), (middle_in, middle_grad), (normed_in, normed_t))
        )
    ]
    for i in range(rows // size):
        for copy in early(i):
            copy.start()
    for copy in late:
        copy.start()

    def before(j):
        step = size // BLK

        @pl.when(j == 0)
        def _():
            for copy in early(0):
                copy.wait()

        @pl.when(((j + 2) % step == 0) & ((j + 2) // step < rows // size))
        def _():
            for copy in early((j + 2) // step):
                copy.wait()

    attend_back(
        seg, offs, counts, qkv, key_t, mixed_grad, stats_a, stats_b, seg_rows, seg_cols,
        qkv_grad, key_grad, value_grad, stats, before,
    )
    for copy in late:
        copy.wait()
    weights = w_t[: 3 * HALF // 2].reshape(3 * width, width)
    sums[...] = jnp.zeros_like(sums)

    def result(i):
        sl = tile_rows(i, size)
        return pltpu.make_async_copy(input_grad.at[sl, :], input_out.at[sl, :], out_sems.at[i])

    def one(i, carry):
        sl = tile_rows(i, size)
        qkv_grad[sl, width : 2 * width] = (key_grad[sl, :] * SCALE).astype(bf16)
        qkv_grad[sl, 2 * width :] = value_grad[sl, :].astype(bf16)
        grads = qkv_grad[sl, :]
        normed_grad = dot(grads, weights)
        unit, inverse = norm_parts(packed[sl, :].astype(f32))
        sums[0:8, :] += row_sums(normed_grad * unit)
        sums[8:16, :] += row_sums(normed_grad)
        sums[16:24, :] += row_sums(grads[:, :width].astype(f32))
        sums[24:32, :] += row_sums(grads[:, 2 * width :].astype(f32))
        input_grad[sl, :] = middle_grad[sl, :] + norm_back(unit, inverse, vec[0:1, :], normed_grad)
        result(i).start()
        return carry

    lax.fori_loop(0, rows // size, one, 0)
    for lower in range(0, 3 * width, width):
        pieces = dot(normed_t[...], qkv_grad[:, lower : lower + width]).T.astype(bf16)
        pieces = pieces.reshape(width // piece, piece, width)
        store_pieces(me, lower // piece, pieces, keep, send, 0, piece, plane_first)
    pieces = out_grad[...].reshape(width // piece, piece, width)
    store_pieces(me, 3 * width // piece, pieces, keep, send, 0, piece, plane_first)
    lines = [jnp.sum(sums[8 * row : 8 * row + 8, :], axis=0, keepdims=True) for row in range(4)]
    store_extra(lines, keep, send)
    for i in range(rows // size):
        result(i).wait()


def back_call(
    own, seg, offs, counts, qkv, key_t, mixed_grad, stats_a, stats_b, seg_rows, seg_cols,
    w_t, packed, normed_t, middle_grad, out_grad, vec,
):
    rows, width = packed.shape
    sent = S((HALF * w_t.shape[1] + 2 * EXTRA, width), bf16)
    moved = (qkv, key_t, mixed_grad, w_t, packed, normed_t, middle_grad)
    tiles = rows // 512
    return kernel_call(
        back_body,
        [SM] * 4 + [HB] * 3 + [VM] * 4 + [HB] * 4 + [VM] * 2,
        (S((rows, width), f32), sent, sent),
        [pltpu.VMEM(v.shape, v.dtype) for v in moved]
        + [
            pltpu.VMEM((rows, width), f32),
            pltpu.VMEM((rows, 3 * width), bf16),
            pltpu.VMEM((rows, width), f32),
            pltpu.VMEM((rows, width), f32),
            pltpu.VMEM((rows // BLK, HEADS * BLK), f32),
            pltpu.VMEM((32, width), f32),
            pltpu.SemaphoreType.DMA((3, tiles)),
            pltpu.SemaphoreType.DMA((4,)),
            pltpu.SemaphoreType.DMA((tiles,)),
        ],
        flops=22 * rows * width * width,
        micros=30,
        name="back",
        out_specs=(HB, VM, VM),
    )(
        own, seg, offs, counts, qkv, key_t, mixed_grad, stats_a, stats_b, seg_rows, seg_cols,
        w_t, packed, normed_t, middle_grad, out_grad, vec,
    )


def unpack_body(win, first, count, offs, keep, input_grad, *refs):
    image_grads, slots = refs[-2], refs[-1]
    images_here, length = keep.shape
    rows, width = input_grad.shape
    before = lax.broadcasted_iota(jnp.int32, (length, length), 0)
    after = lax.broadcasted_iota(jnp.int32, (length, length), 1)
    tri = jnp.where(before <= after, 1.0, 0.0).astype(bf16)
    place = lax.broadcasted_iota(jnp.int32, (win, length), 0)

    @pl.when(pl.program_id(0) == 0)
    def _():
        kept = keep[...]
        ranks = dot(kept.astype(f32).astype(bf16), tri).astype(jnp.int32) - 1
        slots[...] = jnp.where(kept > 0, ranks, -4 * win)

    chosen, values = [], []
    for k in range(image_grads.shape[0]):
        i = first + pl.program_id(0) * image_grads.shape[0] + k
        base = pl.multiple_of(jnp.minimum((offs[i] // 8) * 8, rows - win), 8)
        shift = offs[i] - base
        chosen.append(jnp.where(place == slots[pl.ds(i, 1), :] + shift, 1.0, 0.0).astype(bf16))
        values.append(input_grad[pl.ds(base, win), :])
    highs = [value.astype(bf16) for value in values]
    rests = [(value - high.astype(f32)).astype(bf16) for value, high in zip(values, highs)]
    for k in range(image_grads.shape[0]):
        image_grads[k] = dot(chosen[k], highs[k], TN) + dot(chosen[k], rests[k], TN)


def unpack_call(offs, keep, input_grad, first, last, filled=None):
    count = last - first
    images_here, length = keep.shape
    rows, width = input_grad.shape
    win = (length + 7 + 7) // 8 * 8
    size = 5
    out = pl.BlockSpec((size, length, width), lambda i: (first // size + i, 0, 0))
    extra_in = [] if filled is None else [pl.BlockSpec(memory_space=pl.ANY)]
    extra = [] if filled is None else [filled]
    return pl.pallas_call(
        functools.partial(unpack_body, win, first, count),
        grid=(count // size,),
        out_shape=S((images_here, length, width), f32),
        in_specs=[SM, whole(keep.shape), whole(input_grad.shape)] + extra_in,
        out_specs=out,
        scratch_shapes=[pltpu.VMEM((images_here, length), jnp.int32)],
        input_output_aliases={} if filled is None else {3: 0},
        compiler_params=pltpu.CompilerParams(vmem_limit_bytes=58 * 2**20),
        cost_estimate=pl.CostEstimate(flops=0, bytes_accessed=7 * 3_500_000, transcendentals=0),
        name="unpack",
    )(offs, keep, input_grad, *extra)


def to_halves(chunks):
    _, size, width = chunks.shape
    ordered = chunks.reshape(4, 4, 2, size, width).transpose(2, 1, 0, 3, 4).reshape(2, HALF * size, width)
    return ordered[0], ordered[1]


def from_halves(keep, send, parts, width, line_first):
    size = keep.shape[0] // HALF // parts
    both = jnp.stack([keep, send]).reshape(2, 4, 4, parts, size, width)
    both = both.transpose((1, 2, 0, 3, 4, 5) if line_first else (2, 1, 0, 3, 4, 5))
    return both.reshape(CHUNKS, parts, size, width)


def adamw(weight, grad, first, second, average, count, rate, decay):
    first_new = BETA_ONE * first + (1.0 - BETA_ONE) * grad
    second_new = BETA_TWO * second + (1.0 - BETA_TWO) * grad * grad
    first_hat = first_new / (1.0 - jnp.power(BETA_ONE, count))
    second_hat = second_new / (1.0 - jnp.power(BETA_TWO, count))
    weight_new = weight - rate * (first_hat / (jnp.sqrt(second_hat) + ADAM_EPS) + decay * weight)
    average_new = AVERAGE_DECAY * average + (1.0 - AVERAGE_DECAY) * weight_new
    return (weight_new, first_new, second_new, average_new)


def wide_of(ref, rows):
    return ref[rows, :].astype(f32)


def whole_extra(ref):
    return wide_of(ref, slice(-2 * EXTRA, -EXTRA)) + wide_of(ref, slice(-EXTRA, None))


def paired(values):
    while len(values) > 1:
        values = [values[i] + values[i + 1] for i in range(0, len(values), 2)]
    return values[0]


def put_extra(values, out, pieces):
    high, low = split_low(values)
    out[-EXTRA:, :] = high.astype(f32) + low.astype(f32)
    for piece in pieces:
        piece[-2 * EXTRA : -EXTRA, :] = high
        piece[-EXTRA:, :] = low


def merge_first_body(ffn_own, ffn_a, ffn_b, ffn_c, attn_own, attn_in, own, *pieces):
    ffn_size, attn_size = (ffn_own.shape[0] - EXTRA) // 4, (attn_own.shape[0] - 2 * EXTRA) // 4
    for part in range(4):
        rows = slice(part * ffn_size, (part + 1) * ffn_size)
        ffn = ffn_own[rows, :] + wide_of(ffn_a, rows) + wide_of(ffn_b, rows) + wide_of(ffn_c, rows)
        rows = slice(part * attn_size, (part + 1) * attn_size)
        attn = wide_of(attn_own, rows) + wide_of(attn_in, rows)
        out = own if part == 0 else pieces[part - 1]
        out[:ffn_size, :] = ffn.astype(out.dtype)
        out[ffn_size : ffn_size + attn_size, :] = attn.astype(out.dtype)
    known = paired([ffn_own[-EXTRA:, :]] + [whole_extra(r) for r in (ffn_a, ffn_b, ffn_c)])
    fresh = whole_extra(attn_own) + whole_extra(attn_in)
    put_extra(jnp.concatenate([fresh[:4], known[:8], fresh[12:]], axis=0), own, pieces)


def merge_first_call(ffn_own, ffn_in, attn_own, attn_in):
    width = ffn_own.shape[1]
    size = (ffn_own.shape[0] - EXTRA) // 4 + (attn_own.shape[0] - 2 * EXTRA) // 4
    out = kernel_call(
        merge_first_body,
        [VM] * 6,
        (S((size + EXTRA, width), f32),) + (S((size + 2 * EXTRA, width), bf16),) * 3,
        micros=3,
        name="merge_first",
    )(ffn_own, *ffn_in, attn_own, attn_in)
    return out[0], out[1:]


def merge_second_body(skip, own, in_a, in_b, in_c, out, *pieces):
    received = (in_a, in_b, in_c)
    size = out.shape[0] - EXTRA
    for part in range(4):
        rows = slice(skip + part * size, skip + (part + 1) * size)
        total = own[rows, :] + wide_of(in_a, rows) + wide_of(in_b, rows) + wide_of(in_c, rows)
        to = out if part == 0 else pieces[part - 1]
        to[:size, :] = total.astype(to.dtype)
    put_extra(paired([own[-EXTRA:, :]] + [whole_extra(r) for r in received]), out, pieces)


def merge_second_call(skip, own, received):
    width = own.shape[1]
    size = (own.shape[0] - EXTRA - skip) // 4
    out = kernel_call(
        functools.partial(merge_second_body, skip),
        [VM] * 4,
        (S((size + EXTRA, width), f32),) + (S((size + 2 * EXTRA, width), bf16),) * 3,
        micros=2,
        name="merge_second",
    )(own, *received)
    return out[0], out[1:]


def adamw_with(weight, grad, first, second, average, one, two, rate, decay):
    first_new = BETA_ONE * first + (1.0 - BETA_ONE) * grad
    second_new = BETA_TWO * second + (1.0 - BETA_TWO) * grad * grad
    weight_new = weight - rate * ((first_new / one) / (jnp.sqrt(second_new / two) + ADAM_EPS) + decay * weight)
    average_new = AVERAGE_DECAY * average + (1.0 - AVERAGE_DECAY) * weight_new
    return (weight_new, first_new, second_new, average_new)


def update(powers, states, grad, rate, decay, grad_out, outs, at=slice(None)):
    held = [ref[at] for ref in states]
    grad_out[at] = grad
    for ref, value in zip(outs, adamw_with(held[0], grad, *held[1:], powers[0], powers[1], rate, decay)):
        ref[at] = value


def finish_ffn_body(me, powers, own, in_a, in_b, in_c, *refs):
    states, outs = refs[:8], refs[8:]
    _, piece, width = states[0].shape
    received = (in_a, in_b, in_c)
    for k in range(2):
        rows = slice(k * piece, (k + 1) * piece)
        grad = own[rows, :] + wide_of(in_a, rows) + wide_of(in_b, rows) + wide_of(in_c, rows)
        update(powers, states[:4], grad, MATRIX_RATE, WEIGHT_DECAY, outs[0], outs[2:6], k)
    sums = paired([own[-EXTRA:, :]] + [whole_extra(r) for r in received])
    across = width // piece
    row = lax.broadcasted_iota(jnp.int32, (EXTRA, width), 0)
    line = jnp.sum(jnp.where(row == 8 + me[0] // across, sums, 0.0), axis=0, keepdims=True)
    line = jnp.broadcast_to(line, (8, width))
    shift = (me[0] % across) * piece
    line = jnp.where(shift == 0, line, pltpu.roll(line, width - shift, 1))
    update(powers, states[4:], line[:1, :piece], VECTOR_RATE, 0.0, outs[1], outs[6:])


def finish_ffn_call(me, powers, own, received, states):
    kinds = [S(states[k].shape, f32) for k in (0, 4)]
    out = kernel_call(
        finish_ffn_body,
        [SM, SM] + [VM] * 12,
        tuple(kinds) + tuple(kind for kind in kinds for _ in range(4)),
        micros=2,
        name="finish_ffn",
    )(me, powers, own, *received, *states)
    return out[0], out[1], out[2:6], out[6:]


def finish_attn_body(powers, own, in_a, in_b, in_c, *refs):
    states, outs = refs[:8], refs[8:]
    piece = states[0].shape[0]
    rows = slice(0, piece)
    grad = own[rows, :] + wide_of(in_a, rows) + wide_of(in_b, rows) + wide_of(in_c, rows)
    update(powers, states[:4], grad, MATRIX_RATE, WEIGHT_DECAY, outs[0], outs[2:6])
    sums = paired([own[-EXTRA:, :]] + [whole_extra(r) for r in (in_a, in_b, in_c)])
    vec = jnp.concatenate([sums[:4], own[-EXTRA + 4 : -EXTRA + 8, :]], axis=0)
    update(powers, states[4:], vec, VECTOR_RATE, 0.0, outs[1], outs[6:])


def finish_attn_call(powers, own, received, states):
    kinds = [S(states[k].shape, f32) for k in (0, 4)]
    out = kernel_call(
        finish_attn_body,
        [SM] + [VM] * 12,
        tuple(kinds) + tuple(kind for kind in kinds for _ in range(4)),
        micros=2,
        name="finish_attn",
    )(powers, own, *received, *states)
    return out[0], out[1], out[2:6], out[6:]


def body(
    images, keep_mask, kept_counts, pack_offsets, segment_ids, cotangent,
    attn_weight, ffn_weight, up_bias, vectors,
    attn_first, ffn_first, bias_first, vec_first,
    attn_second, ffn_second, bias_second, vec_second,
    attn_average, ffn_average, bias_average, vec_average, step,
):
    width = images.shape[2]
    rows = segment_ids.shape[0]
    both = ("dp", "mp")
    piece = attn_weight.shape[1]
    tree = lax.axis_size("dp") == 8 and lax.axis_size("mp") == 4
    bias_row = jnp.pad(up_bias.astype(bf16)[None, :], ((0, 15), (0, width - piece)))
    seg_rows = segment_ids.reshape(rows // BLK, BLK)
    placed = place_call(images, keep_mask, pack_offsets, rows)
    count = step[0].astype(f32)
    powers = jnp.stack([1.0 - jnp.power(BETA_ONE, count), 1.0 - jnp.power(BETA_TWO, count)])
    if tree:
        own = (lax.axis_index("dp") * 4 + lax.axis_index("mp")).astype(jnp.int32)[None]
        pieces = jnp.concatenate(
            [attn_weight.astype(bf16).T, ffn_weight[0].astype(bf16).T, ffn_weight[1].astype(bf16).T, bias_row], axis=0
        )
        lines = [pieces] + [over_line(pieces, k) for k in (1, 2, 3)]
        placed, *lines = tie(placed, *lines)
        attn_line = jnp.concatenate([line[:piece] for line in lines], axis=0)
        ffn_line = jnp.concatenate([line[piece:] for line in lines], axis=0)
        attn_mine = gather_plane(attn_line)
        normed, normed_t, seg_cols = norm_call(placed, seg_rows, vectors)
        attn_mine, normed, ffn_line = tie(attn_mine, normed, ffn_line)
        attn_other = over_core(attn_mine)
        attn_other, ffn_line = tie(attn_other, ffn_line)
        ffn_lines = [ffn_line] + [over_plane(ffn_line, k) for k in (1, 2, 3)]
    else:
        own = jnp.zeros((1,), jnp.int32)
        attn_all = lax.all_gather(attn_weight.astype(bf16).T, both, axis=0, tiled=True)
        ffn_all = lax.all_gather(jnp.swapaxes(ffn_weight.astype(bf16), 1, 2), both, axis=1, tiled=True)
        bias_all = lax.all_gather(up_bias.astype(bf16), both, axis=0, tiled=True)
        size = 4 * width // CHUNKS
        ffn_all = jnp.concatenate(
            [
                ffn_all[0].reshape(CHUNKS, size, width),
                ffn_all[1].reshape(CHUNKS, size, width),
                jnp.pad(bias_all.reshape(CHUNKS, 1, size), ((0, 0), (0, 15), (0, width - size))),
            ],
            axis=1,
        )
        attn_mine, attn_other = to_halves(attn_all.reshape(CHUNKS, size, width))
        ffn_mine, ffn_other = to_halves(ffn_all)
        normed, normed_t, seg_cols = norm_call(placed, seg_rows, vectors)
    where = (segment_ids, pack_offsets, kept_counts)
    blocks = rows // BLK
    late = blocks // 4
    qkv, key_t, value_t, w_t, mixed_a, stats_a = attend_first_call(
        blocks - late, own, *where, normed, attn_mine, attn_other, vectors, seg_rows, seg_cols
    )
    if tree:
        qkv, mixed_a, *ffn_lines = tie(qkv, mixed_a, *ffn_lines)
        ffn_mine = jnp.concatenate(ffn_lines, axis=0)
        ffn_other = over_core(ffn_mine)
    mixed_b, stats_b = attend_last_call(late, *where, qkv, value_t, seg_rows, seg_cols)
    if tree:
        mixed_b, ffn_mine, ffn_other = tie(mixed_b, ffn_mine, ffn_other)
    layer_out, middle_grad, mixed_grad, ffn_keep, ffn_send = feed_call(
        own, placed, mixed_a, mixed_b, cotangent, vectors, w_t, ffn_mine, ffn_other
    )
    if tree:
        ffn_in = over_core(ffn_send)
    out_grad = side_call(mixed_a, mixed_b, middle_grad)
    if tree:
        out_grad, ffn_in = tie(out_grad, ffn_in)
        ffn_own, *ffn_out = combine_call(ffn_keep, [ffn_in], 4, EXTRA)
        out_grad, ffn_own, *ffn_out = tie(out_grad, ffn_own, *ffn_out)
        ffn_in = [over_line(p, k + 1) for k, p in enumerate(ffn_out)]
    input_grad, attn_keep, attn_send = back_call(
        own, *where, qkv, key_t, mixed_grad, stats_a, stats_b, seg_rows, seg_cols,
        w_t, placed, normed_t, middle_grad, out_grad, vectors,
    )
    index = lax.axis_index("dp") * lax.axis_size("mp") + lax.axis_index("mp")
    if tree:
        input_grad, attn_send, *ffn_in = tie(input_grad, attn_send, *ffn_in)
        attn_in = over_core(attn_send)
        states = [v.T for v in (attn_weight, attn_first, attn_second, attn_average)]
        states += [vectors, vec_first, vec_second, vec_average]
        ffn_states = [jnp.swapaxes(v, 1, 2) for v in (ffn_weight, ffn_first, ffn_second, ffn_average)]
        ffn_states += [v[None, :] for v in (up_bias, bias_first, bias_second, bias_average)]
        cut = images.shape[0] * 3 // 5
        unpack = functools.partial(unpack_call, pack_offsets, keep_mask)
        merged, pieces = merge_first_call(ffn_own, ffn_in, attn_keep, attn_in)
        input_grad, *pieces = tie(input_grad, *pieces)
        received = [over_plane(p, k + 1) for k, p in enumerate(pieces)]
        image_grads = unpack(input_grad, 0, cut)
        image_grads, *received = tie(image_grads, *received)
        attn_own, pieces = merge_second_call(2 * piece, merged, received)
        image_grads, merged, *pieces = tie(image_grads, merged, *pieces)
        last = [over_line(p, k + 1) for k, p in enumerate(pieces)]
        image_grads = unpack(input_grad, cut, images.shape[0], image_grads)
        ffn_grad, bias_grad, ffn_up, bias_up = finish_ffn_call(own, powers, merged, received, ffn_states)
        image_grads, ffn_grad, *last = tie(image_grads, ffn_grad, *last)
        attn_grad, vec_grad, attn_up, vec_up = finish_attn_call(powers, attn_own, last, states)
        attn_grad, ffn_grad, bias_grad = attn_grad.T, jnp.swapaxes(ffn_grad, 1, 2), bias_grad[0]
        attn_up, ffn_up = [v.T for v in attn_up], [jnp.swapaxes(v, 1, 2) for v in ffn_up]
        bias_up = [v[0] for v in bias_up]
    else:
        image_grads = unpack_call(pack_offsets, keep_mask, input_grad, 0, images.shape[0])
        base = ffn_keep.shape[0] - 2 * EXTRA
        ffn_t = from_halves(ffn_keep[:base], ffn_send[:base], 2, width, True)
        ffn_t = jnp.swapaxes(ffn_t, 0, 1).reshape(2, 4 * width, width)
        ffn_t = lax.psum_scatter(ffn_t.astype(f32), both, scatter_dimension=1, tiled=True)
        ffn_grad = jnp.swapaxes(ffn_t, 1, 2)
        known = ffn_keep[base : base + EXTRA].astype(f32) + ffn_keep[base + EXTRA :].astype(f32)
        base = attn_keep.shape[0] - 2 * EXTRA
        attn_t = from_halves(attn_keep[:base], attn_send[:base], 1, width, False).reshape(4 * width, width)
        attn_grad = lax.psum_scatter(attn_t.astype(f32), both, scatter_dimension=0, tiled=True).T
        sums = attn_keep[base : base + EXTRA].astype(f32) + attn_keep[base + EXTRA :].astype(f32)
        sums = lax.psum(jnp.concatenate([sums[:4], known[:8]], axis=0), both)
        vec_grad, bias_sums = sums[:8], sums[8:]
        bias_grad = lax.dynamic_slice_in_dim(bias_sums.reshape(4 * width), index * piece, piece, 0)
        attn_up = adamw(attn_weight, attn_grad, attn_first, attn_second, attn_average, count, MATRIX_RATE, WEIGHT_DECAY)
        vec_up = adamw(vectors, vec_grad, vec_first, vec_second, vec_average, count, VECTOR_RATE, 0.0)
        ffn_up = adamw(ffn_weight, ffn_grad, ffn_first, ffn_second, ffn_average, count, MATRIX_RATE, WEIGHT_DECAY)
        bias_up = adamw(up_bias, bias_grad, bias_first, bias_second, bias_average, count, VECTOR_RATE, 0.0)
    news = [part[k] for k in range(4) for part in (attn_up, ffn_up, bias_up, vec_up)]
    return (layer_out, image_grads, attn_grad, ffn_grad, bias_grad, vec_grad, *news)


def solution(mesh):
    both = ("dp", "mp")
    matrix, slab, line = P(None, both), P(None, None, both), P(both)
    states = (matrix, slab, line, P())
    return jax.shard_map(
        body,
        mesh=mesh,
        in_specs=(P(both, None, None), P(both, None), line, line, line, P(both, None), *states * 4, P()),
        out_specs=(P(both, None), P(both, None, None), *states, *states * 4),
        check_vma=False,
    )
```

```python
import functools
import math

import jax
import jax.numpy as jnp
from jax import lax
from jax.experimental import pallas as pl
from jax.experimental.pallas import tpu as pltpu
from jax.sharding import PartitionSpec as P

HEADS = 6
HEAD = 64
PAIR = 2 * HEAD
PAIRS = HEADS // 2
BLK = 128
REACH = 5
CHUNKS = 32
HALF = CHUNKS // 2
EXTRA = 16
EXCLUDED = -8.0e9
INCLUDED = 3.0e38

NORM_EPS = 1e-06
BETA_ONE = 0.9
BETA_TWO = 0.999
ADAM_EPS = 1e-08
MATRIX_RATE = 0.05
VECTOR_RATE = 0.2
WEIGHT_DECAY = 0.05
AVERAGE_DECAY = 0.8

LOG2E = 1.4426950408889634
SCORE_LOG2 = LOG2E / math.sqrt(HEAD)
SCALE = 1.0 / math.sqrt(HEAD)

f32 = jnp.float32
bf16 = jnp.bfloat16
NN = (((1,), (0,)), ((), ()))
NT = (((1,), (1,)), ((), ()))
TN = (((0,), (0,)), ((), ()))
VM = pl.BlockSpec(memory_space=pltpu.VMEM)
SM = pl.BlockSpec(memory_space=pltpu.SMEM)
HB = pl.BlockSpec(memory_space=pl.ANY)
S = jax.ShapeDtypeStruct


def dot(left, right, dims=NN):
    return lax.dot_general(left, right, dims, preferred_element_type=f32)


def kernel_call(body, ins, outs, scratch=(), flops=0, micros=1, name=None, grid=(), out_specs=None, mib=16):
    return pl.pallas_call(
        body,
        grid=grid,
        out_shape=outs,
        in_specs=ins,
        out_specs=out_specs or tuple(VM for _ in outs),
        scratch_shapes=list(scratch),
        compiler_params=pltpu.CompilerParams(vmem_limit_bytes=mib * 2**20),
        cost_estimate=pl.CostEstimate(flops=flops, bytes_accessed=micros * 3_500_000, transcendentals=0),
        name=name,
    )


def whole(shape):
    return pl.BlockSpec(shape, lambda i: (0,) * len(shape))


def row_sums(values):
    rows, width = values.shape
    return jnp.sum(values.reshape(rows // 8, 8, width), axis=0)


def norm_parts(values):
    scale = 1.0 / values.shape[-1]
    centre = jnp.sum(values, axis=-1, keepdims=True) * scale
    centred = values - centre
    spread = jnp.sum(centred * centred, axis=-1, keepdims=True) * scale
    inverse = lax.rsqrt(spread + NORM_EPS)
    return centred * inverse, inverse


def norm_back(unit, inverse, gain, grad):
    scale = 1.0 / unit.shape[-1]
    scaled = grad * gain
    mean = jnp.sum(scaled, axis=-1, keepdims=True) * scale
    along = jnp.sum(scaled * unit, axis=-1, keepdims=True) * scale
    return inverse * (scaled - mean - unit * along)


def tile_rows(count, size):
    return pl.ds(pl.multiple_of(count * size, size), size)


def plane_first(apart):
    return (apart & 3) * 4 + lax.shift_right_logical(apart, 2)


def line_first(apart):
    return apart


def spread_pieces(own, halves, out):
    for near in range(2):
        for slot in range(HALF):
            apart = near + 2 * ((slot // 4) + 4 * (slot % 4))
            out[own ^ apart] = halves[near][slot * out.shape[1] : (slot + 1) * out.shape[1], :]


def store_pieces(own, start, pieces, keep, send, at, step, order):
    count, size, _ = pieces.shape
    odd = (own & 1) == 1
    for e in range(0, count, 2):
        apart = lax.shift_right_logical(own, 1) ^ ((start + e) // 2)
        row = pl.multiple_of(order(apart) * step + at, 16)
        even_piece, odd_piece = pieces[e], pieces[e + 1]
        keep[pl.ds(row, size), :] = jnp.where(odd, odd_piece, even_piece)
        send[pl.ds(row, size), :] = jnp.where(odd, even_piece, odd_piece)


def split_low(values):
    high = values.astype(bf16)
    return high, (values - high.astype(f32)).astype(bf16)


def combine_body(parts, size, extra, count, *refs):
    own, received, outs = refs[0], refs[1 : 1 + count], refs[1 + count :]
    base = parts * size
    for part in range(parts):
        rows = slice(part * size, (part + 1) * size)
        total = own[rows, :].astype(f32)
        for other in received:
            total = total + other[rows, :].astype(f32)
        if part == 0:
            outs[0][:size, :] = total
        else:
            outs[part][:size, :] = total.astype(bf16)
    if extra:
        if own.dtype == bf16:
            sums = [own[base : base + extra, :].astype(f32) + own[base + extra :, :].astype(f32)]
        else:
            sums = [own[base:, :]]
        sums += [r[base : base + extra, :].astype(f32) + r[base + extra :, :].astype(f32) for r in received]
        while len(sums) > 1:
            sums = [sums[i] + sums[i + 1] for i in range(0, len(sums), 2)]
        high, low = split_low(sums[0])
        outs[0][size:, :] = high.astype(f32) + low.astype(f32) if parts > 1 else sums[0]
        for out in outs[1:]:
            out[size : size + extra, :] = high
            out[size + extra :, :] = low


def combine_call(own, received, parts, extra):
    size = (received[0].shape[0] - 2 * extra) // parts
    width = own.shape[1]
    outs = (S((size + extra, width), f32),) + (S((size + 2 * extra, width), bf16),) * (parts - 1)
    return kernel_call(
        functools.partial(combine_body, parts, size, extra, len(received)),
        [VM] * (1 + len(received)),
        outs,
        flops=own.size * len(received),
        micros=2,
        name="combine",
    )(own, *received)


def over_core(values):
    return lax.ppermute(values, "mp", [(i, i ^ 1) for i in range(lax.axis_size("mp"))])


def over_plane(values, apart):
    devices = lax.axis_size("dp") * lax.axis_size("mp")
    return lax.ppermute(values, ("dp", "mp"), [(i, i ^ (2 * apart)) for i in range(devices)])


def over_line(values, apart):
    return lax.ppermute(values, "dp", [(i, i ^ (2 * apart)) for i in range(lax.axis_size("dp"))])


def tie(*values):
    return lax.optimization_barrier(values)


def gather_plane(pieces):
    return jnp.concatenate([pieces] + [over_plane(pieces, k) for k in (1, 2, 3)], axis=0)


def place_body(win, offs, images, keep, packed, acc, slots):
    images_here, length = keep.shape
    rows, width = packed.shape
    size = images.shape[0]
    step = pl.program_id(0)

    @pl.when(step == 0)
    def _():
        before = lax.broadcasted_iota(jnp.int32, (length, length), 0)
        after = lax.broadcasted_iota(jnp.int32, (length, length), 1)
        tri = jnp.where(before <= after, 1.0, 0.0).astype(bf16)
        kept = keep[...]
        ranks = dot(kept.astype(f32).astype(bf16), tri).astype(jnp.int32) - 1
        slots[...] = jnp.where(kept > 0, ranks, -4 * win)
        acc[0:8, :] = jnp.zeros((8, width), f32)

    place = lax.broadcasted_iota(jnp.int32, (win, length), 0)
    starts = [offs[step * size + k] for k in range(size)]
    bases = [pl.multiple_of((start // 8) * 8, 8) for start in starts]
    lines = [slots[pl.ds(step * size + k, 1), :] + (starts[k] - bases[k]) for k in range(size)]
    chosen = [jnp.where(place == line, 1.0, 0.0).astype(bf16) for line in lines]
    moved = [dot(chosen[k], images[k]) for k in range(size)]
    for base, part in zip(bases, moved):
        acc[pl.ds(base, 8), :] += part[0:8]
        acc[pl.ds(base + 8, win - 8), :] = part[8:]

    @pl.when(step == pl.num_programs(0) - 1)
    def _():
        packed[...] = acc[:rows, :].astype(bf16)


def place_call(images, keep, offs, rows):
    images_here, length, width = images.shape
    win = (length + 7 + 7) // 8 * 8
    size = 5
    return kernel_call(
        functools.partial(place_body, win),
        [SM, pl.BlockSpec((size, length, width), lambda i: (i, 0, 0)), whole(keep.shape)],
        (S((rows, width), bf16),),
        [pltpu.VMEM((rows + win, width), f32), pltpu.VMEM((images_here, length), jnp.int32)],
        flops=2 * images_here * win * length * width,
        micros=6,
        name="place",
        mib=60,
        grid=(images_here // size,),
        out_specs=(whole((rows, width)),),
    )(offs, images, keep)[0]


def norm_body(packed, seg_rows, vec, normed, normed_t, seg_cols):
    rows, width = packed.shape
    step = pl.program_id(0)
    sub = 128
    parts = [slice(k * sub, (k + 1) * sub) for k in range(rows // sub)]
    units = [norm_parts(packed[at, :].astype(f32))[0] for at in parts]
    lows = [(unit * vec[0:1, :] + vec[1:2, :]).astype(bf16) for unit in units]
    for at, low in zip(parts, lows):
        normed[at, :] = low
    for at, low in zip(parts, lows):
        normed_t[:, at] = low.T
    for k in range(rows // BLK):
        line = seg_rows[pl.ds(step * (rows // BLK) + k, 1), :]
        seg_cols[k * BLK : (k + 1) * BLK, :] = jnp.broadcast_to(line, (BLK, BLK)).T


def norm_call(packed, seg_rows, vec):
    rows, width = packed.shape
    size = 512
    return kernel_call(
        norm_body,
        [pl.BlockSpec((size, width), lambda i: (i, 0)), whole(seg_rows.shape), whole(vec.shape)],
        (S((rows, width), bf16), S((width, rows), bf16), S((rows, BLK), jnp.int32)),
        flops=rows * width * 12,
        micros=5,
        name="norm",
        mib=60,
        grid=(rows // size,),
        out_specs=(
            pl.BlockSpec((size, width), lambda i: (i, 0)),
            pl.BlockSpec((width, size), lambda i: (0, i)),
            pl.BlockSpec((size, BLK), lambda i: (i, 0)),
        ),
    )(packed, seg_rows, vec)


def window(seg, offs, counts, j, images_here, tiles):
    first = seg[j * BLK]
    last = seg[j * BLK + BLK - 1]
    used = last < images_here
    last_here = jnp.where(used, last, 0)
    end = jnp.where(used, offs[last_here] + counts[last_here], tiles * BLK)
    low = offs[first] // BLK
    size = jnp.maximum((end + BLK - 1) // BLK - low, 2)
    return jnp.minimum(low, tiles - size), size


def masked_pair(pair):
    lane = lax.broadcasted_iota(jnp.int32, pair.shape, 1)
    none = jnp.zeros_like(pair)
    return jnp.concatenate([jnp.where(lane < HEAD, pair, none), jnp.where(lane >= HEAD, pair, none)], axis=0)


def limits(seg_rows, seg_cols, j, keys):
    same = seg_cols[keys, :] == seg_rows[pl.ds(j, 1), :]
    lim = jnp.where(same, INCLUDED, EXCLUDED)
    return jnp.concatenate([lim, lim], axis=1)


def over_windows(seg, offs, counts, tiles, base, first, blocks, block, before=None):
    def one(j, carry):
        if before is not None:
            before(j)
        low, size = window(seg, offs, counts, j, offs.shape[0], tiles)
        for n in range(2, REACH + 1):

            @pl.when(size == n)
            def _():
                block(j, pl.ds(pl.multiple_of((low - base) * BLK, BLK), n * BLK))

        return carry

    lax.fori_loop(first, first + blocks, one, 0)


def attend_blocks(base, first, blocks, seg, offs, counts, qkv, value_t, seg_rows, seg_cols, mixed_t, stats):
    width = value_t.shape[0]
    tiles = seg.shape[0] // BLK

    def block(j, keys):
        here = tile_rows(j - base, BLK)
        there = tile_rows(j - first, BLK)
        lim = limits(seg_rows, seg_cols, j, keys)
        ats = [slice(p * PAIR, (p + 1) * PAIR) for p in range(PAIRS)]
        raws = [
            dot(qkv[keys, width + p * PAIR : width + (p + 1) * PAIR], masked_pair(qkv[here, ats[p]]), NT)
            for p in range(PAIRS)
        ]
        raws = [jnp.minimum(raw, lim) for raw in raws]
        tops = [jnp.max(raw, axis=0, keepdims=True) for raw in raws]
        expos = [jnp.exp2((raw - top) * SCORE_LOG2) for raw, top in zip(raws, tops)]
        totals = [jnp.sum(expo, axis=0, keepdims=True) for expo in expos]
        lows = [(expo * (1.0 / total)).astype(bf16) for expo, total in zip(expos, totals)]
        outs = [dot(value_t[at, keys], low) for at, low in zip(ats, lows)]
        for p in range(PAIRS):
            out = outs[p]
            mixed_t[p * PAIR : p * PAIR + HEAD, there] = out[:HEAD, :BLK].astype(bf16)
            mixed_t[p * PAIR + HEAD : (p + 1) * PAIR, there] = out[HEAD:, BLK:].astype(bf16)
            level = tops[p] * SCORE_LOG2 + jnp.log2(totals[p])
            stats[pl.ds(j - first, 1), p * 2 * BLK : (p + 1) * 2 * BLK] = level

    over_windows(seg, offs, counts, tiles, base, first, blocks, block)


def attend_first_body(
    own, seg, offs, counts, normed, mine, other, vec, seg_rows, seg_cols,
    qkv_out, key_out, value_out, w_out, mixed_t, stats,
    qkv, key_t, value_t, w_t, sems,
):
    rows, width = normed.shape
    size = 512
    spread_pieces(own[0], (mine, other), w_t)
    units = w_t.shape[0] * w_t.shape[1]
    weights = w_t[...].reshape(units, width)[: 3 * width]
    bias = jnp.concatenate([vec[2:3, :], jnp.zeros((1, width), f32), vec[3:4, :]], axis=1)
    last = pltpu.make_async_copy(w_t, w_out, sems.at[3, 0])
    last.start()

    def copies(i):
        sl = tile_rows(i, size)
        return [
            pltpu.make_async_copy(qkv.at[sl, :], qkv_out.at[sl, :], sems.at[0, i]),
            pltpu.make_async_copy(key_t.at[:, sl], key_out.at[:, sl], sems.at[1, i]),
            pltpu.make_async_copy(value_t.at[:, sl], value_out.at[:, sl], sems.at[2, i]),
        ]

    def project(i, carry):
        sl = tile_rows(i, size)
        low = (dot(normed[sl, :], weights, NT) + bias).astype(bf16)
        qkv[sl, :] = low
        key_t[:, sl] = low[:, width : 2 * width].T
        value_t[:, sl] = low[:, 2 * width :].T
        for copy in copies(i):
            copy.start()
        return carry

    lax.fori_loop(0, rows // size, project, 0)
    attend_blocks(
        0, 0, mixed_t.shape[1] // BLK, seg, offs, counts, qkv, value_t, seg_rows, seg_cols, mixed_t, stats
    )
    for i in range(rows // size):
        for copy in copies(i):
            copy.wait()
    last.wait()


def attend_first_call(blocks, own, seg, offs, counts, normed, mine, other, vec, seg_rows, seg_cols):
    rows, width = normed.shape
    piece = mine.shape[0] // HALF
    kept = ((rows, 3 * width), (width, rows), (width, rows), (CHUNKS, piece, width))
    return kernel_call(
        attend_first_body,
        [SM, SM, SM, SM, VM, VM, VM, VM, VM, VM],
        tuple(S(shape, bf16) for shape in kept)
        + (S((width, blocks * BLK), bf16), S((blocks, HEADS * BLK), f32)),
        [pltpu.VMEM(shape, bf16) for shape in kept] + [pltpu.SemaphoreType.DMA((4, rows // 512))],
        flops=2 * rows * width * 3 * width,
        micros=20,
        name="attend_first",
        mib=60,
        out_specs=(HB, HB, HB, HB, VM, VM),
    )(own, seg, offs, counts, normed, mine, other, vec, seg_rows, seg_cols)


def attend_last_call(blocks, seg, offs, counts, qkv, value_t, seg_rows, seg_cols):
    width, rows = value_t.shape
    part = (blocks + REACH - 1) * BLK
    while rows % part:
        part += BLK
    at = rows // part - 1
    tiles = rows // BLK
    return kernel_call(
        functools.partial(attend_blocks, tiles - part // BLK, tiles - blocks, blocks),
        [
            SM,
            SM,
            SM,
            pl.BlockSpec((part, 3 * width), lambda i: (at, 0)),
            pl.BlockSpec((width, part), lambda i: (0, at)),
            whole(seg_rows.shape),
            pl.BlockSpec((part, BLK), lambda i: (at, 0)),
        ],
        (S((width, blocks * BLK), bf16), S((blocks, HEADS * BLK), f32)),
        grid=(1,),
        out_specs=(whole((width, blocks * BLK)), whole((blocks, HEADS * BLK))),
        flops=4 * blocks * BLK * 512 * width,
        micros=5,
        name="attend_last",
        mib=60,
    )(seg, offs, counts, qkv, value_t, seg_rows, seg_cols)


def attend_back(
    seg, offs, counts, qkv, key_t, mixed_grad, stats_a, stats_b, seg_rows, seg_cols, qkv_grad, key_grad, value_grad, stats, before
):
    rows, width = mixed_grad.shape
    key_grad[...] = jnp.zeros_like(key_grad)
    value_grad[...] = jnp.zeros_like(value_grad)
    stats[: stats_a.shape[0], :] = stats_a[...]
    stats[stats_a.shape[0] :, :] = stats_b[...]

    def block(j, keys):
        here = tile_rows(j, BLK)
        lim = limits(seg_rows, seg_cols, j, keys)
        ats = [slice(p * PAIR, (p + 1) * PAIR) for p in range(PAIRS)]
        levels = stats[pl.ds(j, 1), :]
        levels = [levels[:, p * 2 * BLK : (p + 1) * 2 * BLK] for p in range(PAIRS)]
        queries = [masked_pair(qkv[here, at]) for at in ats]
        outs = [masked_pair(mixed_grad[here, at]) for at in ats]
        raws = [
            dot(qkv[keys, width + p * PAIR : width + (p + 1) * PAIR], queries[p], NT) for p in range(PAIRS)
        ]
        grads = [
            dot(qkv[keys, 2 * width + p * PAIR : 2 * width + (p + 1) * PAIR], outs[p], NT) for p in range(PAIRS)
        ]
        probs = [jnp.exp2(jnp.minimum(raw, lim) * SCORE_LOG2 - level) for raw, level in zip(raws, levels)]
        inners = [jnp.sum(prob * grad, axis=0, keepdims=True) for prob, grad in zip(probs, grads)]
        lows = [prob.astype(bf16) for prob in probs]
        score_grads = [
            (prob * (grad - inner)).astype(bf16) for prob, grad, inner in zip(probs, grads, inners)
        ]
        for p in range(PAIRS):
            value_grad[keys, ats[p]] += dot(lows[p], outs[p])
        for p in range(PAIRS):
            key_grad[keys, ats[p]] += dot(score_grads[p], queries[p])
        for p in range(PAIRS):
            query_t = dot(key_t[ats[p], keys], score_grads[p]) * SCALE
            joined = jnp.concatenate([query_t[:HEAD, :BLK], query_t[HEAD:, BLK:]], axis=0)
            qkv_grad[here, ats[p]] = joined.T.astype(bf16)

    over_windows(seg, offs, counts, rows // BLK, 0, 0, rows // BLK, block, before)


def bias_line(rows_of, units):
    chunks, size = rows_of.shape
    column = lax.broadcasted_iota(jnp.int32, (size, units), 1)
    within = lax.broadcasted_iota(jnp.int32, (size, units), 0)
    repeat = jnp.where(column % size == within, 1.0, 0.0).astype(bf16)
    wide = dot(rows_of, repeat)
    owner = lax.broadcasted_iota(jnp.int32, (chunks, units), 1) // size
    mine = owner == lax.broadcasted_iota(jnp.int32, (chunks, units), 0)
    return jnp.sum(jnp.where(mine, wide, 0.0), axis=0, keepdims=True)


def feed_body(
    sub, own, packed, mixed_a, mixed_b, cot, vec, w_t, mine, other,
    layer_out, middle_grad, mixed_grad, keep, send,
    all_s, up_s, down_s, hid_s, gi_s, n2t_s, glt_s, bias_s, sums, bias_sum, mixed,
):
    size, width = packed.shape
    step, steps = pl.program_id(0), pl.num_programs(0)
    me = own[0]
    units = up_s.shape[0]
    piece = units // CHUNKS

    @pl.when(step == 0)
    def _():
        spread_pieces(me, (mine, other), all_s)
        up_s[...] = all_s[:, :piece, :].reshape(units, width)
        down_s[...] = all_s[:, piece : 2 * piece, :].reshape(units, width)
        bias_s[...] = bias_line(all_s[:, 2 * piece, :piece], units)
        bias_sum[...] = jnp.zeros_like(bias_sum)
        sums[...] = jnp.zeros_like(sums)

    @pl.when(step < steps - 1)
    def _():
        mixed[...] = mixed_a[...]

    @pl.when(step == steps - 1)
    def _():
        mixed[...] = mixed_b[...]

    w_out_t = w_t[...].reshape(width, width)
    parts = [slice(k * sub, (k + 1) * sub) for k in range(size // sub)]
    rows = [pl.ds(pl.multiple_of(step * size + k * sub, sub), sub) for k in range(size // sub)]
    mids = [packed[at, :].astype(f32) + dot(mixed[:, at].T, w_out_t, NT) + vec[4:5, :] for at in parts]
    valids = [
        lax.broadcasted_iota(jnp.int32, (sub, 1), 0) + step * size + k * sub < steps * size - 1
        for k in range(size // sub)
    ]
    outs = [jnp.where(valid, cot[at, :].astype(f32), 0.0) for valid, at in zip(valids, parts)]
    out_lows = [out.astype(bf16) for out in outs]
    grads = [dot(out_low, down_s[...], NT) for out_low in out_lows]
    units_of = [norm_parts(middle) for middle in mids]
    lows = [(unit * vec[5:6, :] + vec[6:7, :]).astype(bf16) for unit, _ in units_of]
    us = [dot(low, up_s[...], NT) + bias_s[...] for low in lows]
    downs, backs = [], []
    for k in range(size // sub):
        n2t_s[:, rows[k]] = lows[k].T
        glt_s[:, rows[k]] = out_lows[k].T
        u = us[k]
        phi = 0.5 + 0.5 * lax.erf(u * (1.0 / math.sqrt(2.0)))
        hidden = (u * phi).astype(bf16)
        hid_s[rows[k], :] = hidden
        slope = phi + u * jnp.exp2(u * u * (-0.5 * LOG2E)) * (1.0 / math.sqrt(2.0 * math.pi))
        grad_in = grads[k] * slope
        bias_sum[...] += row_sums(grad_in)
        grad_in_low = grad_in.astype(bf16)
        gi_s[rows[k], :] = grad_in_low
        downs.append(dot(hidden, down_s[...]))
        backs.append(dot(grad_in_low, up_s[...]))
    totals = []
    for k, at in enumerate(parts):
        unit, inverse = units_of[k]
        layer_out[at, :] = jnp.where(valids[k], mids[k] + downs[k] + vec[7:8, :], 0.0).astype(bf16)
        n2_grad = backs[k]
        sums[8:16, :] += row_sums(n2_grad * unit)
        sums[16:24, :] += row_sums(n2_grad)
        total = outs[k] + norm_back(unit, inverse, vec[5:6, :], n2_grad)
        middle_grad[at, :] = total
        sums[0:8, :] += row_sums(total)
        sums[24:32, :] += row_sums(outs[k])
        totals.append(total.astype(bf16))
    for k, at in enumerate(parts):
        mixed_grad[at, :] = dot(totals[k], w_out_t).astype(bf16)

    @pl.when(step == steps - 1)
    def _():
        wide = 2 * width
        for lower in range(0, units, wide):
            hs = slice(lower, lower + wide)
            for index, (left, right) in enumerate(((n2t_s, gi_s), (glt_s, hid_s))):
                pieces = dot(left[...], right[:, hs]).T.astype(bf16).reshape(wide // piece, piece, width)
                store_pieces(me, lower // piece, pieces, keep, send, index * piece, 2 * piece, line_first)
        line = jnp.sum(bias_sum[...], axis=0, keepdims=True)
        lines = [jnp.sum(sums[8 * row : 8 * row + 8, :], axis=0, keepdims=True) for row in range(4)]
        lines += [line[:, row * width : (row + 1) * width] for row in range(units // width)]
        store_extra(lines, keep, send)


def store_extra(lines, keep, send):
    width = keep.shape[1]
    lines = jnp.concatenate(lines + [jnp.zeros((EXTRA - len(lines), width), f32)], axis=0)
    high, low = split_low(lines)
    base = keep.shape[0] - 2 * EXTRA
    for out in (keep, send):
        out[base : base + EXTRA, :] = high
        out[base + EXTRA :, :] = low


def feed_call(own, packed, mixed_a, mixed_b, cot, vec, w_t, mine, other):
    rows, width = packed.shape
    units = 4 * width
    size = mixed_b.shape[1]
    steps = rows // size
    row_block = pl.BlockSpec((size, width), lambda i: (i, 0))
    sent = (units + 2 * EXTRA, width)
    return kernel_call(
        functools.partial(feed_body, size),
        [
            SM,
            row_block,
            pl.BlockSpec((width, size), lambda i: (0, jnp.minimum(i, steps - 2))),
            whole(mixed_b.shape),
            row_block,
            whole((8, width)),
            pl.BlockSpec((CHUNKS // 4, units // CHUNKS, width), lambda i: (3, 0, 0)),
            whole(mine.shape),
            whole(other.shape),
        ],
        (S((rows, width), bf16), S((rows, width), f32), S((rows, width), bf16), S(sent, bf16), S(sent, bf16)),
        [
            pltpu.VMEM((CHUNKS, mine.shape[0] // HALF, width), bf16),
            pltpu.VMEM((units, width), bf16),
            pltpu.VMEM((units, width), bf16),
            pltpu.VMEM((rows, units), bf16),
            pltpu.VMEM((rows, units), bf16),
            pltpu.VMEM((width, rows), bf16),
            pltpu.VMEM((width, rows), bf16),
            pltpu.VMEM((1, units), f32),
            pltpu.VMEM((32, width), f32),
            pltpu.VMEM((8, units), f32),
            pltpu.VMEM((width, size), bf16),
        ],
        grid=(steps,),
        out_specs=(row_block, row_block, row_block, whole(sent), whole(sent)),
        flops=12 * rows * width * units + 6 * rows * width * width,
        micros=30,
        name="feed",
        mib=60,
    )(own, packed, mixed_a, mixed_b, cot, vec, w_t, mine, other)


def side_body(mixed_a, mixed_b, middle_grad, out_grad):
    first = mixed_a.shape[1]
    total = dot(mixed_a[...], middle_grad[:first, :].astype(bf16))
    total += dot(mixed_b[...], middle_grad[first:, :].astype(bf16))
    out_grad[...] = total.T.astype(bf16)


def side_call(mixed_a, mixed_b, middle_grad):
    rows, width = middle_grad.shape
    return kernel_call(
        side_body,
        [VM] * 3,
        (S((width, width), bf16),),
        flops=2 * rows * width * width,
        micros=4,
        name="side",
        mib=20,
    )(mixed_a, mixed_b, middle_grad)[0]


def back_body(
    own, seg, offs, counts, qkv_in, key_in, mixed_in, stats_a, stats_b, seg_rows, seg_cols,
    w_in, packed_in, normed_in, middle_in, out_grad, vec,
    input_out, keep, send,
    qkv, key_t, mixed_grad, w_t, packed, normed_t, middle_grad, input_grad,
    qkv_grad, key_grad, value_grad, stats, sums, sems, late_sems, out_sems,
):
    rows, width = packed.shape
    me = own[0]
    piece = w_t.shape[1]
    size = 512

    def early(i):
        sl = tile_rows(i, size)
        return [
            pltpu.make_async_copy(qkv_in.at[sl, :], qkv.at[sl, :], sems.at[0, i]),
            pltpu.make_async_copy(key_in.at[:, sl], key_t.at[:, sl], sems.at[1, i]),
            pltpu.make_async_copy(mixed_in.at[sl, :], mixed_grad.at[sl, :], sems.at[2, i]),
        ]

    late = [
        pltpu.make_async_copy(source, target, late_sems.at[k])
        for k, (source, target) in enumerate(
            ((w_in, w_t), (packed_in, packed), (middle_in, middle_grad), (normed_in, normed_t))
        )
    ]
    for i in range(rows // size):
        for copy in early(i):
            copy.start()
    for copy in late:
        copy.start()

    def before(j):
        step = size // BLK

        @pl.when(j == 0)
        def _():
            for copy in early(0):
                copy.wait()

        @pl.when(((j + 2) % step == 0) & ((j + 2) // step < rows // size))
        def _():
            for copy in early((j + 2) // step):
                copy.wait()

    attend_back(
        seg, offs, counts, qkv, key_t, mixed_grad, stats_a, stats_b, seg_rows, seg_cols,
        qkv_grad, key_grad, value_grad, stats, before,
    )
    for copy in late:
        copy.wait()
    weights = w_t[: 3 * HALF // 2].reshape(3 * width, width)
    sums[...] = jnp.zeros_like(sums)

    def result(i):
        sl = tile_rows(i, size)
        return pltpu.make_async_copy(input_grad.at[sl, :], input_out.at[sl, :], out_sems.at[i])

    def one(i, carry):
        sl = tile_rows(i, size)
        qkv_grad[sl, width : 2 * width] = (key_grad[sl, :] * SCALE).astype(bf16)
        qkv_grad[sl, 2 * width :] = value_grad[sl, :].astype(bf16)
        grads = qkv_grad[sl, :]
        normed_grad = dot(grads, weights)
        unit, inverse = norm_parts(packed[sl, :].astype(f32))
        sums[0:8, :] += row_sums(normed_grad * unit)
        sums[8:16, :] += row_sums(normed_grad)
        sums[16:24, :] += row_sums(grads[:, :width].astype(f32))
        sums[24:32, :] += row_sums(grads[:, 2 * width :].astype(f32))
        input_grad[sl, :] = middle_grad[sl, :] + norm_back(unit, inverse, vec[0:1, :], normed_grad)
        result(i).start()
        return carry

    lax.fori_loop(0, rows // size, one, 0)
    for lower in range(0, 3 * width, width):
        pieces = dot(normed_t[...], qkv_grad[:, lower : lower + width]).T.astype(bf16)
        pieces = pieces.reshape(width // piece, piece, width)
        store_pieces(me, lower // piece, pieces, keep, send, 0, piece, plane_first)
    pieces = out_grad[...].reshape(width // piece, piece, width)
    store_pieces(me, 3 * width // piece, pieces, keep, send, 0, piece, plane_first)
    lines = [jnp.sum(sums[8 * row : 8 * row + 8, :], axis=0, keepdims=True) for row in range(4)]
    store_extra(lines, keep, send)
    for i in range(rows // size):
        result(i).wait()


def back_call(
    own, seg, offs, counts, qkv, key_t, mixed_grad, stats_a, stats_b, seg_rows, seg_cols,
    w_t, packed, normed_t, middle_grad, out_grad, vec,
):
    rows, width = packed.shape
    sent = S((HALF * w_t.shape[1] + 2 * EXTRA, width), bf16)
    moved = (qkv, key_t, mixed_grad, w_t, packed, normed_t, middle_grad)
    tiles = rows // 512
    return kernel_call(
        back_body,
        [SM] * 4 + [HB] * 3 + [VM] * 4 + [HB] * 4 + [VM] * 2,
        (S((rows, width), f32), sent, sent),
        [pltpu.VMEM(v.shape, v.dtype) for v in moved]
        + [
            pltpu.VMEM((rows, width), f32),
            pltpu.VMEM((rows, 3 * width), bf16),
            pltpu.VMEM((rows, width), f32),
            pltpu.VMEM((rows, width), f32),
            pltpu.VMEM((rows // BLK, HEADS * BLK), f32),
            pltpu.VMEM((32, width), f32),
            pltpu.SemaphoreType.DMA((3, tiles)),
            pltpu.SemaphoreType.DMA((4,)),
            pltpu.SemaphoreType.DMA((tiles,)),
        ],
        flops=22 * rows * width * width,
        micros=30,
        name="back",
        mib=60,
        out_specs=(HB, VM, VM),
    )(
        own, seg, offs, counts, qkv, key_t, mixed_grad, stats_a, stats_b, seg_rows, seg_cols,
        w_t, packed, normed_t, middle_grad, out_grad, vec,
    )


def unpack_body(win, offs, keep, input_grad, image_grads, slots):
    images_here, length = keep.shape
    rows, width = input_grad.shape
    before = lax.broadcasted_iota(jnp.int32, (length, length), 0)
    after = lax.broadcasted_iota(jnp.int32, (length, length), 1)
    tri = jnp.where(before <= after, 1.0, 0.0).astype(bf16)
    place = lax.broadcasted_iota(jnp.int32, (win, length), 0)

    @pl.when(pl.program_id(0) == 0)
    def _():
        kept = keep[...]
        ranks = dot(kept.astype(f32).astype(bf16), tri).astype(jnp.int32) - 1
        slots[...] = jnp.where(kept > 0, ranks, -4 * win)

    chosen, values = [], []
    for k in range(image_grads.shape[0]):
        i = pl.program_id(0) * image_grads.shape[0] + k
        base = pl.multiple_of(jnp.minimum((offs[i] // 8) * 8, rows - win), 8)
        shift = offs[i] - base
        chosen.append(jnp.where(place == slots[pl.ds(i, 1), :] + shift, 1.0, 0.0).astype(bf16))
        values.append(input_grad[pl.ds(base, win), :])
    highs = [value.astype(bf16) for value in values]
    rests = [(value - high.astype(f32)).astype(bf16) for value, high in zip(values, highs)]
    for k in range(image_grads.shape[0]):
        image_grads[k] = dot(chosen[k], highs[k], TN) + dot(chosen[k], rests[k], TN)


def unpack_call(offs, keep, input_grad):
    images_here, length = keep.shape
    rows, width = input_grad.shape
    win = (length + 7 + 7) // 8 * 8
    size = 5
    return kernel_call(
        functools.partial(unpack_body, win),
        [SM, whole(keep.shape), whole(input_grad.shape)],
        (S((images_here, length, width), f32),),
        [pltpu.VMEM((images_here, length), jnp.int32)],
        flops=4 * images_here * win * length * width,
        micros=9,
        name="unpack",
        mib=60,
        grid=(images_here // size,),
        out_specs=(pl.BlockSpec((size, length, width), lambda i: (i, 0, 0)),),
    )(offs, keep, input_grad)[0]


def to_halves(chunks):
    _, size, width = chunks.shape
    ordered = chunks.reshape(4, 4, 2, size, width).transpose(2, 1, 0, 3, 4).reshape(2, HALF * size, width)
    return ordered[0], ordered[1]


def from_halves(keep, send, parts, width, line_first):
    size = keep.shape[0] // HALF // parts
    both = jnp.stack([keep, send]).reshape(2, 4, 4, parts, size, width)
    both = both.transpose((1, 2, 0, 3, 4, 5) if line_first else (2, 1, 0, 3, 4, 5))
    return both.reshape(CHUNKS, parts, size, width)


def adamw(weight, grad, first, second, average, count, rate, decay):
    first_new = BETA_ONE * first + (1.0 - BETA_ONE) * grad
    second_new = BETA_TWO * second + (1.0 - BETA_TWO) * grad * grad
    first_hat = first_new / (1.0 - jnp.power(BETA_ONE, count))
    second_hat = second_new / (1.0 - jnp.power(BETA_TWO, count))
    weight_new = weight - rate * (first_hat / (jnp.sqrt(second_hat) + ADAM_EPS) + decay * weight)
    average_new = AVERAGE_DECAY * average + (1.0 - AVERAGE_DECAY) * weight_new
    return (weight_new, first_new, second_new, average_new)


def wide_of(ref, rows):
    return ref[rows, :].astype(f32)


def whole_extra(ref):
    return wide_of(ref, slice(-2 * EXTRA, -EXTRA)) + wide_of(ref, slice(-EXTRA, None))


def paired(values):
    while len(values) > 1:
        values = [values[i] + values[i + 1] for i in range(0, len(values), 2)]
    return values[0]


def put_extra(values, out, pieces):
    high, low = split_low(values)
    out[-EXTRA:, :] = high.astype(f32) + low.astype(f32)
    for piece in pieces:
        piece[-2 * EXTRA : -EXTRA, :] = high
        piece[-EXTRA:, :] = low


def merge_first_body(ffn_own, ffn_a, ffn_b, ffn_c, attn_own, attn_in, own, *pieces):
    ffn_size, attn_size = (ffn_own.shape[0] - EXTRA) // 4, (attn_own.shape[0] - 2 * EXTRA) // 4
    for part in range(4):
        rows = slice(part * ffn_size, (part + 1) * ffn_size)
        ffn = ffn_own[rows, :] + wide_of(ffn_a, rows) + wide_of(ffn_b, rows) + wide_of(ffn_c, rows)
        rows = slice(part * attn_size, (part + 1) * attn_size)
        attn = wide_of(attn_own, rows) + wide_of(attn_in, rows)
        out = own if part == 0 else pieces[part - 1]
        out[:ffn_size, :] = ffn.astype(out.dtype)
        out[ffn_size : ffn_size + attn_size, :] = attn.astype(out.dtype)
    known = paired([ffn_own[-EXTRA:, :]] + [whole_extra(r) for r in (ffn_a, ffn_b, ffn_c)])
    fresh = whole_extra(attn_own) + whole_extra(attn_in)
    put_extra(jnp.concatenate([fresh[:4], known[:8], fresh[12:]], axis=0), own, pieces)


def merge_first_call(ffn_own, ffn_in, attn_own, attn_in):
    width = ffn_own.shape[1]
    size = (ffn_own.shape[0] - EXTRA) // 4 + (attn_own.shape[0] - 2 * EXTRA) // 4
    out = kernel_call(
        merge_first_body,
        [VM] * 6,
        (S((size + EXTRA, width), f32),) + (S((size + 2 * EXTRA, width), bf16),) * 3,
        micros=3,
        name="merge_first",
    )(ffn_own, *ffn_in, attn_own, attn_in)
    return out[0], out[1:]


def merge_second_body(skip, own, in_a, in_b, in_c, out, *pieces):
    received = (in_a, in_b, in_c)
    size = out.shape[0] - EXTRA
    for part in range(4):
        rows = slice(skip + part * size, skip + (part + 1) * size)
        total = own[rows, :] + wide_of(in_a, rows) + wide_of(in_b, rows) + wide_of(in_c, rows)
        to = out if part == 0 else pieces[part - 1]
        to[:size, :] = total.astype(to.dtype)
    put_extra(paired([own[-EXTRA:, :]] + [whole_extra(r) for r in received]), out, pieces)


def merge_second_call(skip, own, received):
    width = own.shape[1]
    size = (own.shape[0] - EXTRA - skip) // 4
    out = kernel_call(
        functools.partial(merge_second_body, skip),
        [VM] * 4,
        (S((size + EXTRA, width), f32),) + (S((size + 2 * EXTRA, width), bf16),) * 3,
        micros=2,
        name="merge_second",
    )(own, *received)
    return out[0], out[1:]


def adamw_with(weight, grad, first, second, average, one, two, rate, decay):
    first_new = BETA_ONE * first + (1.0 - BETA_ONE) * grad
    second_new = BETA_TWO * second + (1.0 - BETA_TWO) * grad * grad
    weight_new = weight - rate * ((first_new / one) / (jnp.sqrt(second_new / two) + ADAM_EPS) + decay * weight)
    average_new = AVERAGE_DECAY * average + (1.0 - AVERAGE_DECAY) * weight_new
    return (weight_new, first_new, second_new, average_new)


def update(powers, states, grad, rate, decay, grad_out, outs, at=slice(None)):
    held = [ref[at] for ref in states]
    grad_out[at] = grad
    for ref, value in zip(outs, adamw_with(held[0], grad, *held[1:], powers[0], powers[1], rate, decay)):
        ref[at] = value


def finish_ffn_body(me, powers, own, in_a, in_b, in_c, *refs):
    states, outs = refs[:8], refs[8:]
    _, piece, width = states[0].shape
    received = (in_a, in_b, in_c)
    for k in range(2):
        rows = slice(k * piece, (k + 1) * piece)
        grad = own[rows, :] + wide_of(in_a, rows) + wide_of(in_b, rows) + wide_of(in_c, rows)
        update(powers, states[:4], grad, MATRIX_RATE, WEIGHT_DECAY, outs[0], outs[2:6], k)
    sums = paired([own[-EXTRA:, :]] + [whole_extra(r) for r in received])
    across = width // piece
    row = lax.broadcasted_iota(jnp.int32, (EXTRA, width), 0)
    line = jnp.sum(jnp.where(row == 8 + me[0] // across, sums, 0.0), axis=0, keepdims=True)
    line = jnp.broadcast_to(line, (8, width))
    shift = (me[0] % across) * piece
    line = jnp.where(shift == 0, line, pltpu.roll(line, width - shift, 1))
    update(powers, states[4:], line[:1, :piece], VECTOR_RATE, 0.0, outs[1], outs[6:])


def finish_ffn_call(me, powers, own, received, states):
    kinds = [S(states[k].shape, f32) for k in (0, 4)]
    out = kernel_call(
        finish_ffn_body,
        [SM, SM] + [VM] * 12,
        tuple(kinds) + tuple(kind for kind in kinds for _ in range(4)),
        micros=2,
        name="finish_ffn",
    )(me, powers, own, *received, *states)
    return out[0], out[1], out[2:6], out[6:]


def finish_attn_body(powers, own, in_a, in_b, in_c, *refs):
    states, outs = refs[:8], refs[8:]
    piece = states[0].shape[0]
    rows = slice(0, piece)
    grad = own[rows, :] + wide_of(in_a, rows) + wide_of(in_b, rows) + wide_of(in_c, rows)
    update(powers, states[:4], grad, MATRIX_RATE, WEIGHT_DECAY, outs[0], outs[2:6])
    sums = paired([own[-EXTRA:, :]] + [whole_extra(r) for r in (in_a, in_b, in_c)])
    vec = jnp.concatenate([sums[:4], own[-EXTRA + 4 : -EXTRA + 8, :]], axis=0)
    update(powers, states[4:], vec, VECTOR_RATE, 0.0, outs[1], outs[6:])


def finish_attn_call(powers, own, received, states):
    kinds = [S(states[k].shape, f32) for k in (0, 4)]
    out = kernel_call(
        finish_attn_body,
        [SM] + [VM] * 12,
        tuple(kinds) + tuple(kind for kind in kinds for _ in range(4)),
        micros=2,
        name="finish_attn",
    )(powers, own, *received, *states)
    return out[0], out[1], out[2:6], out[6:]


def body(
    images, keep_mask, kept_counts, pack_offsets, segment_ids, cotangent,
    attn_weight, ffn_weight, up_bias, vectors,
    attn_first, ffn_first, bias_first, vec_first,
    attn_second, ffn_second, bias_second, vec_second,
    attn_average, ffn_average, bias_average, vec_average, step,
):
    width = images.shape[2]
    rows = segment_ids.shape[0]
    both = ("dp", "mp")
    piece = attn_weight.shape[1]
    tree = lax.axis_size("dp") == 8 and lax.axis_size("mp") == 4
    bias_row = jnp.pad(up_bias.astype(bf16)[None, :], ((0, 15), (0, width - piece)))
    seg_rows = segment_ids.reshape(rows // BLK, BLK)
    placed = place_call(images, keep_mask, pack_offsets, rows)
    count = step[0].astype(f32)
    powers = jnp.stack([1.0 - jnp.power(BETA_ONE, count), 1.0 - jnp.power(BETA_TWO, count)])
    if tree:
        own = (lax.axis_index("dp") * 4 + lax.axis_index("mp")).astype(jnp.int32)[None]
        pieces = jnp.concatenate(
            [attn_weight.astype(bf16).T, ffn_weight[0].astype(bf16).T, ffn_weight[1].astype(bf16).T, bias_row], axis=0
        )
        lines = [pieces] + [over_line(pieces, k) for k in (1, 2, 3)]
        placed, *lines = tie(placed, *lines)
        attn_line = jnp.concatenate([line[:piece] for line in lines], axis=0)
        ffn_line = jnp.concatenate([line[piece:] for line in lines], axis=0)
        attn_mine = gather_plane(attn_line)
        normed, normed_t, seg_cols = norm_call(placed, seg_rows, vectors)
        attn_mine, normed, ffn_line = tie(attn_mine, normed, ffn_line)
        attn_other = over_core(attn_mine)
        ffn_lines = [ffn_line] + [over_plane(ffn_line, k) for k in (1, 2, 3)]
    else:
        own = jnp.zeros((1,), jnp.int32)
        attn_all = lax.all_gather(attn_weight.astype(bf16).T, both, axis=0, tiled=True)
        ffn_all = lax.all_gather(jnp.swapaxes(ffn_weight.astype(bf16), 1, 2), both, axis=1, tiled=True)
        bias_all = lax.all_gather(up_bias.astype(bf16), both, axis=0, tiled=True)
        size = 4 * width // CHUNKS
        ffn_all = jnp.concatenate(
            [
                ffn_all[0].reshape(CHUNKS, size, width),
                ffn_all[1].reshape(CHUNKS, size, width),
                jnp.pad(bias_all.reshape(CHUNKS, 1, size), ((0, 0), (0, 15), (0, width - size))),
            ],
            axis=1,
        )
        attn_mine, attn_other = to_halves(attn_all.reshape(CHUNKS, size, width))
        ffn_mine, ffn_other = to_halves(ffn_all)
        normed, normed_t, seg_cols = norm_call(placed, seg_rows, vectors)
    where = (segment_ids, pack_offsets, kept_counts)
    blocks = rows // BLK
    late = blocks // 4
    qkv, key_t, value_t, w_t, mixed_a, stats_a = attend_first_call(
        blocks - late, own, *where, normed, attn_mine, attn_other, vectors, seg_rows, seg_cols
    )
    if tree:
        qkv, mixed_a, *ffn_lines = tie(qkv, mixed_a, *ffn_lines)
        ffn_mine = jnp.concatenate(ffn_lines, axis=0)
        ffn_other = over_core(ffn_mine)
    mixed_b, stats_b = attend_last_call(late, *where, qkv, value_t, seg_rows, seg_cols)
    if tree:
        mixed_b, ffn_mine, ffn_other = tie(mixed_b, ffn_mine, ffn_other)
    layer_out, middle_grad, mixed_grad, ffn_keep, ffn_send = feed_call(
        own, placed, mixed_a, mixed_b, cotangent, vectors, w_t, ffn_mine, ffn_other
    )
    if tree:
        ffn_in = over_core(ffn_send)
    out_grad = side_call(mixed_a, mixed_b, middle_grad)
    if tree:
        out_grad, ffn_in = tie(out_grad, ffn_in)
        ffn_own, *ffn_out = combine_call(ffn_keep, [ffn_in], 4, EXTRA)
        out_grad, ffn_own, *ffn_out = tie(out_grad, ffn_own, *ffn_out)
        ffn_in = [over_line(p, k + 1) for k, p in enumerate(ffn_out)]
    input_grad, attn_keep, attn_send = back_call(
        own, *where, qkv, key_t, mixed_grad, stats_a, stats_b, seg_rows, seg_cols,
        w_t, placed, normed_t, middle_grad, out_grad, vectors,
    )
    index = lax.axis_index("dp") * lax.axis_size("mp") + lax.axis_index("mp")
    if tree:
        input_grad, attn_send, *ffn_in = tie(input_grad, attn_send, *ffn_in)
        attn_in = over_core(attn_send)
        states = [v.T for v in (attn_weight, attn_first, attn_second, attn_average)]
        states += [vectors, vec_first, vec_second, vec_average]
        ffn_states = [jnp.swapaxes(v, 1, 2) for v in (ffn_weight, ffn_first, ffn_second, ffn_average)]
        ffn_states += [v[None, :] for v in (up_bias, bias_first, bias_second, bias_average)]
        merged, pieces = merge_first_call(ffn_own, ffn_in, attn_keep, attn_in)
        input_grad, *pieces = tie(input_grad, *pieces)
        received = [over_plane(p, k + 1) for k, p in enumerate(pieces)]
        image_grads = unpack_call(pack_offsets, keep_mask, input_grad)
        image_grads, *received = tie(image_grads, *received)
        attn_own, pieces = merge_second_call(2 * piece, merged, received)
        image_grads, merged, *pieces = tie(image_grads, merged, *pieces)
        last = [over_line(p, k + 1) for k, p in enumerate(pieces)]
        ffn_grad, bias_grad, ffn_up, bias_up = finish_ffn_call(own, powers, merged, received, ffn_states)
        image_grads, ffn_grad, *last = tie(image_grads, ffn_grad, *last)
        attn_grad, vec_grad, attn_up, vec_up = finish_attn_call(powers, attn_own, last, states)
        attn_grad, ffn_grad, bias_grad = attn_grad.T, jnp.swapaxes(ffn_grad, 1, 2), bias_grad[0]
        attn_up, ffn_up = [v.T for v in attn_up], [jnp.swapaxes(v, 1, 2) for v in ffn_up]
        bias_up = [v[0] for v in bias_up]
    else:
        image_grads = unpack_call(pack_offsets, keep_mask, input_grad)
        base = ffn_keep.shape[0] - 2 * EXTRA
        ffn_t = from_halves(ffn_keep[:base], ffn_send[:base], 2, width, True)
        ffn_t = jnp.swapaxes(ffn_t, 0, 1).reshape(2, 4 * width, width)
        ffn_t = lax.psum_scatter(ffn_t.astype(f32), both, scatter_dimension=1, tiled=True)
        ffn_grad = jnp.swapaxes(ffn_t, 1, 2)
        known = ffn_keep[base : base + EXTRA].astype(f32) + ffn_keep[base + EXTRA :].astype(f32)
        base = attn_keep.shape[0] - 2 * EXTRA
        attn_t = from_halves(attn_keep[:base], attn_send[:base], 1, width, False).reshape(4 * width, width)
        attn_grad = lax.psum_scatter(attn_t.astype(f32), both, scatter_dimension=0, tiled=True).T
        sums = attn_keep[base : base + EXTRA].astype(f32) + attn_keep[base + EXTRA :].astype(f32)
        sums = lax.psum(jnp.concatenate([sums[:4], known[:8]], axis=0), both)
        vec_grad, bias_sums = sums[:8], sums[8:]
        bias_grad = lax.dynamic_slice_in_dim(bias_sums.reshape(4 * width), index * piece, piece, 0)
        attn_up = adamw(attn_weight, attn_grad, attn_first, attn_second, attn_average, count, MATRIX_RATE, WEIGHT_DECAY)
        vec_up = adamw(vectors, vec_grad, vec_first, vec_second, vec_average, count, VECTOR_RATE, 0.0)
        ffn_up = adamw(ffn_weight, ffn_grad, ffn_first, ffn_second, ffn_average, count, MATRIX_RATE, WEIGHT_DECAY)
        bias_up = adamw(up_bias, bias_grad, bias_first, bias_second, bias_average, count, VECTOR_RATE, 0.0)
    news = [part[k] for k in range(4) for part in (attn_up, ffn_up, bias_up, vec_up)]
    return (layer_out, image_grads, attn_grad, ffn_grad, bias_grad, vec_grad, *news)


def solution(mesh):
    both = ("dp", "mp")
    matrix, slab, line = P(None, both), P(None, None, both), P(both)
    states = (matrix, slab, line, P())
    return jax.shard_map(
        body,
        mesh=mesh,
        in_specs=(P(both, None, None), P(both, None), line, line, line, P(both, None), *states * 4, P()),
        out_specs=(P(both, None), P(both, None, None), *states, *states * 4),
        check_vma=False,
    )
```

```python
import functools
import math

import jax
import jax.numpy as jnp
from jax import lax
from jax.experimental import pallas as pl
from jax.experimental.pallas import tpu as pltpu
from jax.sharding import PartitionSpec as P

HEADS = 6
HEAD = 64
PAIR = 2 * HEAD
PAIRS = HEADS // 2
BLK = 128
REACH = 5
CHUNKS = 32
HALF = CHUNKS // 2
EXTRA = 16
EXCLUDED = -8.0e9
INCLUDED = 3.0e38

NORM_EPS = 1e-06
BETA_ONE = 0.9
BETA_TWO = 0.999
ADAM_EPS = 1e-08
MATRIX_RATE = 0.05
VECTOR_RATE = 0.2
WEIGHT_DECAY = 0.05
AVERAGE_DECAY = 0.8

LOG2E = 1.4426950408889634
SCORE_LOG2 = LOG2E / math.sqrt(HEAD)
SCALE = 1.0 / math.sqrt(HEAD)

f32 = jnp.float32
bf16 = jnp.bfloat16
NN = (((1,), (0,)), ((), ()))
NT = (((1,), (1,)), ((), ()))
TN = (((0,), (0,)), ((), ()))
VM = pl.BlockSpec(memory_space=pltpu.VMEM)
SM = pl.BlockSpec(memory_space=pltpu.SMEM)
HB = pl.BlockSpec(memory_space=pl.ANY)
S = jax.ShapeDtypeStruct


def dot(left, right, dims=NN):
    return lax.dot_general(left, right, dims, preferred_element_type=f32)


def kernel_call(body, ins, outs, scratch=(), flops=0, micros=1, name=None, grid=(), out_specs=None, mib=16):
    return pl.pallas_call(
        body,
        grid=grid,
        out_shape=outs,
        in_specs=ins,
        out_specs=out_specs or tuple(VM for _ in outs),
        scratch_shapes=list(scratch),
        compiler_params=pltpu.CompilerParams(vmem_limit_bytes=mib * 2**20),
        cost_estimate=pl.CostEstimate(flops=flops, bytes_accessed=micros * 3_500_000, transcendentals=0),
        name=name,
    )


def whole(shape):
    return pl.BlockSpec(shape, lambda i: (0,) * len(shape))


def row_sums(values):
    rows, width = values.shape
    return jnp.sum(values.reshape(rows // 8, 8, width), axis=0)


def norm_parts(values):
    scale = 1.0 / values.shape[-1]
    centre = jnp.sum(values, axis=-1, keepdims=True) * scale
    centred = values - centre
    spread = jnp.sum(centred * centred, axis=-1, keepdims=True) * scale
    inverse = lax.rsqrt(spread + NORM_EPS)
    return centred * inverse, inverse


def norm_back(unit, inverse, gain, grad):
    scale = 1.0 / unit.shape[-1]
    scaled = grad * gain
    mean = jnp.sum(scaled, axis=-1, keepdims=True) * scale
    along = jnp.sum(scaled * unit, axis=-1, keepdims=True) * scale
    return inverse * (scaled - mean - unit * along)


def tile_rows(count, size):
    return pl.ds(pl.multiple_of(count * size, size), size)


def plane_first(apart):
    return (apart & 3) * 4 + lax.shift_right_logical(apart, 2)


def line_first(apart):
    return apart


def spread_pieces(own, halves, out):
    for near in range(2):
        for slot in range(HALF):
            apart = near + 2 * ((slot // 4) + 4 * (slot % 4))
            out[own ^ apart] = halves[near][slot * out.shape[1] : (slot + 1) * out.shape[1], :]


def store_pieces(own, start, pieces, keep, send, at, step, order):
    count, size, _ = pieces.shape
    odd = (own & 1) == 1
    for e in range(0, count, 2):
        apart = lax.shift_right_logical(own, 1) ^ ((start + e) // 2)
        row = pl.multiple_of(order(apart) * step + at, 16)
        even_piece, odd_piece = pieces[e], pieces[e + 1]
        keep[pl.ds(row, size), :] = jnp.where(odd, odd_piece, even_piece)
        send[pl.ds(row, size), :] = jnp.where(odd, even_piece, odd_piece)


def split_low(values):
    high = values.astype(bf16)
    return high, (values - high.astype(f32)).astype(bf16)


def combine_body(parts, size, extra, count, *refs):
    own, received, outs = refs[0], refs[1 : 1 + count], refs[1 + count :]
    base = parts * size
    for part in range(parts):
        rows = slice(part * size, (part + 1) * size)
        total = own[rows, :].astype(f32)
        for other in received:
            total = total + other[rows, :].astype(f32)
        if part == 0:
            outs[0][:size, :] = total
        else:
            outs[part][:size, :] = total.astype(bf16)
    if extra:
        if own.dtype == bf16:
            sums = [own[base : base + extra, :].astype(f32) + own[base + extra :, :].astype(f32)]
        else:
            sums = [own[base:, :]]
        sums += [r[base : base + extra, :].astype(f32) + r[base + extra :, :].astype(f32) for r in received]
        while len(sums) > 1:
            sums = [sums[i] + sums[i + 1] for i in range(0, len(sums), 2)]
        high, low = split_low(sums[0])
        outs[0][size:, :] = high.astype(f32) + low.astype(f32) if parts > 1 else sums[0]
        for out in outs[1:]:
            out[size : size + extra, :] = high
            out[size + extra :, :] = low


def combine_call(own, received, parts, extra):
    size = (received[0].shape[0] - 2 * extra) // parts
    width = own.shape[1]
    outs = (S((size + extra, width), f32),) + (S((size + 2 * extra, width), bf16),) * (parts - 1)
    return kernel_call(
        functools.partial(combine_body, parts, size, extra, len(received)),
        [VM] * (1 + len(received)),
        outs,
        flops=own.size * len(received),
        micros=2,
        name="combine",
    )(own, *received)


def pieces_body(attn, ffn, bias, out, line):
    piece, width = attn.shape
    line[...] = jnp.zeros_like(line)
    line[0:1, :piece] = bias[...]
    out[:piece, :] = attn[...].astype(bf16)
    for k in range(2):
        out[(1 + k) * piece : (2 + k) * piece, :] = ffn[k].astype(bf16)
    out[3 * piece :, :] = line[...].astype(bf16)


def pieces_call(attn, ffn, bias):
    piece, width = attn.shape
    return kernel_call(
        pieces_body,
        [VM] * 3,
        (S((3 * piece + 16, width), bf16),),
        [pltpu.VMEM((16, width), f32)],
        name="pieces",
        mib=60,
    )(attn, ffn, bias)[0]


def over_core(values):
    return lax.ppermute(values, "mp", [(i, i ^ 1) for i in range(lax.axis_size("mp"))])


def over_plane(values, apart):
    devices = lax.axis_size("dp") * lax.axis_size("mp")
    return lax.ppermute(values, ("dp", "mp"), [(i, i ^ (2 * apart)) for i in range(devices)])


def over_line(values, apart):
    return lax.ppermute(values, "dp", [(i, i ^ (2 * apart)) for i in range(lax.axis_size("dp"))])


def tie(*values):
    return lax.optimization_barrier(values)


def gather_plane(pieces):
    return jnp.concatenate([pieces] + [over_plane(pieces, k) for k in (1, 2, 3)], axis=0)


def place_body(win, offs, images, keep, packed, acc, slots):
    images_here, length = keep.shape
    rows, width = packed.shape
    size = images.shape[0]
    step = pl.program_id(0)

    @pl.when(step == 0)
    def _():
        before = lax.broadcasted_iota(jnp.int32, (length, length), 0)
        after = lax.broadcasted_iota(jnp.int32, (length, length), 1)
        tri = jnp.where(before <= after, 1.0, 0.0).astype(bf16)
        kept = keep[...]
        ranks = dot(kept.astype(f32).astype(bf16), tri).astype(jnp.int32) - 1
        slots[...] = jnp.where(kept > 0, ranks, -4 * win)
        acc[0:8, :] = jnp.zeros((8, width), f32)

    place = lax.broadcasted_iota(jnp.int32, (win, length), 0)
    starts = [offs[step * size + k] for k in range(size)]
    bases = [pl.multiple_of((start // 8) * 8, 8) for start in starts]
    lines = [slots[pl.ds(step * size + k, 1), :] + (starts[k] - bases[k]) for k in range(size)]
    chosen = [jnp.where(place == line, 1.0, 0.0).astype(bf16) for line in lines]
    moved = [dot(chosen[k], images[k]) for k in range(size)]
    for base, part in zip(bases, moved):
        acc[pl.ds(base, 8), :] += part[0:8]
        acc[pl.ds(base + 8, win - 8), :] = part[8:]

    @pl.when(step == pl.num_programs(0) - 1)
    def _():
        packed[...] = acc[:rows, :].astype(bf16)


def place_call(images, keep, offs, rows):
    images_here, length, width = images.shape
    win = (length + 7 + 7) // 8 * 8
    size = 5
    return kernel_call(
        functools.partial(place_body, win),
        [SM, pl.BlockSpec((size, length, width), lambda i: (i, 0, 0)), whole(keep.shape)],
        (S((rows, width), bf16),),
        [pltpu.VMEM((rows + win, width), f32), pltpu.VMEM((images_here, length), jnp.int32)],
        flops=2 * images_here * win * length * width,
        micros=6,
        name="place",
        mib=60,
        grid=(images_here // size,),
        out_specs=(whole((rows, width)),),
    )(offs, images, keep)[0]


def norm_body(packed, seg_rows, vec, normed, normed_t, seg_cols):
    rows, width = packed.shape
    step = pl.program_id(0)
    sub = 128
    parts = [slice(k * sub, (k + 1) * sub) for k in range(rows // sub)]
    units = [norm_parts(packed[at, :].astype(f32))[0] for at in parts]
    lows = [(unit * vec[0:1, :] + vec[1:2, :]).astype(bf16) for unit in units]
    for at, low in zip(parts, lows):
        normed[at, :] = low
    for at, low in zip(parts, lows):
        normed_t[:, at] = low.T
    for k in range(rows // BLK):
        line = seg_rows[pl.ds(step * (rows // BLK) + k, 1), :]
        seg_cols[k * BLK : (k + 1) * BLK, :] = jnp.broadcast_to(line, (BLK, BLK)).T


def norm_call(packed, seg_rows, vec):
    rows, width = packed.shape
    size = 512
    return kernel_call(
        norm_body,
        [pl.BlockSpec((size, width), lambda i: (i, 0)), whole(seg_rows.shape), whole(vec.shape)],
        (S((rows, width), bf16), S((width, rows), bf16), S((rows, BLK), jnp.int32)),
        flops=rows * width * 12,
        micros=5,
        name="norm",
        mib=60,
        grid=(rows // size,),
        out_specs=(
            pl.BlockSpec((size, width), lambda i: (i, 0)),
            pl.BlockSpec((width, size), lambda i: (0, i)),
            pl.BlockSpec((size, BLK), lambda i: (i, 0)),
        ),
    )(packed, seg_rows, vec)


def window(seg, offs, counts, j, images_here, tiles, step):
    first = seg[j * BLK]
    last = seg[j * BLK + BLK - 1]
    used = last < images_here
    last_here = jnp.where(used, last, 0)
    end = jnp.where(used, offs[last_here] + counts[last_here], tiles * BLK)
    low = jnp.minimum(offs[first] // BLK, tiles - 2)
    return low, jnp.maximum((end + step - 1) // step - low * (BLK // step), 2 * BLK // step)


def masked_pair(pair):
    lane = lax.broadcasted_iota(jnp.int32, pair.shape, 1)
    none = jnp.zeros_like(pair)
    return jnp.concatenate([jnp.where(lane < HEAD, pair, none), jnp.where(lane >= HEAD, pair, none)], axis=0)


def limits(seg_rows, seg_cols, j, keys):
    same = seg_cols[keys, :] == seg_rows[pl.ds(j, 1), :]
    lim = jnp.where(same, INCLUDED, EXCLUDED)
    return jnp.concatenate([lim, lim], axis=1)


def over_windows(seg, offs, counts, tiles, base, first, blocks, block, step=BLK, before=None):
    def one(j, carry):
        if before is not None:
            before(j)
        low, size = window(seg, offs, counts, j, offs.shape[0], tiles, step)
        for n in range(2 * BLK // step, REACH * BLK // step + 1):

            @pl.when(size == n)
            def _():
                block(j, pl.ds(pl.multiple_of((low - base) * BLK, BLK), n * step))

        return carry

    lax.fori_loop(first, first + blocks, one, 0)


def attend_blocks(base, first, blocks, seg, offs, counts, qkv, value_t, seg_rows, seg_cols, mixed_t, stats):
    width = value_t.shape[0]
    tiles = seg.shape[0] // BLK

    def block(j, keys):
        here = tile_rows(j - base, BLK)
        there = tile_rows(j - first, BLK)
        lim = limits(seg_rows, seg_cols, j, keys)
        ats = [slice(p * PAIR, (p + 1) * PAIR) for p in range(PAIRS)]
        raws = [
            dot(qkv[keys, width + p * PAIR : width + (p + 1) * PAIR], masked_pair(qkv[here, ats[p]]), NT)
            for p in range(PAIRS)
        ]
        raws = [jnp.minimum(raw, lim) for raw in raws]
        tops = [jnp.max(raw, axis=0, keepdims=True) for raw in raws]
        expos = [jnp.exp2((raw - top) * SCORE_LOG2) for raw, top in zip(raws, tops)]
        totals = [jnp.sum(expo, axis=0, keepdims=True) for expo in expos]
        lows = [(expo * (1.0 / total)).astype(bf16) for expo, total in zip(expos, totals)]
        outs = [dot(value_t[at, keys], low) for at, low in zip(ats, lows)]
        for p in range(PAIRS):
            out = outs[p]
            mixed_t[p * PAIR : p * PAIR + HEAD, there] = out[:HEAD, :BLK].astype(bf16)
            mixed_t[p * PAIR + HEAD : (p + 1) * PAIR, there] = out[HEAD:, BLK:].astype(bf16)
            level = tops[p] * SCORE_LOG2 + jnp.log2(totals[p])
            stats[pl.ds(j - first, 1), p * 2 * BLK : (p + 1) * 2 * BLK] = level

    over_windows(seg, offs, counts, tiles, base, first, blocks, block)


def attend_first_body(
    own, seg, offs, counts, normed, mine, other, vec, seg_rows, seg_cols,
    qkv_out, key_out, value_out, w_out, mixed_t, stats,
    qkv, key_t, value_t, w_t, sems,
):
    rows, width = normed.shape
    size = 512
    spread_pieces(own[0], (mine, other), w_t)
    units = w_t.shape[0] * w_t.shape[1]
    weights = w_t[...].reshape(units, width)[: 3 * width]
    bias = jnp.concatenate([vec[2:3, :], jnp.zeros((1, width), f32), vec[3:4, :]], axis=1)
    last = pltpu.make_async_copy(w_t, w_out, sems.at[3, 0])
    last.start()

    def copies(i):
        sl = tile_rows(i, size)
        return [
            pltpu.make_async_copy(qkv.at[sl, :], qkv_out.at[sl, :], sems.at[0, i]),
            pltpu.make_async_copy(key_t.at[:, sl], key_out.at[:, sl], sems.at[1, i]),
            pltpu.make_async_copy(value_t.at[:, sl], value_out.at[:, sl], sems.at[2, i]),
        ]

    def project(i, carry):
        sl = tile_rows(i, size)
        low = (dot(normed[sl, :], weights, NT) + bias).astype(bf16)
        qkv[sl, :] = low
        key_t[:, sl] = low[:, width : 2 * width].T
        value_t[:, sl] = low[:, 2 * width :].T
        for copy in copies(i):
            copy.start()
        return carry

    lax.fori_loop(0, rows // size, project, 0)
    attend_blocks(
        0, 0, mixed_t.shape[1] // BLK, seg, offs, counts, qkv, value_t, seg_rows, seg_cols, mixed_t, stats
    )
    for i in range(rows // size):
        for copy in copies(i):
            copy.wait()
    last.wait()


def attend_first_call(blocks, own, seg, offs, counts, normed, mine, other, vec, seg_rows, seg_cols):
    rows, width = normed.shape
    piece = mine.shape[0] // HALF
    kept = ((rows, 3 * width), (width, rows), (width, rows), (CHUNKS, piece, width))
    return kernel_call(
        attend_first_body,
        [SM, SM, SM, SM, VM, VM, VM, VM, VM, VM],
        tuple(S(shape, bf16) for shape in kept)
        + (S((width, blocks * BLK), bf16), S((blocks, HEADS * BLK), f32)),
        [pltpu.VMEM(shape, bf16) for shape in kept] + [pltpu.SemaphoreType.DMA((4, rows // 512))],
        flops=2 * rows * width * 3 * width,
        micros=20,
        name="attend_first",
        mib=60,
        out_specs=(HB, HB, HB, HB, VM, VM),
    )(own, seg, offs, counts, normed, mine, other, vec, seg_rows, seg_cols)


def attend_last_call(blocks, seg, offs, counts, qkv, value_t, seg_rows, seg_cols):
    width, rows = value_t.shape
    part = (blocks + REACH - 1) * BLK
    while rows % part:
        part += BLK
    at = rows // part - 1
    tiles = rows // BLK
    return kernel_call(
        functools.partial(attend_blocks, tiles - part // BLK, tiles - blocks, blocks),
        [
            SM,
            SM,
            SM,
            pl.BlockSpec((part, 3 * width), lambda i: (at, 0)),
            pl.BlockSpec((width, part), lambda i: (0, at)),
            whole(seg_rows.shape),
            pl.BlockSpec((part, BLK), lambda i: (at, 0)),
        ],
        (S((width, blocks * BLK), bf16), S((blocks, HEADS * BLK), f32)),
        grid=(1,),
        out_specs=(whole((width, blocks * BLK)), whole((blocks, HEADS * BLK))),
        flops=4 * blocks * BLK * 512 * width,
        micros=5,
        name="attend_last",
        mib=60,
    )(seg, offs, counts, qkv, value_t, seg_rows, seg_cols)


def attend_back(
    seg, offs, counts, qkv, key_t, mixed_grad, stats_a, stats_b, seg_rows, seg_cols, qkv_grad, key_grad, value_grad, stats, before
):
    rows, width = mixed_grad.shape
    key_grad[...] = jnp.zeros_like(key_grad)
    value_grad[...] = jnp.zeros_like(value_grad)
    stats[: stats_a.shape[0], :] = stats_a[...]
    stats[stats_a.shape[0] :, :] = stats_b[...]

    def block(j, keys):
        here = tile_rows(j, BLK)
        lim = limits(seg_rows, seg_cols, j, keys)
        ats = [slice(p * PAIR, (p + 1) * PAIR) for p in range(PAIRS)]
        levels = stats[pl.ds(j, 1), :]
        levels = [levels[:, p * 2 * BLK : (p + 1) * 2 * BLK] for p in range(PAIRS)]
        queries = [masked_pair(qkv[here, at]) for at in ats]
        outs = [masked_pair(mixed_grad[here, at]) for at in ats]
        raws = [
            dot(qkv[keys, width + p * PAIR : width + (p + 1) * PAIR], queries[p], NT) for p in range(PAIRS)
        ]
        grads = [
            dot(qkv[keys, 2 * width + p * PAIR : 2 * width + (p + 1) * PAIR], outs[p], NT) for p in range(PAIRS)
        ]
        probs = [jnp.exp2(jnp.minimum(raw, lim) * SCORE_LOG2 - level) for raw, level in zip(raws, levels)]
        inners = [jnp.sum(prob * grad, axis=0, keepdims=True) for prob, grad in zip(probs, grads)]
        lows = [prob.astype(bf16) for prob in probs]
        score_grads = [
            (prob * (grad - inner)).astype(bf16) for prob, grad, inner in zip(probs, grads, inners)
        ]
        for p in range(PAIRS):
            value_grad[keys, ats[p]] += dot(lows[p], outs[p])
        for p in range(PAIRS):
            key_grad[keys, ats[p]] += dot(score_grads[p], queries[p])
        for p in range(PAIRS):
            query_t = dot(key_t[ats[p], keys], score_grads[p]) * SCALE
            joined = jnp.concatenate([query_t[:HEAD, :BLK], query_t[HEAD:, BLK:]], axis=0)
            qkv_grad[here, ats[p]] = joined.T.astype(bf16)

    over_windows(seg, offs, counts, rows // BLK, 0, 0, rows // BLK, block, BLK // 2, before)


def bias_line(rows_of, units):
    chunks, size = rows_of.shape
    column = lax.broadcasted_iota(jnp.int32, (size, units), 1)
    within = lax.broadcasted_iota(jnp.int32, (size, units), 0)
    repeat = jnp.where(column % size == within, 1.0, 0.0).astype(bf16)
    wide = dot(rows_of, repeat)
    owner = lax.broadcasted_iota(jnp.int32, (chunks, units), 1) // size
    mine = owner == lax.broadcasted_iota(jnp.int32, (chunks, units), 0)
    return jnp.sum(jnp.where(mine, wide, 0.0), axis=0, keepdims=True)


def feed_body(
    sub, own, packed, mixed_a, mixed_b, cot, vec, w_t, mine, other,
    layer_out, middle_grad, mixed_grad, keep, send,
    all_s, up_s, down_s, hid_s, gi_s, n2t_s, glt_s, bias_s, sums, bias_sum, mixed,
):
    size, width = packed.shape
    step, steps = pl.program_id(0), pl.num_programs(0)
    me = own[0]
    units = up_s.shape[0]
    piece = units // CHUNKS

    @pl.when(step == 0)
    def _():
        spread_pieces(me, (mine, other), all_s)
        up_s[...] = all_s[:, :piece, :].reshape(units, width)
        down_s[...] = all_s[:, piece : 2 * piece, :].reshape(units, width)
        bias_s[...] = bias_line(all_s[:, 2 * piece, :piece], units)
        bias_sum[...] = jnp.zeros_like(bias_sum)
        sums[...] = jnp.zeros_like(sums)

    @pl.when(step < steps - 1)
    def _():
        mixed[...] = mixed_a[...]

    @pl.when(step == steps - 1)
    def _():
        mixed[...] = mixed_b[...]

    w_out_t = w_t[...].reshape(width, width)
    parts = [slice(k * sub, (k + 1) * sub) for k in range(size // sub)]
    rows = [pl.ds(pl.multiple_of(step * size + k * sub, sub), sub) for k in range(size // sub)]
    mids = [packed[at, :].astype(f32) + dot(mixed[:, at].T, w_out_t, NT) + vec[4:5, :] for at in parts]
    valids = [
        lax.broadcasted_iota(jnp.int32, (sub, 1), 0) + step * size + k * sub < steps * size - 1
        for k in range(size // sub)
    ]
    outs = [jnp.where(valid, cot[at, :].astype(f32), 0.0) for valid, at in zip(valids, parts)]
    out_lows = [out.astype(bf16) for out in outs]
    grads = [dot(out_low, down_s[...], NT) for out_low in out_lows]
    units_of = [norm_parts(middle) for middle in mids]
    lows = [(unit * vec[5:6, :] + vec[6:7, :]).astype(bf16) for unit, _ in units_of]
    us = [dot(low, up_s[...], NT) + bias_s[...] for low in lows]
    downs, backs = [], []
    for k in range(size // sub):
        n2t_s[:, rows[k]] = lows[k].T
        glt_s[:, rows[k]] = out_lows[k].T
        u = us[k]
        phi = 0.5 + 0.5 * lax.erf(u * (1.0 / math.sqrt(2.0)))
        hidden = (u * phi).astype(bf16)
        hid_s[rows[k], :] = hidden
        slope = phi + u * jnp.exp2(u * u * (-0.5 * LOG2E)) * (1.0 / math.sqrt(2.0 * math.pi))
        grad_in = grads[k] * slope
        bias_sum[...] += row_sums(grad_in)
        grad_in_low = grad_in.astype(bf16)
        gi_s[rows[k], :] = grad_in_low
        downs.append(dot(hidden, down_s[...]))
        backs.append(dot(grad_in_low, up_s[...]))
    totals = []
    for k, at in enumerate(parts):
        unit, inverse = units_of[k]
        layer_out[at, :] = jnp.where(valids[k], mids[k] + downs[k] + vec[7:8, :], 0.0).astype(bf16)
        n2_grad = backs[k]
        sums[8:16, :] += row_sums(n2_grad * unit)
        sums[16:24, :] += row_sums(n2_grad)
        total = outs[k] + norm_back(unit, inverse, vec[5:6, :], n2_grad)
        middle_grad[at, :] = total
        sums[0:8, :] += row_sums(total)
        sums[24:32, :] += row_sums(outs[k])
        totals.append(total.astype(bf16))
    for k, at in enumerate(parts):
        mixed_grad[at, :] = dot(totals[k], w_out_t).astype(bf16)

    @pl.when(step == steps - 1)
    def _():
        wide = 2 * width
        for lower in range(0, units, wide):
            hs = slice(lower, lower + wide)
            for index, (left, right) in enumerate(((n2t_s, gi_s), (glt_s, hid_s))):
                pieces = dot(left[...], right[:, hs]).T.astype(bf16).reshape(wide // piece, piece, width)
                store_pieces(me, lower // piece, pieces, keep, send, index * piece, 2 * piece, line_first)
        line = jnp.sum(bias_sum[...], axis=0, keepdims=True)
        lines = [jnp.sum(sums[8 * row : 8 * row + 8, :], axis=0, keepdims=True) for row in range(4)]
        lines += [line[:, row * width : (row + 1) * width] for row in range(units // width)]
        store_extra(lines, keep, send)


def store_extra(lines, keep, send):
    width = keep.shape[1]
    lines = jnp.concatenate(lines + [jnp.zeros((EXTRA - len(lines), width), f32)], axis=0)
    high, low = split_low(lines)
    base = keep.shape[0] - 2 * EXTRA
    for out in (keep, send):
        out[base : base + EXTRA, :] = high
        out[base + EXTRA :, :] = low


def feed_call(own, packed, mixed_a, mixed_b, cot, vec, w_t, mine, other):
    rows, width = packed.shape
    units = 4 * width
    size = mixed_b.shape[1]
    steps = rows // size
    row_block = pl.BlockSpec((size, width), lambda i: (i, 0))
    sent = (units + 2 * EXTRA, width)
    return kernel_call(
        functools.partial(feed_body, size),
        [
            SM,
            row_block,
            pl.BlockSpec((width, size), lambda i: (0, jnp.minimum(i, steps - 2))),
            whole(mixed_b.shape),
            row_block,
            whole((8, width)),
            pl.BlockSpec((CHUNKS // 4, units // CHUNKS, width), lambda i: (3, 0, 0)),
            whole(mine.shape),
            whole(other.shape),
        ],
        (S((rows, width), bf16), S((rows, width), f32), S((rows, width), bf16), S(sent, bf16), S(sent, bf16)),
        [
            pltpu.VMEM((CHUNKS, mine.shape[0] // HALF, width), bf16),
            pltpu.VMEM((units, width), bf16),
            pltpu.VMEM((units, width), bf16),
            pltpu.VMEM((rows, units), bf16),
            pltpu.VMEM((rows, units), bf16),
            pltpu.VMEM((width, rows), bf16),
            pltpu.VMEM((width, rows), bf16),
            pltpu.VMEM((1, units), f32),
            pltpu.VMEM((32, width), f32),
            pltpu.VMEM((8, units), f32),
            pltpu.VMEM((width, size), bf16),
        ],
        grid=(steps,),
        out_specs=(row_block, row_block, row_block, whole(sent), whole(sent)),
        flops=12 * rows * width * units + 6 * rows * width * width,
        micros=30,
        name="feed",
        mib=60,
    )(own, packed, mixed_a, mixed_b, cot, vec, w_t, mine, other)


def side_body(mixed_a, mixed_b, middle_grad, out_grad):
    first = mixed_a.shape[1]
    total = dot(mixed_a[...], middle_grad[:first, :].astype(bf16))
    total += dot(mixed_b[...], middle_grad[first:, :].astype(bf16))
    out_grad[...] = total.T.astype(bf16)


def side_call(mixed_a, mixed_b, middle_grad):
    rows, width = middle_grad.shape
    return kernel_call(
        side_body,
        [VM] * 3,
        (S((width, width), bf16),),
        flops=2 * rows * width * width,
        micros=4,
        name="side",
        mib=20,
    )(mixed_a, mixed_b, middle_grad)[0]


def back_body(
    own, seg, offs, counts, qkv_in, key_in, mixed_in, stats_a, stats_b, seg_rows, seg_cols,
    w_in, packed_in, normed_in, middle_in, out_grad, vec,
    input_out, keep, send,
    qkv, key_t, mixed_grad, w_t, packed, normed_t, middle_grad, input_grad,
    qkv_grad, key_grad, value_grad, stats, sums, sems, late_sems, out_sems,
):
    rows, width = packed.shape
    me = own[0]
    piece = w_t.shape[1]
    size = 512

    def early(i):
        sl = tile_rows(i, size)
        return [
            pltpu.make_async_copy(qkv_in.at[sl, :], qkv.at[sl, :], sems.at[0, i]),
            pltpu.make_async_copy(key_in.at[:, sl], key_t.at[:, sl], sems.at[1, i]),
            pltpu.make_async_copy(mixed_in.at[sl, :], mixed_grad.at[sl, :], sems.at[2, i]),
        ]

    late = [
        pltpu.make_async_copy(source, target, late_sems.at[k])
        for k, (source, target) in enumerate(
            ((w_in, w_t), (packed_in, packed), (middle_in, middle_grad), (normed_in, normed_t))
        )
    ]
    for i in range(rows // size):
        for copy in early(i):
            copy.start()
    for copy in late:
        copy.start()

    def before(j):
        step = size // BLK

        @pl.when(j == 0)
        def _():
            for copy in early(0):
                copy.wait()

        @pl.when(((j + 2) % step == 0) & ((j + 2) // step < rows // size))
        def _():
            for copy in early((j + 2) // step):
                copy.wait()

    attend_back(
        seg, offs, counts, qkv, key_t, mixed_grad, stats_a, stats_b, seg_rows, seg_cols,
        qkv_grad, key_grad, value_grad, stats, before,
    )
    for copy in late:
        copy.wait()
    weights = w_t[: 3 * HALF // 2].reshape(3 * width, width)
    sums[...] = jnp.zeros_like(sums)

    def result(i):
        sl = tile_rows(i, size)
        return pltpu.make_async_copy(input_grad.at[sl, :], input_out.at[sl, :], out_sems.at[i])

    tiles = [slice(i * size, (i + 1) * size) for i in range(rows // size)]
    for sl in tiles:
        qkv_grad[sl, width : 2 * width] = (key_grad[sl, :] * SCALE).astype(bf16)
        qkv_grad[sl, 2 * width :] = value_grad[sl, :].astype(bf16)

    def finish(i, normed_grad):
        sl = tiles[i]
        unit, inverse = norm_parts(packed[sl, :].astype(f32))
        sums[0:8, :] += row_sums(normed_grad * unit)
        sums[8:16, :] += row_sums(normed_grad)
        sums[16:24, :] += row_sums(qkv_grad[sl, :width].astype(f32))
        sums[24:32, :] += row_sums(qkv_grad[sl, 2 * width :].astype(f32))
        input_grad[sl, :] = middle_grad[sl, :] + norm_back(unit, inverse, vec[0:1, :], normed_grad)
        result(i).start()

    def weight_part(lower, wide):
        pieces = dot(normed_t[...], qkv_grad[:, lower : lower + wide]).T.astype(bf16)
        pieces = pieces.reshape(wide // piece, piece, width)
        store_pieces(me, lower // piece, pieces, keep, send, 0, piece, plane_first)

    grads = [dot(qkv_grad[sl, :], weights) for sl in tiles]
    for i in range(len(tiles)):
        if i == 0:
            weight_part(0, 2 * width)
        if i == 2:
            weight_part(2 * width, width)
        finish(i, grads[i])
    pieces = out_grad[...].reshape(width // piece, piece, width)
    store_pieces(me, 3 * width // piece, pieces, keep, send, 0, piece, plane_first)
    lines = [jnp.sum(sums[8 * row : 8 * row + 8, :], axis=0, keepdims=True) for row in range(4)]
    store_extra(lines, keep, send)
    for i in range(rows // size):
        result(i).wait()


def back_call(
    own, seg, offs, counts, qkv, key_t, mixed_grad, stats_a, stats_b, seg_rows, seg_cols,
    w_t, packed, normed_t, middle_grad, out_grad, vec,
):
    rows, width = packed.shape
    sent = S((HALF * w_t.shape[1] + 2 * EXTRA, width), bf16)
    moved = (qkv, key_t, mixed_grad, w_t, packed, normed_t, middle_grad)
    tiles = rows // 512
    return kernel_call(
        back_body,
        [SM] * 4 + [HB] * 3 + [VM] * 4 + [HB] * 4 + [VM] * 2,
        (S((rows, width), f32), sent, sent),
        [pltpu.VMEM(v.shape, v.dtype) for v in moved]
        + [
            pltpu.VMEM((rows, width), f32),
            pltpu.VMEM((rows, 3 * width), bf16),
            pltpu.VMEM((rows, width), f32),
            pltpu.VMEM((rows, width), f32),
            pltpu.VMEM((rows // BLK, HEADS * BLK), f32),
            pltpu.VMEM((32, width), f32),
            pltpu.SemaphoreType.DMA((3, tiles)),
            pltpu.SemaphoreType.DMA((4,)),
            pltpu.SemaphoreType.DMA((tiles,)),
        ],
        flops=22 * rows * width * width,
        micros=30,
        name="back",
        mib=60,
        out_specs=(HB, VM, VM),
    )(
        own, seg, offs, counts, qkv, key_t, mixed_grad, stats_a, stats_b, seg_rows, seg_cols,
        w_t, packed, normed_t, middle_grad, out_grad, vec,
    )


def unpack_body(win, offs, keep, input_grad, image_grads, slots):
    images_here, length = keep.shape
    rows, width = input_grad.shape
    before = lax.broadcasted_iota(jnp.int32, (length, length), 0)
    after = lax.broadcasted_iota(jnp.int32, (length, length), 1)
    tri = jnp.where(before <= after, 1.0, 0.0).astype(bf16)
    place = lax.broadcasted_iota(jnp.int32, (win, length), 0)

    @pl.when(pl.program_id(0) == 0)
    def _():
        kept = keep[...]
        ranks = dot(kept.astype(f32).astype(bf16), tri).astype(jnp.int32) - 1
        slots[...] = jnp.where(kept > 0, ranks, -4 * win)

    chosen, values = [], []
    for k in range(image_grads.shape[0]):
        i = pl.program_id(0) * image_grads.shape[0] + k
        base = pl.multiple_of(jnp.minimum((offs[i] // 8) * 8, rows - win), 8)
        shift = offs[i] - base
        chosen.append(jnp.where(place == slots[pl.ds(i, 1), :] + shift, 1.0, 0.0).astype(bf16))
        values.append(input_grad[pl.ds(base, win), :])
    highs = [value.astype(bf16) for value in values]
    rests = [(value - high.astype(f32)).astype(bf16) for value, high in zip(values, highs)]
    for k in range(image_grads.shape[0]):
        image_grads[k] = dot(chosen[k], highs[k], TN) + dot(chosen[k], rests[k], TN)


def unpack_call(offs, keep, input_grad):
    images_here, length = keep.shape
    rows, width = input_grad.shape
    win = (length + 7 + 7) // 8 * 8
    size = 5
    return kernel_call(
        functools.partial(unpack_body, win),
        [SM, whole(keep.shape), whole(input_grad.shape)],
        (S((images_here, length, width), f32),),
        [pltpu.VMEM((images_here, length), jnp.int32)],
        flops=4 * images_here * win * length * width,
        micros=9,
        name="unpack",
        mib=60,
        grid=(images_here // size,),
        out_specs=(pl.BlockSpec((size, length, width), lambda i: (i, 0, 0)),),
    )(offs, keep, input_grad)[0]


def to_halves(chunks):
    _, size, width = chunks.shape
    ordered = chunks.reshape(4, 4, 2, size, width).transpose(2, 1, 0, 3, 4).reshape(2, HALF * size, width)
    return ordered[0], ordered[1]


def from_halves(keep, send, parts, width, line_first):
    size = keep.shape[0] // HALF // parts
    both = jnp.stack([keep, send]).reshape(2, 4, 4, parts, size, width)
    both = both.transpose((1, 2, 0, 3, 4, 5) if line_first else (2, 1, 0, 3, 4, 5))
    return both.reshape(CHUNKS, parts, size, width)


def adamw(weight, grad, first, second, average, count, rate, decay):
    first_new = BETA_ONE * first + (1.0 - BETA_ONE) * grad
    second_new = BETA_TWO * second + (1.0 - BETA_TWO) * grad * grad
    first_hat = first_new / (1.0 - jnp.power(BETA_ONE, count))
    second_hat = second_new / (1.0 - jnp.power(BETA_TWO, count))
    weight_new = weight - rate * (first_hat / (jnp.sqrt(second_hat) + ADAM_EPS) + decay * weight)
    average_new = AVERAGE_DECAY * average + (1.0 - AVERAGE_DECAY) * weight_new
    return (weight_new, first_new, second_new, average_new)


def wide_of(ref, rows):
    return ref[rows, :].astype(f32)


def whole_extra(ref):
    return wide_of(ref, slice(-2 * EXTRA, -EXTRA)) + wide_of(ref, slice(-EXTRA, None))


def paired(values):
    while len(values) > 1:
        values = [values[i] + values[i + 1] for i in range(0, len(values), 2)]
    return values[0]


def put_extra(values, out, pieces):
    high, low = split_low(values)
    out[-EXTRA:, :] = high.astype(f32) + low.astype(f32)
    for piece in pieces:
        piece[-2 * EXTRA : -EXTRA, :] = high
        piece[-EXTRA:, :] = low


def merge_first_body(ffn_own, ffn_a, ffn_b, ffn_c, attn_own, attn_in, own, *pieces):
    ffn_size, attn_size = (ffn_own.shape[0] - EXTRA) // 4, (attn_own.shape[0] - 2 * EXTRA) // 4
    for part in range(4):
        rows = slice(part * ffn_size, (part + 1) * ffn_size)
        ffn = ffn_own[rows, :] + wide_of(ffn_a, rows) + wide_of(ffn_b, rows) + wide_of(ffn_c, rows)
        rows = slice(part * attn_size, (part + 1) * attn_size)
        attn = wide_of(attn_own, rows) + wide_of(attn_in, rows)
        out = own if part == 0 else pieces[part - 1]
        out[:ffn_size, :] = ffn.astype(out.dtype)
        out[ffn_size : ffn_size + attn_size, :] = attn.astype(out.dtype)
    known = paired([ffn_own[-EXTRA:, :]] + [whole_extra(r) for r in (ffn_a, ffn_b, ffn_c)])
    fresh = whole_extra(attn_own) + whole_extra(attn_in)
    put_extra(jnp.concatenate([fresh[:4], known[:8], fresh[12:]], axis=0), own, pieces)


def merge_first_call(ffn_own, ffn_in, attn_own, attn_in):
    width = ffn_own.shape[1]
    size = (ffn_own.shape[0] - EXTRA) // 4 + (attn_own.shape[0] - 2 * EXTRA) // 4
    out = kernel_call(
        merge_first_body,
        [VM] * 6,
        (S((size + EXTRA, width), f32),) + (S((size + 2 * EXTRA, width), bf16),) * 3,
        micros=3,
        name="merge_first",
    )(ffn_own, *ffn_in, attn_own, attn_in)
    return out[0], out[1:]


def merge_second_body(skip, own, in_a, in_b, in_c, out, *pieces):
    received = (in_a, in_b, in_c)
    size = out.shape[0] - EXTRA
    for part in range(4):
        rows = slice(skip + part * size, skip + (part + 1) * size)
        total = own[rows, :] + wide_of(in_a, rows) + wide_of(in_b, rows) + wide_of(in_c, rows)
        to = out if part == 0 else pieces[part - 1]
        to[:size, :] = total.astype(to.dtype)
    put_extra(paired([own[-EXTRA:, :]] + [whole_extra(r) for r in received]), out, pieces)


def merge_second_call(skip, own, received):
    width = own.shape[1]
    size = (own.shape[0] - EXTRA - skip) // 4
    out = kernel_call(
        functools.partial(merge_second_body, skip),
        [VM] * 4,
        (S((size + EXTRA, width), f32),) + (S((size + 2 * EXTRA, width), bf16),) * 3,
        micros=2,
        name="merge_second",
    )(own, *received)
    return out[0], out[1:]


def adamw_with(weight, grad, first, second, average, one, two, rate, decay):
    first_new = BETA_ONE * first + (1.0 - BETA_ONE) * grad
    second_new = BETA_TWO * second + (1.0 - BETA_TWO) * grad * grad
    weight_new = weight - rate * ((first_new / one) / (jnp.sqrt(second_new / two) + ADAM_EPS) + decay * weight)
    average_new = AVERAGE_DECAY * average + (1.0 - AVERAGE_DECAY) * weight_new
    return (weight_new, first_new, second_new, average_new)


def update(powers, states, grad, rate, decay, grad_out, outs, at=slice(None)):
    held = [ref[at] for ref in states]
    grad_out[at] = grad
    for ref, value in zip(outs, adamw_with(held[0], grad, *held[1:], powers[0], powers[1], rate, decay)):
        ref[at] = value


def finish_ffn_body(me, powers, own, in_a, in_b, in_c, *refs):
    states, outs = refs[:8], refs[8:]
    _, piece, width = states[0].shape
    received = (in_a, in_b, in_c)
    for k in range(2):
        rows = slice(k * piece, (k + 1) * piece)
        grad = own[rows, :] + wide_of(in_a, rows) + wide_of(in_b, rows) + wide_of(in_c, rows)
        update(powers, states[:4], grad, MATRIX_RATE, WEIGHT_DECAY, outs[0], outs[2:6], k)
    sums = paired([own[-EXTRA:, :]] + [whole_extra(r) for r in received])
    across = width // piece
    row = lax.broadcasted_iota(jnp.int32, (EXTRA, width), 0)
    line = jnp.sum(jnp.where(row == 8 + me[0] // across, sums, 0.0), axis=0, keepdims=True)
    line = jnp.broadcast_to(line, (8, width))
    shift = (me[0] % across) * piece
    line = jnp.where(shift == 0, line, pltpu.roll(line, width - shift, 1))
    update(powers, states[4:], line[:1, :piece], VECTOR_RATE, 0.0, outs[1], outs[6:])


def finish_ffn_call(me, powers, own, received, states):
    kinds = [S(states[k].shape, f32) for k in (0, 4)]
    out = kernel_call(
        finish_ffn_body,
        [SM, SM] + [VM] * 12,
        tuple(kinds) + tuple(kind for kind in kinds for _ in range(4)),
        micros=2,
        name="finish_ffn",
    )(me, powers, own, *received, *states)
    return out[0], out[1], out[2:6], out[6:]


def finish_attn_body(powers, own, in_a, in_b, in_c, *refs):
    states, outs = refs[:8], refs[8:]
    piece = states[0].shape[0]
    rows = slice(0, piece)
    grad = own[rows, :] + wide_of(in_a, rows) + wide_of(in_b, rows) + wide_of(in_c, rows)
    update(powers, states[:4], grad, MATRIX_RATE, WEIGHT_DECAY, outs[0], outs[2:6])
    sums = paired([own[-EXTRA:, :]] + [whole_extra(r) for r in (in_a, in_b, in_c)])
    vec = jnp.concatenate([sums[:4], own[-EXTRA + 4 : -EXTRA + 8, :]], axis=0)
    update(powers, states[4:], vec, VECTOR_RATE, 0.0, outs[1], outs[6:])


def finish_attn_call(powers, own, received, states):
    kinds = [S(states[k].shape, f32) for k in (0, 4)]
    out = kernel_call(
        finish_attn_body,
        [SM] + [VM] * 12,
        tuple(kinds) + tuple(kind for kind in kinds for _ in range(4)),
        micros=2,
        name="finish_attn",
    )(powers, own, *received, *states)
    return out[0], out[1], out[2:6], out[6:]


def body(
    images, keep_mask, kept_counts, pack_offsets, segment_ids, cotangent,
    attn_weight, ffn_weight, up_bias, vectors,
    attn_first, ffn_first, bias_first, vec_first,
    attn_second, ffn_second, bias_second, vec_second,
    attn_average, ffn_average, bias_average, vec_average, step,
):
    width = images.shape[2]
    rows = segment_ids.shape[0]
    both = ("dp", "mp")
    piece = attn_weight.shape[1]
    tree = lax.axis_size("dp") == 8 and lax.axis_size("mp") == 4
    seg_rows = segment_ids.reshape(rows // BLK, BLK)
    placed = place_call(images, keep_mask, pack_offsets, rows)
    count = step[0].astype(f32)
    powers = jnp.stack([1.0 - jnp.power(BETA_ONE, count), 1.0 - jnp.power(BETA_TWO, count)])
    if tree:
        own = (lax.axis_index("dp") * 4 + lax.axis_index("mp")).astype(jnp.int32)[None]
        pieces = pieces_call(attn_weight.T, jnp.swapaxes(ffn_weight, 1, 2), up_bias[None, :])
        lines = [pieces] + [over_line(pieces, k) for k in (1, 2, 3)]
        placed, *lines = tie(placed, *lines)
        attn_line = jnp.concatenate([line[:piece] for line in lines], axis=0)
        ffn_line = jnp.concatenate([line[piece:] for line in lines], axis=0)
        attn_mine = gather_plane(attn_line)
        normed, normed_t, seg_cols = norm_call(placed, seg_rows, vectors)
        attn_mine, normed, ffn_line = tie(attn_mine, normed, ffn_line)
        attn_other = over_core(attn_mine)
        ffn_lines = [ffn_line] + [over_plane(ffn_line, k) for k in (1, 2, 3)]
    else:
        own = jnp.zeros((1,), jnp.int32)
        attn_all = lax.all_gather(attn_weight.astype(bf16).T, both, axis=0, tiled=True)
        ffn_all = lax.all_gather(jnp.swapaxes(ffn_weight.astype(bf16), 1, 2), both, axis=1, tiled=True)
        bias_all = lax.all_gather(up_bias.astype(bf16), both, axis=0, tiled=True)
        size = 4 * width // CHUNKS
        ffn_all = jnp.concatenate(
            [
                ffn_all[0].reshape(CHUNKS, size, width),
                ffn_all[1].reshape(CHUNKS, size, width),
                jnp.pad(bias_all.reshape(CHUNKS, 1, size), ((0, 0), (0, 15), (0, width - size))),
            ],
            axis=1,
        )
        attn_mine, attn_other = to_halves(attn_all.reshape(CHUNKS, size, width))
        ffn_mine, ffn_other = to_halves(ffn_all)
        normed, normed_t, seg_cols = norm_call(placed, seg_rows, vectors)
    where = (segment_ids, pack_offsets, kept_counts)
    blocks = rows // BLK
    late = blocks // 4
    qkv, key_t, value_t, w_t, mixed_a, stats_a = attend_first_call(
        blocks - late, own, *where, normed, attn_mine, attn_other, vectors, seg_rows, seg_cols
    )
    if tree:
        qkv, mixed_a, *ffn_lines = tie(qkv, mixed_a, *ffn_lines)
        ffn_mine = jnp.concatenate(ffn_lines, axis=0)
        ffn_other = over_core(ffn_mine)
    mixed_b, stats_b = attend_last_call(late, *where, qkv, value_t, seg_rows, seg_cols)
    if tree:
        mixed_b, ffn_mine, ffn_other = tie(mixed_b, ffn_mine, ffn_other)
    layer_out, middle_grad, mixed_grad, ffn_keep, ffn_send = feed_call(
        own, placed, mixed_a, mixed_b, cotangent, vectors, w_t, ffn_mine, ffn_other
    )
    if tree:
        ffn_in = over_core(ffn_send)
    out_grad = side_call(mixed_a, mixed_b, middle_grad)
    if tree:
        out_grad, ffn_in = tie(out_grad, ffn_in)
        ffn_own, *ffn_out = combine_call(ffn_keep, [ffn_in], 4, EXTRA)
        out_grad, ffn_own, *ffn_out = tie(out_grad, ffn_own, *ffn_out)
        ffn_in = [over_line(p, k + 1) for k, p in enumerate(ffn_out)]
    input_grad, attn_keep, attn_send = back_call(
        own, *where, qkv, key_t, mixed_grad, stats_a, stats_b, seg_rows, seg_cols,
        w_t, placed, normed_t, middle_grad, out_grad, vectors,
    )
    index = lax.axis_index("dp") * lax.axis_size("mp") + lax.axis_index("mp")
    if tree:
        input_grad, attn_send, *ffn_in = tie(input_grad, attn_send, *ffn_in)
        attn_in = over_core(attn_send)
        states = [v.T for v in (attn_weight, attn_first, attn_second, attn_average)]
        states += [vectors, vec_first, vec_second, vec_average]
        ffn_states = [jnp.swapaxes(v, 1, 2) for v in (ffn_weight, ffn_first, ffn_second, ffn_average)]
        ffn_states += [v[None, :] for v in (up_bias, bias_first, bias_second, bias_average)]
        merged, pieces = merge_first_call(ffn_own, ffn_in, attn_keep, attn_in)
        input_grad, *pieces = tie(input_grad, *pieces)
        received = [over_plane(p, k + 1) for k, p in enumerate(pieces)]
        image_grads = unpack_call(pack_offsets, keep_mask, input_grad)
        image_grads, *received = tie(image_grads, *received)
        attn_own, pieces = merge_second_call(2 * piece, merged, received)
        image_grads, merged, *pieces = tie(image_grads, merged, *pieces)
        last = [over_line(p, k + 1) for k, p in enumerate(pieces)]
        ffn_grad, bias_grad, ffn_up, bias_up = finish_ffn_call(own, powers, merged, received, ffn_states)
        image_grads, ffn_grad, *last = tie(image_grads, ffn_grad, *last)
        attn_grad, vec_grad, attn_up, vec_up = finish_attn_call(powers, attn_own, last, states)
        attn_grad, ffn_grad, bias_grad = attn_grad.T, jnp.swapaxes(ffn_grad, 1, 2), bias_grad[0]
        attn_up, ffn_up = [v.T for v in attn_up], [jnp.swapaxes(v, 1, 2) for v in ffn_up]
        bias_up = [v[0] for v in bias_up]
    else:
        image_grads = unpack_call(pack_offsets, keep_mask, input_grad)
        base = ffn_keep.shape[0] - 2 * EXTRA
        ffn_t = from_halves(ffn_keep[:base], ffn_send[:base], 2, width, True)
        ffn_t = jnp.swapaxes(ffn_t, 0, 1).reshape(2, 4 * width, width)
        ffn_t = lax.psum_scatter(ffn_t.astype(f32), both, scatter_dimension=1, tiled=True)
        ffn_grad = jnp.swapaxes(ffn_t, 1, 2)
        known = ffn_keep[base : base + EXTRA].astype(f32) + ffn_keep[base + EXTRA :].astype(f32)
        base = attn_keep.shape[0] - 2 * EXTRA
        attn_t = from_halves(attn_keep[:base], attn_send[:base], 1, width, False).reshape(4 * width, width)
        attn_grad = lax.psum_scatter(attn_t.astype(f32), both, scatter_dimension=0, tiled=True).T
        sums = attn_keep[base : base + EXTRA].astype(f32) + attn_keep[base + EXTRA :].astype(f32)
        sums = lax.psum(jnp.concatenate([sums[:4], known[:8]], axis=0), both)
        vec_grad, bias_sums = sums[:8], sums[8:]
        bias_grad = lax.dynamic_slice_in_dim(bias_sums.reshape(4 * width), index * piece, piece, 0)
        attn_up = adamw(attn_weight, attn_grad, attn_first, attn_second, attn_average, count, MATRIX_RATE, WEIGHT_DECAY)
        vec_up = adamw(vectors, vec_grad, vec_first, vec_second, vec_average, count, VECTOR_RATE, 0.0)
        ffn_up = adamw(ffn_weight, ffn_grad, ffn_first, ffn_second, ffn_average, count, MATRIX_RATE, WEIGHT_DECAY)
        bias_up = adamw(up_bias, bias_grad, bias_first, bias_second, bias_average, count, VECTOR_RATE, 0.0)
    news = [part[k] for k in range(4) for part in (attn_up, ffn_up, bias_up, vec_up)]
    return (layer_out, image_grads, attn_grad, ffn_grad, bias_grad, vec_grad, *news)


def solution(mesh):
    both = ("dp", "mp")
    matrix, slab, line = P(None, both), P(None, None, both), P(both)
    states = (matrix, slab, line, P())
    return jax.shard_map(
        body,
        mesh=mesh,
        in_specs=(P(both, None, None), P(both, None), line, line, line, P(both, None), *states * 4, P()),
        out_specs=(P(both, None), P(both, None, None), *states, *states * 4),
        check_vma=False,
    )
```

```python
import functools
import math

import jax
import jax.numpy as jnp
from jax import lax
from jax.experimental import pallas as pl
from jax.experimental.pallas import tpu as pltpu
from jax.sharding import PartitionSpec as P

HEADS = 6
HEAD = 64
PAIR = 2 * HEAD
PAIRS = HEADS // 2
BLK = 128
REACH = 5
CHUNKS = 32
HALF = CHUNKS // 2
EXTRA = 16
EXCLUDED = -8.0e9
INCLUDED = 3.0e38

NORM_EPS = 1e-06
BETA_ONE = 0.9
BETA_TWO = 0.999
ADAM_EPS = 1e-08
MATRIX_RATE = 0.05
VECTOR_RATE = 0.2
WEIGHT_DECAY = 0.05
AVERAGE_DECAY = 0.8

LOG2E = 1.4426950408889634
SCORE_LOG2 = LOG2E / math.sqrt(HEAD)
SCALE = 1.0 / math.sqrt(HEAD)

f32 = jnp.float32
bf16 = jnp.bfloat16
NN = (((1,), (0,)), ((), ()))
NT = (((1,), (1,)), ((), ()))
TN = (((0,), (0,)), ((), ()))
VM = pl.BlockSpec(memory_space=pltpu.VMEM)
SM = pl.BlockSpec(memory_space=pltpu.SMEM)
HB = pl.BlockSpec(memory_space=pl.ANY)
S = jax.ShapeDtypeStruct


def dot(left, right, dims=NN):
    return lax.dot_general(left, right, dims, preferred_element_type=f32)


def kernel_call(body, ins, outs, scratch=(), flops=0, micros=1, name=None, grid=(), out_specs=None, mib=16):
    return pl.pallas_call(
        body,
        grid=grid,
        out_shape=outs,
        in_specs=ins,
        out_specs=out_specs or tuple(VM for _ in outs),
        scratch_shapes=list(scratch),
        compiler_params=pltpu.CompilerParams(vmem_limit_bytes=mib * 2**20),
        cost_estimate=pl.CostEstimate(flops=flops, bytes_accessed=micros * 3_500_000, transcendentals=0),
        name=name,
    )


def whole(shape):
    return pl.BlockSpec(shape, lambda i: (0,) * len(shape))


def row_sums(values):
    rows, width = values.shape
    return jnp.sum(values.reshape(rows // 8, 8, width), axis=0)


def norm_parts(values):
    scale = 1.0 / values.shape[-1]
    centre = jnp.sum(values, axis=-1, keepdims=True) * scale
    centred = values - centre
    spread = jnp.sum(centred * centred, axis=-1, keepdims=True) * scale
    inverse = lax.rsqrt(spread + NORM_EPS)
    return centred * inverse, inverse


def norm_back(unit, inverse, gain, grad):
    scale = 1.0 / unit.shape[-1]
    scaled = grad * gain
    mean = jnp.sum(scaled, axis=-1, keepdims=True) * scale
    along = jnp.sum(scaled * unit, axis=-1, keepdims=True) * scale
    return inverse * (scaled - mean - unit * along)


def tile_rows(count, size):
    return pl.ds(pl.multiple_of(count * size, size), size)


def plane_first(apart):
    return (apart & 3) * 4 + lax.shift_right_logical(apart, 2)


def line_first(apart):
    return apart


def spread_pieces(own, halves, out):
    for near in range(2):
        for slot in range(HALF):
            apart = near + 2 * ((slot // 4) + 4 * (slot % 4))
            out[own ^ apart] = halves[near][slot * out.shape[1] : (slot + 1) * out.shape[1], :]


def store_pieces(own, start, pieces, keep, send, at, step, order):
    count, size, _ = pieces.shape
    odd = (own & 1) == 1
    for e in range(0, count, 2):
        apart = lax.shift_right_logical(own, 1) ^ ((start + e) // 2)
        row = pl.multiple_of(order(apart) * step + at, 16)
        even_piece, odd_piece = pieces[e], pieces[e + 1]
        keep[pl.ds(row, size), :] = jnp.where(odd, odd_piece, even_piece)
        send[pl.ds(row, size), :] = jnp.where(odd, even_piece, odd_piece)


def split_low(values):
    high = values.astype(bf16)
    return high, (values - high.astype(f32)).astype(bf16)


def combine_body(parts, size, extra, count, *refs):
    own, received, outs = refs[0], refs[1 : 1 + count], refs[1 + count :]
    base = parts * size
    for part in range(parts):
        rows = slice(part * size, (part + 1) * size)
        total = own[rows, :].astype(f32)
        for other in received:
            total = total + other[rows, :].astype(f32)
        if part == 0:
            outs[0][:size, :] = total
        else:
            outs[part][:size, :] = total.astype(bf16)
    if extra:
        if own.dtype == bf16:
            sums = [own[base : base + extra, :].astype(f32) + own[base + extra :, :].astype(f32)]
        else:
            sums = [own[base:, :]]
        sums += [r[base : base + extra, :].astype(f32) + r[base + extra :, :].astype(f32) for r in received]
        while len(sums) > 1:
            sums = [sums[i] + sums[i + 1] for i in range(0, len(sums), 2)]
        high, low = split_low(sums[0])
        outs[0][size:, :] = high.astype(f32) + low.astype(f32) if parts > 1 else sums[0]
        for out in outs[1:]:
            out[size : size + extra, :] = high
            out[size + extra :, :] = low


def combine_call(own, received, parts, extra):
    size = (received[0].shape[0] - 2 * extra) // parts
    width = own.shape[1]
    outs = (S((size + extra, width), f32),) + (S((size + 2 * extra, width), bf16),) * (parts - 1)
    return kernel_call(
        functools.partial(combine_body, parts, size, extra, len(received)),
        [VM] * (1 + len(received)),
        outs,
        flops=own.size * len(received),
        micros=2,
        name="combine",
    )(own, *received)


def pieces_body(attn, ffn, bias, out, line):
    piece, width = attn.shape
    line[...] = jnp.zeros_like(line)
    line[0:1, :piece] = bias[...]
    out[:piece, :] = attn[...].astype(bf16)
    for k in range(2):
        out[(1 + k) * piece : (2 + k) * piece, :] = ffn[k].astype(bf16)
    out[3 * piece :, :] = line[...].astype(bf16)


def pieces_call(attn, ffn, bias):
    piece, width = attn.shape
    return kernel_call(
        pieces_body,
        [VM] * 3,
        (S((3 * piece + 16, width), bf16),),
        [pltpu.VMEM((16, width), f32)],
        name="pieces",
        mib=60,
    )(attn, ffn, bias)[0]


def over_core(values):
    return lax.ppermute(values, "mp", [(i, i ^ 1) for i in range(lax.axis_size("mp"))])


def over_plane(values, apart):
    devices = lax.axis_size("dp") * lax.axis_size("mp")
    return lax.ppermute(values, ("dp", "mp"), [(i, i ^ (2 * apart)) for i in range(devices)])


def over_line(values, apart):
    return lax.ppermute(values, "dp", [(i, i ^ (2 * apart)) for i in range(lax.axis_size("dp"))])


def tie(*values):
    return lax.optimization_barrier(values)


def gather_plane(pieces):
    return jnp.concatenate([pieces] + [over_plane(pieces, k) for k in (1, 2, 3)], axis=0)


def place_body(win, offs, images, keep, packed, acc, slots):
    images_here, length = keep.shape
    rows, width = packed.shape
    size = images.shape[0]
    step = pl.program_id(0)

    @pl.when(step == 0)
    def _():
        before = lax.broadcasted_iota(jnp.int32, (length, length), 0)
        after = lax.broadcasted_iota(jnp.int32, (length, length), 1)
        tri = jnp.where(before <= after, 1.0, 0.0).astype(bf16)
        kept = keep[...]
        ranks = dot(kept.astype(f32).astype(bf16), tri).astype(jnp.int32) - 1
        slots[...] = jnp.where(kept > 0, ranks, -4 * win)
        acc[0:8, :] = jnp.zeros((8, width), f32)

    place = lax.broadcasted_iota(jnp.int32, (win, length), 0)
    starts = [offs[step * size + k] for k in range(size)]
    bases = [pl.multiple_of((start // 8) * 8, 8) for start in starts]
    lines = [slots[pl.ds(step * size + k, 1), :] + (starts[k] - bases[k]) for k in range(size)]
    chosen = [jnp.where(place == line, 1.0, 0.0).astype(bf16) for line in lines]
    moved = [dot(chosen[k], images[k]) for k in range(size)]
    for base, part in zip(bases, moved):
        acc[pl.ds(base, 8), :] += part[0:8]
        acc[pl.ds(base + 8, win - 8), :] = part[8:]

    @pl.when(step == pl.num_programs(0) - 1)
    def _():
        packed[...] = acc[:rows, :].astype(bf16)


def place_call(images, keep, offs, rows):
    images_here, length, width = images.shape
    win = (length + 7 + 7) // 8 * 8
    size = 5
    return kernel_call(
        functools.partial(place_body, win),
        [SM, pl.BlockSpec((size, length, width), lambda i: (i, 0, 0)), whole(keep.shape)],
        (S((rows, width), bf16),),
        [pltpu.VMEM((rows + win, width), f32), pltpu.VMEM((images_here, length), jnp.int32)],
        flops=2 * images_here * win * length * width,
        micros=6,
        name="place",
        mib=60,
        grid=(images_here // size,),
        out_specs=(whole((rows, width)),),
    )(offs, images, keep)[0]


def norm_body(packed, seg_rows, vec, normed, normed_t, seg_cols):
    rows, width = packed.shape
    step = pl.program_id(0)
    sub = 128
    parts = [slice(k * sub, (k + 1) * sub) for k in range(rows // sub)]
    units = [norm_parts(packed[at, :].astype(f32))[0] for at in parts]
    lows = [(unit * vec[0:1, :] + vec[1:2, :]).astype(bf16) for unit in units]
    for at, low in zip(parts, lows):
        normed[at, :] = low
    for at, low in zip(parts, lows):
        normed_t[:, at] = low.T
    for k in range(rows // BLK):
        line = seg_rows[pl.ds(step * (rows // BLK) + k, 1), :]
        seg_cols[k * BLK : (k + 1) * BLK, :] = jnp.broadcast_to(line, (BLK, BLK)).T


def norm_call(packed, seg_rows, vec):
    rows, width = packed.shape
    size = 512
    return kernel_call(
        norm_body,
        [pl.BlockSpec((size, width), lambda i: (i, 0)), whole(seg_rows.shape), whole(vec.shape)],
        (S((rows, width), bf16), S((width, rows), bf16), S((rows, BLK), jnp.int32)),
        flops=rows * width * 12,
        micros=5,
        name="norm",
        mib=60,
        grid=(rows // size,),
        out_specs=(
            pl.BlockSpec((size, width), lambda i: (i, 0)),
            pl.BlockSpec((width, size), lambda i: (0, i)),
            pl.BlockSpec((size, BLK), lambda i: (i, 0)),
        ),
    )(packed, seg_rows, vec)


def window(seg, offs, counts, j, images_here, tiles, step):
    first = seg[j * BLK]
    last = seg[j * BLK + BLK - 1]
    used = last < images_here
    last_here = jnp.where(used, last, 0)
    end = jnp.where(used, offs[last_here] + counts[last_here], tiles * BLK)
    low = jnp.minimum(offs[first] // BLK, tiles - 2)
    return low, jnp.maximum((end + step - 1) // step - low * (BLK // step), 2 * BLK // step)


def masked_pair(pair):
    lane = lax.broadcasted_iota(jnp.int32, pair.shape, 1)
    none = jnp.zeros_like(pair)
    return jnp.concatenate([jnp.where(lane < HEAD, pair, none), jnp.where(lane >= HEAD, pair, none)], axis=0)


def limits(seg_rows, seg_cols, j, keys):
    same = seg_cols[keys, :] == seg_rows[pl.ds(j, 1), :]
    lim = jnp.where(same, INCLUDED, EXCLUDED)
    return jnp.concatenate([lim, lim], axis=1)


def over_windows(seg, offs, counts, tiles, base, first, blocks, block, step=BLK, before=None):
    def one(j, carry):
        if before is not None:
            before(j)
        low, size = window(seg, offs, counts, j, offs.shape[0], tiles, step)
        for n in range(2 * BLK // step, REACH * BLK // step + 1):

            @pl.when(size == n)
            def _():
                block(j, pl.ds(pl.multiple_of((low - base) * BLK, BLK), n * step))

        return carry

    lax.fori_loop(first, first + blocks, one, 0)


def attend_blocks(base, first, blocks, seg, offs, counts, qkv, value_t, seg_rows, seg_cols, mixed_t, stats):
    width = value_t.shape[0]
    tiles = seg.shape[0] // BLK

    def block(j, keys):
        here = tile_rows(j - base, BLK)
        there = tile_rows(j - first, BLK)
        lim = limits(seg_rows, seg_cols, j, keys)
        ats = [slice(p * PAIR, (p + 1) * PAIR) for p in range(PAIRS)]
        raws = [
            dot(qkv[keys, width + p * PAIR : width + (p + 1) * PAIR], masked_pair(qkv[here, ats[p]]), NT)
            for p in range(PAIRS)
        ]
        raws = [jnp.minimum(raw, lim) for raw in raws]
        tops = [jnp.max(raw, axis=0, keepdims=True) for raw in raws]
        expos = [jnp.exp2((raw - top) * SCORE_LOG2) for raw, top in zip(raws, tops)]
        totals = [jnp.sum(expo, axis=0, keepdims=True) for expo in expos]
        lows = [(expo * (1.0 / total)).astype(bf16) for expo, total in zip(expos, totals)]
        outs = [dot(value_t[at, keys], low) for at, low in zip(ats, lows)]
        for p in range(PAIRS):
            out = outs[p]
            mixed_t[p * PAIR : p * PAIR + HEAD, there] = out[:HEAD, :BLK].astype(bf16)
            mixed_t[p * PAIR + HEAD : (p + 1) * PAIR, there] = out[HEAD:, BLK:].astype(bf16)
            level = tops[p] * SCORE_LOG2 + jnp.log2(totals[p])
            stats[pl.ds(j - first, 1), p * 2 * BLK : (p + 1) * 2 * BLK] = level

    over_windows(seg, offs, counts, tiles, base, first, blocks, block)


def attend_first_body(
    own, seg, offs, counts, normed_in, mine, other, vec, seg_rows, cols_in,
    qkv_out, key_out, value_out, w_out, mixed_t, stats,
    qkv, key_t, value_t, w_t, normed, seg_cols, sems, in_sems,
):
    rows, width = normed.shape
    size = 512

    def reads(i):
        sl = tile_rows(i, size)
        return pltpu.make_async_copy(normed_in.at[sl, :], normed.at[sl, :], in_sems.at[i])

    cols = pltpu.make_async_copy(cols_in, seg_cols, in_sems.at[rows // size])
    for i in range(rows // size):
        reads(i).start()
    cols.start()
    spread_pieces(own[0], (mine, other), w_t)
    units = w_t.shape[0] * w_t.shape[1]
    weights = w_t[...].reshape(units, width)[: 3 * width]
    bias = jnp.concatenate([vec[2:3, :], jnp.zeros((1, width), f32), vec[3:4, :]], axis=1)
    last = pltpu.make_async_copy(w_t, w_out, sems.at[3, 0])
    last.start()

    def copies(i):
        sl = tile_rows(i, size)
        return [
            pltpu.make_async_copy(qkv.at[sl, :], qkv_out.at[sl, :], sems.at[0, i]),
            pltpu.make_async_copy(key_t.at[:, sl], key_out.at[:, sl], sems.at[1, i]),
            pltpu.make_async_copy(value_t.at[:, sl], value_out.at[:, sl], sems.at[2, i]),
        ]

    def project(i, carry):
        sl = tile_rows(i, size)
        reads(i).wait()
        low = (dot(normed[sl, :], weights, NT) + bias).astype(bf16)
        qkv[sl, :] = low
        key_t[:, sl] = low[:, width : 2 * width].T
        value_t[:, sl] = low[:, 2 * width :].T
        for copy in copies(i):
            copy.start()
        return carry

    lax.fori_loop(0, rows // size, project, 0)
    cols.wait()
    attend_blocks(
        0, 0, mixed_t.shape[1] // BLK, seg, offs, counts, qkv, value_t, seg_rows, seg_cols, mixed_t, stats
    )
    for i in range(rows // size):
        for copy in copies(i):
            copy.wait()
    last.wait()


def attend_first_call(blocks, own, seg, offs, counts, normed, mine, other, vec, seg_rows, seg_cols):
    rows, width = normed.shape
    piece = mine.shape[0] // HALF
    kept = ((rows, 3 * width), (width, rows), (width, rows), (CHUNKS, piece, width))
    return kernel_call(
        attend_first_body,
        [SM, SM, SM, SM, HB, VM, VM, VM, VM, HB],
        tuple(S(shape, bf16) for shape in kept)
        + (S((width, blocks * BLK), bf16), S((blocks, HEADS * BLK), f32)),
        [pltpu.VMEM(shape, bf16) for shape in kept]
        + [
            pltpu.VMEM(normed.shape, bf16),
            pltpu.VMEM(seg_cols.shape, jnp.int32),
            pltpu.SemaphoreType.DMA((4, rows // 512)),
            pltpu.SemaphoreType.DMA((rows // 512 + 1,)),
        ],
        flops=2 * rows * width * 3 * width,
        micros=20,
        name="attend_first",
        mib=60,
        out_specs=(HB, HB, HB, HB, VM, VM),
    )(own, seg, offs, counts, normed, mine, other, vec, seg_rows, seg_cols)


def attend_last_call(blocks, seg, offs, counts, qkv, value_t, seg_rows, seg_cols):
    width, rows = value_t.shape
    part = (blocks + REACH - 1) * BLK
    while rows % part:
        part += BLK
    at = rows // part - 1
    tiles = rows // BLK
    return kernel_call(
        functools.partial(attend_blocks, tiles - part // BLK, tiles - blocks, blocks),
        [
            SM,
            SM,
            SM,
            pl.BlockSpec((part, 3 * width), lambda i: (at, 0)),
            pl.BlockSpec((width, part), lambda i: (0, at)),
            whole(seg_rows.shape),
            pl.BlockSpec((part, BLK), lambda i: (at, 0)),
        ],
        (S((width, blocks * BLK), bf16), S((blocks, HEADS * BLK), f32)),
        grid=(1,),
        out_specs=(whole((width, blocks * BLK)), whole((blocks, HEADS * BLK))),
        flops=4 * blocks * BLK * 512 * width,
        micros=5,
        name="attend_last",
        mib=60,
    )(seg, offs, counts, qkv, value_t, seg_rows, seg_cols)


def attend_back(
    seg, offs, counts, qkv, key_t, mixed_grad, stats_a, stats_b, seg_rows, seg_cols, qkv_grad, key_grad, value_grad, stats, before
):
    rows, width = mixed_grad.shape
    key_grad[...] = jnp.zeros_like(key_grad)
    value_grad[...] = jnp.zeros_like(value_grad)
    stats[: stats_a.shape[0], :] = stats_a[...]
    stats[stats_a.shape[0] :, :] = stats_b[...]

    def block(j, keys):
        here = tile_rows(j, BLK)
        lim = limits(seg_rows, seg_cols, j, keys)
        ats = [slice(p * PAIR, (p + 1) * PAIR) for p in range(PAIRS)]
        levels = stats[pl.ds(j, 1), :]
        levels = [levels[:, p * 2 * BLK : (p + 1) * 2 * BLK] for p in range(PAIRS)]
        queries = [masked_pair(qkv[here, at]) for at in ats]
        outs = [masked_pair(mixed_grad[here, at]) for at in ats]
        raws = [
            dot(qkv[keys, width + p * PAIR : width + (p + 1) * PAIR], queries[p], NT) for p in range(PAIRS)
        ]
        grads = [
            dot(qkv[keys, 2 * width + p * PAIR : 2 * width + (p + 1) * PAIR], outs[p], NT) for p in range(PAIRS)
        ]
        probs = [jnp.exp2(jnp.minimum(raw, lim) * SCORE_LOG2 - level) for raw, level in zip(raws, levels)]
        inners = [jnp.sum(prob * grad, axis=0, keepdims=True) for prob, grad in zip(probs, grads)]
        lows = [prob.astype(bf16) for prob in probs]
        score_grads = [
            (prob * (grad - inner)).astype(bf16) for prob, grad, inner in zip(probs, grads, inners)
        ]
        for p in range(PAIRS):
            value_grad[keys, ats[p]] += dot(lows[p], outs[p])
        for p in range(PAIRS):
            key_grad[keys, ats[p]] += dot(score_grads[p], queries[p])
        for p in range(PAIRS):
            query_t = dot(key_t[ats[p], keys], score_grads[p]) * SCALE
            joined = jnp.concatenate([query_t[:HEAD, :BLK], query_t[HEAD:, BLK:]], axis=0)
            qkv_grad[here, ats[p]] = joined.T.astype(bf16)

    over_windows(seg, offs, counts, rows // BLK, 0, 0, rows // BLK, block, BLK // 2, before)


def bias_line(rows_of, units):
    chunks, size = rows_of.shape
    column = lax.broadcasted_iota(jnp.int32, (size, units), 1)
    within = lax.broadcasted_iota(jnp.int32, (size, units), 0)
    repeat = jnp.where(column % size == within, 1.0, 0.0).astype(bf16)
    wide = dot(rows_of, repeat)
    owner = lax.broadcasted_iota(jnp.int32, (chunks, units), 1) // size
    mine = owner == lax.broadcasted_iota(jnp.int32, (chunks, units), 0)
    return jnp.sum(jnp.where(mine, wide, 0.0), axis=0, keepdims=True)


def feed_body(
    sub, own, packed, mixed_a, mixed_b, cot, vec, w_t, mine, other,
    layer_out, middle_grad, mixed_grad, keep, send,
    all_s, up_s, down_s, hid_s, gi_s, n2t_s, glt_s, bias_s, sums, bias_sum, mixed,
):
    size, width = packed.shape
    step, steps = pl.program_id(0), pl.num_programs(0)
    me = own[0]
    units = up_s.shape[0]
    piece = units // CHUNKS

    @pl.when(step == 0)
    def _():
        spread_pieces(me, (mine, other), all_s)
        up_s[...] = all_s[:, :piece, :].reshape(units, width)
        down_s[...] = all_s[:, piece : 2 * piece, :].reshape(units, width)
        bias_s[...] = bias_line(all_s[:, 2 * piece, :piece], units)
        bias_sum[...] = jnp.zeros_like(bias_sum)
        sums[...] = jnp.zeros_like(sums)

    @pl.when(step < steps - 1)
    def _():
        mixed[...] = mixed_a[...]

    @pl.when(step == steps - 1)
    def _():
        mixed[...] = mixed_b[...]

    w_out_t = w_t[...].reshape(width, width)
    parts = [slice(k * sub, (k + 1) * sub) for k in range(size // sub)]
    rows = [pl.ds(pl.multiple_of(step * size + k * sub, sub), sub) for k in range(size // sub)]
    mids = [packed[at, :].astype(f32) + dot(mixed[:, at].T, w_out_t, NT) + vec[4:5, :] for at in parts]
    valids = [
        lax.broadcasted_iota(jnp.int32, (sub, 1), 0) + step * size + k * sub < steps * size - 1
        for k in range(size // sub)
    ]
    outs = [jnp.where(valid, cot[at, :].astype(f32), 0.0) for valid, at in zip(valids, parts)]
    out_lows = [out.astype(bf16) for out in outs]
    grads = [dot(out_low, down_s[...], NT) for out_low in out_lows]
    units_of = [norm_parts(middle) for middle in mids]
    lows = [(unit * vec[5:6, :] + vec[6:7, :]).astype(bf16) for unit, _ in units_of]
    us = [dot(low, up_s[...], NT) + bias_s[...] for low in lows]
    downs, backs = [], []
    for k in range(size // sub):
        n2t_s[:, rows[k]] = lows[k].T
        glt_s[:, rows[k]] = out_lows[k].T
        u = us[k]
        phi = 0.5 + 0.5 * lax.erf(u * (1.0 / math.sqrt(2.0)))
        hidden = (u * phi).astype(bf16)
        hid_s[rows[k], :] = hidden
        slope = phi + u * jnp.exp2(u * u * (-0.5 * LOG2E)) * (1.0 / math.sqrt(2.0 * math.pi))
        grad_in = grads[k] * slope
        bias_sum[...] += row_sums(grad_in)
        grad_in_low = grad_in.astype(bf16)
        gi_s[rows[k], :] = grad_in_low
        downs.append(dot(hidden, down_s[...]))
        backs.append(dot(grad_in_low, up_s[...]))
    totals = []
    for k, at in enumerate(parts):
        unit, inverse = units_of[k]
        layer_out[at, :] = jnp.where(valids[k], mids[k] + downs[k] + vec[7:8, :], 0.0).astype(bf16)
        n2_grad = backs[k]
        sums[8:16, :] += row_sums(n2_grad * unit)
        sums[16:24, :] += row_sums(n2_grad)
        total = outs[k] + norm_back(unit, inverse, vec[5:6, :], n2_grad)
        middle_grad[at, :] = total
        sums[0:8, :] += row_sums(total)
        sums[24:32, :] += row_sums(outs[k])
        totals.append(total.astype(bf16))
    for k, at in enumerate(parts):
        mixed_grad[at, :] = dot(totals[k], w_out_t).astype(bf16)

    @pl.when(step == steps - 1)
    def _():
        wide = 2 * width
        for lower in range(0, units, wide):
            hs = slice(lower, lower + wide)
            for index, (left, right) in enumerate(((n2t_s, gi_s), (glt_s, hid_s))):
                pieces = dot(left[...], right[:, hs]).T.astype(bf16).reshape(wide // piece, piece, width)
                store_pieces(me, lower // piece, pieces, keep, send, index * piece, 2 * piece, line_first)
        line = jnp.sum(bias_sum[...], axis=0, keepdims=True)
        lines = [jnp.sum(sums[8 * row : 8 * row + 8, :], axis=0, keepdims=True) for row in range(4)]
        lines += [line[:, row * width : (row + 1) * width] for row in range(units // width)]
        store_extra(lines, keep, send)


def store_extra(lines, keep, send):
    width = keep.shape[1]
    lines = jnp.concatenate(lines + [jnp.zeros((EXTRA - len(lines), width), f32)], axis=0)
    high, low = split_low(lines)
    base = keep.shape[0] - 2 * EXTRA
    for out in (keep, send):
        out[base : base + EXTRA, :] = high
        out[base + EXTRA :, :] = low


def feed_call(own, packed, mixed_a, mixed_b, cot, vec, w_t, mine, other):
    rows, width = packed.shape
    units = 4 * width
    size = mixed_b.shape[1]
    steps = rows // size
    row_block = pl.BlockSpec((size, width), lambda i: (i, 0))
    sent = (units + 2 * EXTRA, width)
    return kernel_call(
        functools.partial(feed_body, size),
        [
            SM,
            row_block,
            pl.BlockSpec((width, size), lambda i: (0, jnp.minimum(i, steps - 2))),
            whole(mixed_b.shape),
            row_block,
            whole((8, width)),
            pl.BlockSpec((CHUNKS // 4, units // CHUNKS, width), lambda i: (3, 0, 0)),
            whole(mine.shape),
            whole(other.shape),
        ],
        (S((rows, width), bf16), S((rows, width), f32), S((rows, width), bf16), S(sent, bf16), S(sent, bf16)),
        [
            pltpu.VMEM((CHUNKS, mine.shape[0] // HALF, width), bf16),
            pltpu.VMEM((units, width), bf16),
            pltpu.VMEM((units, width), bf16),
            pltpu.VMEM((rows, units), bf16),
            pltpu.VMEM((rows, units), bf16),
            pltpu.VMEM((width, rows), bf16),
            pltpu.VMEM((width, rows), bf16),
            pltpu.VMEM((1, units), f32),
            pltpu.VMEM((32, width), f32),
            pltpu.VMEM((8, units), f32),
            pltpu.VMEM((width, size), bf16),
        ],
        grid=(steps,),
        out_specs=(row_block, row_block, row_block, whole(sent), whole(sent)),
        flops=12 * rows * width * units + 6 * rows * width * width,
        micros=30,
        name="feed",
        mib=50,
    )(own, packed, mixed_a, mixed_b, cot, vec, w_t, mine, other)


def side_body(mixed_a, mixed_b, middle_grad, out_grad):
    first = mixed_a.shape[1]
    total = dot(mixed_a[...], middle_grad[:first, :].astype(bf16))
    total += dot(mixed_b[...], middle_grad[first:, :].astype(bf16))
    out_grad[...] = total.T.astype(bf16)


def side_call(mixed_a, mixed_b, middle_grad):
    rows, width = middle_grad.shape
    return kernel_call(
        side_body,
        [VM] * 3,
        (S((width, width), bf16),),
        flops=2 * rows * width * width,
        micros=4,
        name="side",
        mib=20,
    )(mixed_a, mixed_b, middle_grad)[0]


def back_body(
    own, seg, offs, counts, qkv_in, key_in, mixed_in, stats_a, stats_b, seg_rows, seg_cols,
    w_in, packed_in, normed_in, middle_in, out_grad, vec,
    input_out, keep, send,
    qkv, key_t, mixed_grad, w_t, packed, normed_t, middle_grad, input_grad,
    qkv_grad, key_grad, value_grad, stats, sums, sems, late_sems, out_sems,
):
    rows, width = packed.shape
    me = own[0]
    piece = w_t.shape[1]
    size = 512

    def early(i):
        sl = tile_rows(i, size)
        return [
            pltpu.make_async_copy(qkv_in.at[sl, :], qkv.at[sl, :], sems.at[0, i]),
            pltpu.make_async_copy(key_in.at[:, sl], key_t.at[:, sl], sems.at[1, i]),
            pltpu.make_async_copy(mixed_in.at[sl, :], mixed_grad.at[sl, :], sems.at[2, i]),
        ]

    late = [
        pltpu.make_async_copy(source, target, late_sems.at[k])
        for k, (source, target) in enumerate(
            ((w_in, w_t), (packed_in, packed), (middle_in, middle_grad), (normed_in, normed_t))
        )
    ]
    for i in range(rows // size):
        for copy in early(i):
            copy.start()
    for copy in late:
        copy.start()

    def before(j):
        step = size // BLK

        @pl.when(j == 0)
        def _():
            for copy in early(0):
                copy.wait()

        @pl.when(((j + 2) % step == 0) & ((j + 2) // step < rows // size))
        def _():
            for copy in early((j + 2) // step):
                copy.wait()

    attend_back(
        seg, offs, counts, qkv, key_t, mixed_grad, stats_a, stats_b, seg_rows, seg_cols,
        qkv_grad, key_grad, value_grad, stats, before,
    )
    for copy in late:
        copy.wait()
    weights = w_t[: 3 * HALF // 2].reshape(3 * width, width)
    sums[...] = jnp.zeros_like(sums)

    def result(i):
        sl = tile_rows(i, size)
        return pltpu.make_async_copy(input_grad.at[sl, :], input_out.at[sl, :], out_sems.at[i])

    tiles = [slice(i * size, (i + 1) * size) for i in range(rows // size)]
    for sl in tiles:
        qkv_grad[sl, width : 2 * width] = (key_grad[sl, :] * SCALE).astype(bf16)
        qkv_grad[sl, 2 * width :] = value_grad[sl, :].astype(bf16)

    def finish(i, normed_grad):
        sl = tiles[i]
        unit, inverse = norm_parts(packed[sl, :].astype(f32))
        sums[0:8, :] += row_sums(normed_grad * unit)
        sums[8:16, :] += row_sums(normed_grad)
        sums[16:24, :] += row_sums(qkv_grad[sl, :width].astype(f32))
        sums[24:32, :] += row_sums(qkv_grad[sl, 2 * width :].astype(f32))
        input_grad[sl, :] = middle_grad[sl, :] + norm_back(unit, inverse, vec[0:1, :], normed_grad)
        result(i).start()

    def weight_part(lower, wide):
        pieces = dot(normed_t[...], qkv_grad[:, lower : lower + wide]).T.astype(bf16)
        pieces = pieces.reshape(wide // piece, piece, width)
        store_pieces(me, lower // piece, pieces, keep, send, 0, piece, plane_first)

    grads = [dot(qkv_grad[sl, :], weights) for sl in tiles]
    for i in range(len(tiles)):
        if i == 0:
            weight_part(0, 2 * width)
        if i == 2:
            weight_part(2 * width, width)
        finish(i, grads[i])
    pieces = out_grad[...].reshape(width // piece, piece, width)
    store_pieces(me, 3 * width // piece, pieces, keep, send, 0, piece, plane_first)
    lines = [jnp.sum(sums[8 * row : 8 * row + 8, :], axis=0, keepdims=True) for row in range(4)]
    store_extra(lines, keep, send)
    for i in range(rows // size):
        result(i).wait()


def back_call(
    own, seg, offs, counts, qkv, key_t, mixed_grad, stats_a, stats_b, seg_rows, seg_cols,
    w_t, packed, normed_t, middle_grad, out_grad, vec,
):
    rows, width = packed.shape
    sent = S((HALF * w_t.shape[1] + 2 * EXTRA, width), bf16)
    moved = (qkv, key_t, mixed_grad, w_t, packed, normed_t, middle_grad)
    tiles = rows // 512
    return kernel_call(
        back_body,
        [SM] * 4 + [HB] * 3 + [VM] * 4 + [HB] * 4 + [VM] * 2,
        (S((rows, width), f32), sent, sent),
        [pltpu.VMEM(v.shape, v.dtype) for v in moved]
        + [
            pltpu.VMEM((rows, width), f32),
            pltpu.VMEM((rows, 3 * width), bf16),
            pltpu.VMEM((rows, width), f32),
            pltpu.VMEM((rows, width), f32),
            pltpu.VMEM((rows // BLK, HEADS * BLK), f32),
            pltpu.VMEM((32, width), f32),
            pltpu.SemaphoreType.DMA((3, tiles)),
            pltpu.SemaphoreType.DMA((4,)),
            pltpu.SemaphoreType.DMA((tiles,)),
        ],
        flops=22 * rows * width * width,
        micros=30,
        name="back",
        mib=60,
        out_specs=(HB, VM, VM),
    )(
        own, seg, offs, counts, qkv, key_t, mixed_grad, stats_a, stats_b, seg_rows, seg_cols,
        w_t, packed, normed_t, middle_grad, out_grad, vec,
    )


def unpack_body(win, offs, keep, input_grad, image_grads, slots):
    images_here, length = keep.shape
    rows, width = input_grad.shape
    before = lax.broadcasted_iota(jnp.int32, (length, length), 0)
    after = lax.broadcasted_iota(jnp.int32, (length, length), 1)
    tri = jnp.where(before <= after, 1.0, 0.0).astype(bf16)
    place = lax.broadcasted_iota(jnp.int32, (win, length), 0)

    @pl.when(pl.program_id(0) == 0)
    def _():
        kept = keep[...]
        ranks = dot(kept.astype(f32).astype(bf16), tri).astype(jnp.int32) - 1
        slots[...] = jnp.where(kept > 0, ranks, -4 * win)

    chosen, values = [], []
    for k in range(image_grads.shape[0]):
        i = pl.program_id(0) * image_grads.shape[0] + k
        base = pl.multiple_of(jnp.minimum((offs[i] // 8) * 8, rows - win), 8)
        shift = offs[i] - base
        chosen.append(jnp.where(place == slots[pl.ds(i, 1), :] + shift, 1.0, 0.0).astype(bf16))
        values.append(input_grad[pl.ds(base, win), :])
    highs = [value.astype(bf16) for value in values]
    rests = [(value - high.astype(f32)).astype(bf16) for value, high in zip(values, highs)]
    for k in range(image_grads.shape[0]):
        image_grads[k] = dot(chosen[k], highs[k], TN) + dot(chosen[k], rests[k], TN)


def unpack_call(offs, keep, input_grad):
    images_here, length = keep.shape
    rows, width = input_grad.shape
    win = (length + 7 + 7) // 8 * 8
    size = 5
    return kernel_call(
        functools.partial(unpack_body, win),
        [SM, whole(keep.shape), whole(input_grad.shape)],
        (S((images_here, length, width), f32),),
        [pltpu.VMEM((images_here, length), jnp.int32)],
        flops=4 * images_here * win * length * width,
        micros=9,
        name="unpack",
        mib=60,
        grid=(images_here // size,),
        out_specs=(pl.BlockSpec((size, length, width), lambda i: (i, 0, 0)),),
    )(offs, keep, input_grad)[0]


def to_halves(chunks):
    _, size, width = chunks.shape
    ordered = chunks.reshape(4, 4, 2, size, width).transpose(2, 1, 0, 3, 4).reshape(2, HALF * size, width)
    return ordered[0], ordered[1]


def from_halves(keep, send, parts, width, line_first):
    size = keep.shape[0] // HALF // parts
    both = jnp.stack([keep, send]).reshape(2, 4, 4, parts, size, width)
    both = both.transpose((1, 2, 0, 3, 4, 5) if line_first else (2, 1, 0, 3, 4, 5))
    return both.reshape(CHUNKS, parts, size, width)


def adamw(weight, grad, first, second, average, count, rate, decay):
    first_new = BETA_ONE * first + (1.0 - BETA_ONE) * grad
    second_new = BETA_TWO * second + (1.0 - BETA_TWO) * grad * grad
    first_hat = first_new / (1.0 - jnp.power(BETA_ONE, count))
    second_hat = second_new / (1.0 - jnp.power(BETA_TWO, count))
    weight_new = weight - rate * (first_hat / (jnp.sqrt(second_hat) + ADAM_EPS) + decay * weight)
    average_new = AVERAGE_DECAY * average + (1.0 - AVERAGE_DECAY) * weight_new
    return (weight_new, first_new, second_new, average_new)


def wide_of(ref, rows):
    return ref[rows, :].astype(f32)


def whole_extra(ref):
    return wide_of(ref, slice(-2 * EXTRA, -EXTRA)) + wide_of(ref, slice(-EXTRA, None))


def paired(values):
    while len(values) > 1:
        values = [values[i] + values[i + 1] for i in range(0, len(values), 2)]
    return values[0]


def put_extra(values, out, pieces):
    high, low = split_low(values)
    out[-EXTRA:, :] = high.astype(f32) + low.astype(f32)
    for piece in pieces:
        piece[-2 * EXTRA : -EXTRA, :] = high
        piece[-EXTRA:, :] = low


def merge_first_body(ffn_own, ffn_a, ffn_b, ffn_c, attn_own, attn_in, own, *pieces):
    ffn_size, attn_size = (ffn_own.shape[0] - EXTRA) // 4, (attn_own.shape[0] - 2 * EXTRA) // 4
    for part in range(4):
        rows = slice(part * ffn_size, (part + 1) * ffn_size)
        ffn = ffn_own[rows, :] + wide_of(ffn_a, rows) + wide_of(ffn_b, rows) + wide_of(ffn_c, rows)
        rows = slice(part * attn_size, (part + 1) * attn_size)
        attn = wide_of(attn_own, rows) + wide_of(attn_in, rows)
        out = own if part == 0 else pieces[part - 1]
        out[:ffn_size, :] = ffn.astype(out.dtype)
        out[ffn_size : ffn_size + attn_size, :] = attn.astype(out.dtype)
    known = paired([ffn_own[-EXTRA:, :]] + [whole_extra(r) for r in (ffn_a, ffn_b, ffn_c)])
    fresh = whole_extra(attn_own) + whole_extra(attn_in)
    put_extra(jnp.concatenate([fresh[:4], known[:8], fresh[12:]], axis=0), own, pieces)


def merge_first_call(ffn_own, ffn_in, attn_own, attn_in):
    width = ffn_own.shape[1]
    size = (ffn_own.shape[0] - EXTRA) // 4 + (attn_own.shape[0] - 2 * EXTRA) // 4
    out = kernel_call(
        merge_first_body,
        [VM] * 6,
        (S((size + EXTRA, width), f32),) + (S((size + 2 * EXTRA, width), bf16),) * 3,
        micros=3,
        name="merge_first",
    )(ffn_own, *ffn_in, attn_own, attn_in)
    return out[0], out[1:]


def merge_second_body(skip, own, in_a, in_b, in_c, out, *pieces):
    received = (in_a, in_b, in_c)
    size = out.shape[0] - EXTRA
    for part in range(4):
        rows = slice(skip + part * size, skip + (part + 1) * size)
        total = own[rows, :] + wide_of(in_a, rows) + wide_of(in_b, rows) + wide_of(in_c, rows)
        to = out if part == 0 else pieces[part - 1]
        to[:size, :] = total.astype(to.dtype)
    high, low = split_low(paired([own[-EXTRA:, :]] + [whole_extra(r) for r in received]))
    high, low = high.astype(f32), low.astype(f32)
    out[-EXTRA:, :] = high + low
    few = jnp.concatenate([high[: EXTRA // 2], low[: EXTRA // 2]], axis=0).astype(bf16)
    for piece in pieces:
        piece[-EXTRA:, :] = few


def merge_second_call(skip, own, received):
    width = own.shape[1]
    size = (own.shape[0] - EXTRA - skip) // 4
    out = kernel_call(
        functools.partial(merge_second_body, skip),
        [VM] * 4,
        (S((size + EXTRA, width), f32),) + (S((size + EXTRA, width), bf16),) * 3,
        micros=2,
        name="merge_second",
    )(own, *received)
    return out[0], out[1:]


def adamw_with(weight, grad, first, second, average, one, two, rate, decay):
    first_new = BETA_ONE * first + (1.0 - BETA_ONE) * grad
    second_new = BETA_TWO * second + (1.0 - BETA_TWO) * grad * grad
    weight_new = weight - rate * ((first_new / one) / (jnp.sqrt(second_new / two) + ADAM_EPS) + decay * weight)
    average_new = AVERAGE_DECAY * average + (1.0 - AVERAGE_DECAY) * weight_new
    return (weight_new, first_new, second_new, average_new)


def update(powers, states, grad, rate, decay, grad_out, outs, at=slice(None)):
    held = [ref[at] for ref in states]
    grad_out[at] = grad
    for ref, value in zip(outs, adamw_with(held[0], grad, *held[1:], powers[0], powers[1], rate, decay)):
        ref[at] = value


def finish_ffn_body(me, powers, own, in_a, in_b, in_c, *refs):
    states, outs = refs[:8], refs[8:]
    _, piece, width = states[0].shape
    received = (in_a, in_b, in_c)
    for k in range(2):
        rows = slice(k * piece, (k + 1) * piece)
        grad = own[rows, :] + wide_of(in_a, rows) + wide_of(in_b, rows) + wide_of(in_c, rows)
        update(powers, states[:4], grad, MATRIX_RATE, WEIGHT_DECAY, outs[0], outs[2:6], k)
    sums = paired([own[-EXTRA:, :]] + [whole_extra(r) for r in received])
    across = width // piece
    row = lax.broadcasted_iota(jnp.int32, (EXTRA, width), 0)
    line = jnp.sum(jnp.where(row == 8 + me[0] // across, sums, 0.0), axis=0, keepdims=True)
    line = jnp.broadcast_to(line, (8, width))
    shift = (me[0] % across) * piece
    line = jnp.where(shift == 0, line, pltpu.roll(line, width - shift, 1))
    update(powers, states[4:], line[:1, :piece], VECTOR_RATE, 0.0, outs[1], outs[6:])


def finish_ffn_call(me, powers, own, received, states):
    kinds = [S(states[k].shape, f32) for k in (0, 4)]
    out = kernel_call(
        finish_ffn_body,
        [SM, SM] + [VM] * 12,
        tuple(kinds) + tuple(kind for kind in kinds for _ in range(4)),
        micros=2,
        name="finish_ffn",
    )(me, powers, own, *received, *states)
    return out[0], out[1], out[2:6], out[6:]


def finish_attn_body(powers, own, in_a, in_b, in_c, *refs):
    states, outs = refs[:8], refs[8:]
    piece = states[0].shape[0]
    rows = slice(0, piece)
    grad = own[rows, :] + wide_of(in_a, rows) + wide_of(in_b, rows) + wide_of(in_c, rows)
    update(powers, states[:4], grad, MATRIX_RATE, WEIGHT_DECAY, outs[0], outs[2:6])
    few = [wide_of(r, slice(-EXTRA, None)) for r in (in_a, in_b, in_c)]
    sums = paired([own[-EXTRA : -EXTRA // 2, :]] + [v[: EXTRA // 2] + v[EXTRA // 2 :] for v in few])
    vec = jnp.concatenate([sums[:4], own[-EXTRA + 4 : -EXTRA + 8, :]], axis=0)
    update(powers, states[4:], vec, VECTOR_RATE, 0.0, outs[1], outs[6:])


def finish_attn_call(powers, own, received, states):
    kinds = [S(states[k].shape, f32) for k in (0, 4)]
    out = kernel_call(
        finish_attn_body,
        [SM] + [VM] * 12,
        tuple(kinds) + tuple(kind for kind in kinds for _ in range(4)),
        micros=2,
        name="finish_attn",
    )(powers, own, *received, *states)
    return out[0], out[1], out[2:6], out[6:]


def body(
    images, keep_mask, kept_counts, pack_offsets, segment_ids, cotangent,
    attn_weight, ffn_weight, up_bias, vectors,
    attn_first, ffn_first, bias_first, vec_first,
    attn_second, ffn_second, bias_second, vec_second,
    attn_average, ffn_average, bias_average, vec_average, step,
):
    width = images.shape[2]
    rows = segment_ids.shape[0]
    both = ("dp", "mp")
    piece = attn_weight.shape[1]
    tree = lax.axis_size("dp") == 8 and lax.axis_size("mp") == 4
    seg_rows = segment_ids.reshape(rows // BLK, BLK)
    placed = place_call(images, keep_mask, pack_offsets, rows)
    count = step[0].astype(f32)
    powers = jnp.stack([1.0 - jnp.power(BETA_ONE, count), 1.0 - jnp.power(BETA_TWO, count)])
    if tree:
        own = (lax.axis_index("dp") * 4 + lax.axis_index("mp")).astype(jnp.int32)[None]
        pieces = pieces_call(attn_weight.T, jnp.swapaxes(ffn_weight, 1, 2), up_bias[None, :])
        lines = [pieces] + [over_line(pieces, k) for k in (1, 2, 3)]
        placed, *lines = tie(placed, *lines)
        attn_line = jnp.concatenate([line[:piece] for line in lines], axis=0)
        ffn_line = jnp.concatenate([line[piece:] for line in lines], axis=0)
        attn_mine = gather_plane(attn_line)
        normed, normed_t, seg_cols = norm_call(placed, seg_rows, vectors)
        attn_mine, normed, ffn_line = tie(attn_mine, normed, ffn_line)
        attn_other = over_core(attn_mine)
        ffn_lines = [ffn_line] + [over_plane(ffn_line, k) for k in (1, 2, 3)]
    else:
        own = jnp.zeros((1,), jnp.int32)
        attn_all = lax.all_gather(attn_weight.astype(bf16).T, both, axis=0, tiled=True)
        ffn_all = lax.all_gather(jnp.swapaxes(ffn_weight.astype(bf16), 1, 2), both, axis=1, tiled=True)
        bias_all = lax.all_gather(up_bias.astype(bf16), both, axis=0, tiled=True)
        size = 4 * width // CHUNKS
        ffn_all = jnp.concatenate(
            [
                ffn_all[0].reshape(CHUNKS, size, width),
                ffn_all[1].reshape(CHUNKS, size, width),
                jnp.pad(bias_all.reshape(CHUNKS, 1, size), ((0, 0), (0, 15), (0, width - size))),
            ],
            axis=1,
        )
        attn_mine, attn_other = to_halves(attn_all.reshape(CHUNKS, size, width))
        ffn_mine, ffn_other = to_halves(ffn_all)
        normed, normed_t, seg_cols = norm_call(placed, seg_rows, vectors)
    where = (segment_ids, pack_offsets, kept_counts)
    blocks = rows // BLK
    late = blocks // 4
    qkv, key_t, value_t, w_t, mixed_a, stats_a = attend_first_call(
        blocks - late, own, *where, normed, attn_mine, attn_other, vectors, seg_rows, seg_cols
    )
    if tree:
        qkv, mixed_a, *ffn_lines = tie(qkv, mixed_a, *ffn_lines)
        ffn_mine = jnp.concatenate(ffn_lines, axis=0)
        ffn_other = over_core(ffn_mine)
    mixed_b, stats_b = attend_last_call(late, *where, qkv, value_t, seg_rows, seg_cols)
    if tree:
        mixed_b, ffn_mine, ffn_other = tie(mixed_b, ffn_mine, ffn_other)
    layer_out, middle_grad, mixed_grad, ffn_keep, ffn_send = feed_call(
        own, placed, mixed_a, mixed_b, cotangent, vectors, w_t, ffn_mine, ffn_other
    )
    if tree:
        ffn_in = over_core(ffn_send)
    out_grad = side_call(mixed_a, mixed_b, middle_grad)
    if tree:
        out_grad, ffn_in = tie(out_grad, ffn_in)
        ffn_own, *ffn_out = combine_call(ffn_keep, [ffn_in], 4, EXTRA)
        out_grad, ffn_own, *ffn_out = tie(out_grad, ffn_own, *ffn_out)
        ffn_in = [over_line(p, k + 1) for k, p in enumerate(ffn_out)]
    input_grad, attn_keep, attn_send = back_call(
        own, *where, qkv, key_t, mixed_grad, stats_a, stats_b, seg_rows, seg_cols,
        w_t, placed, normed_t, middle_grad, out_grad, vectors,
    )
    index = lax.axis_index("dp") * lax.axis_size("mp") + lax.axis_index("mp")
    if tree:
        input_grad, attn_send, *ffn_in = tie(input_grad, attn_send, *ffn_in)
        attn_in = over_core(attn_send)
        states = [v.T for v in (attn_weight, attn_first, attn_second, attn_average)]
        states += [vectors, vec_first, vec_second, vec_average]
        ffn_states = [jnp.swapaxes(v, 1, 2) for v in (ffn_weight, ffn_first, ffn_second, ffn_average)]
        ffn_states += [v[None, :] for v in (up_bias, bias_first, bias_second, bias_average)]
        merged, pieces = merge_first_call(ffn_own, ffn_in, attn_keep, attn_in)
        input_grad, *pieces = tie(input_grad, *pieces)
        received = [over_plane(p, k + 1) for k, p in enumerate(pieces)]
        image_grads = unpack_call(pack_offsets, keep_mask, input_grad)
        image_grads, *received = tie(image_grads, *received)
        attn_own, pieces = merge_second_call(2 * piece, merged, received)
        image_grads, merged, *pieces = tie(image_grads, merged, *pieces)
        last = [over_line(p, k + 1) for k, p in enumerate(pieces)]
        ffn_grad, bias_grad, ffn_up, bias_up = finish_ffn_call(own, powers, merged, received, ffn_states)
        image_grads, ffn_grad, *last = tie(image_grads, ffn_grad, *last)
        attn_grad, vec_grad, attn_up, vec_up = finish_attn_call(powers, attn_own, last, states)
        attn_grad, ffn_grad, bias_grad = attn_grad.T, jnp.swapaxes(ffn_grad, 1, 2), bias_grad[0]
        attn_up, ffn_up = [v.T for v in attn_up], [jnp.swapaxes(v, 1, 2) for v in ffn_up]
        bias_up = [v[0] for v in bias_up]
    else:
        image_grads = unpack_call(pack_offsets, keep_mask, input_grad)
        base = ffn_keep.shape[0] - 2 * EXTRA
        ffn_t = from_halves(ffn_keep[:base], ffn_send[:base], 2, width, True)
        ffn_t = jnp.swapaxes(ffn_t, 0, 1).reshape(2, 4 * width, width)
        ffn_t = lax.psum_scatter(ffn_t.astype(f32), both, scatter_dimension=1, tiled=True)
        ffn_grad = jnp.swapaxes(ffn_t, 1, 2)
        known = ffn_keep[base : base + EXTRA].astype(f32) + ffn_keep[base + EXTRA :].astype(f32)
        base = attn_keep.shape[0] - 2 * EXTRA
        attn_t = from_halves(attn_keep[:base], attn_send[:base], 1, width, False).reshape(4 * width, width)
        attn_grad = lax.psum_scatter(attn_t.astype(f32), both, scatter_dimension=0, tiled=True).T
        sums = attn_keep[base : base + EXTRA].astype(f32) + attn_keep[base + EXTRA :].astype(f32)
        sums = lax.psum(jnp.concatenate([sums[:4], known[:8]], axis=0), both)
        vec_grad, bias_sums = sums[:8], sums[8:]
        bias_grad = lax.dynamic_slice_in_dim(bias_sums.reshape(4 * width), index * piece, piece, 0)
        attn_up = adamw(attn_weight, attn_grad, attn_first, attn_second, attn_average, count, MATRIX_RATE, WEIGHT_DECAY)
        vec_up = adamw(vectors, vec_grad, vec_first, vec_second, vec_average, count, VECTOR_RATE, 0.0)
        ffn_up = adamw(ffn_weight, ffn_grad, ffn_first, ffn_second, ffn_average, count, MATRIX_RATE, WEIGHT_DECAY)
        bias_up = adamw(up_bias, bias_grad, bias_first, bias_second, bias_average, count, VECTOR_RATE, 0.0)
    news = [part[k] for k in range(4) for part in (attn_up, ffn_up, bias_up, vec_up)]
    return (layer_out, image_grads, attn_grad, ffn_grad, bias_grad, vec_grad, *news)


def solution(mesh):
    both = ("dp", "mp")
    matrix, slab, line = P(None, both), P(None, None, both), P(both)
    states = (matrix, slab, line, P())
    return jax.shard_map(
        body,
        mesh=mesh,
        in_specs=(P(both, None, None), P(both, None), line, line, line, P(both, None), *states * 4, P()),
        out_specs=(P(both, None), P(both, None, None), *states, *states * 4),
        check_vma=False,
    )
```

```python
import functools
import math

import jax
import jax.numpy as jnp
from jax import lax
from jax.experimental import pallas as pl
from jax.experimental.pallas import tpu as pltpu
from jax.sharding import PartitionSpec as P

HEADS = 6
HEAD = 64
PAIR = 2 * HEAD
PAIRS = HEADS // 2
BLK = 128
REACH = 5
CHUNKS = 32
HALF = CHUNKS // 2
EXTRA = 16
EXCLUDED = -8.0e9
INCLUDED = 3.0e38

NORM_EPS = 1e-06
BETA_ONE = 0.9
BETA_TWO = 0.999
ADAM_EPS = 1e-08
MATRIX_RATE = 0.05
VECTOR_RATE = 0.2
WEIGHT_DECAY = 0.05
AVERAGE_DECAY = 0.8

LOG2E = 1.4426950408889634
SCORE_LOG2 = LOG2E / math.sqrt(HEAD)
SCALE = 1.0 / math.sqrt(HEAD)

f32 = jnp.float32
bf16 = jnp.bfloat16
NN = (((1,), (0,)), ((), ()))
NT = (((1,), (1,)), ((), ()))
TN = (((0,), (0,)), ((), ()))
VM = pl.BlockSpec(memory_space=pltpu.VMEM)
SM = pl.BlockSpec(memory_space=pltpu.SMEM)
HB = pl.BlockSpec(memory_space=pl.ANY)
S = jax.ShapeDtypeStruct


def dot(left, right, dims=NN):
    return lax.dot_general(left, right, dims, preferred_element_type=f32)


def kernel_call(body, ins, outs, scratch=(), flops=0, micros=1, name=None, grid=(), out_specs=None, mib=16):
    return pl.pallas_call(
        body,
        grid=grid,
        out_shape=outs,
        in_specs=ins,
        out_specs=out_specs or tuple(VM for _ in outs),
        scratch_shapes=list(scratch),
        compiler_params=pltpu.CompilerParams(vmem_limit_bytes=mib * 2**20),
        cost_estimate=pl.CostEstimate(flops=flops, bytes_accessed=micros * 3_500_000, transcendentals=0),
        name=name,
    )


def whole(shape):
    return pl.BlockSpec(shape, lambda i: (0,) * len(shape))


def row_sums(values):
    rows, width = values.shape
    return jnp.sum(values.reshape(rows // 8, 8, width), axis=0)


def norm_parts(values):
    scale = 1.0 / values.shape[-1]
    centre = jnp.sum(values, axis=-1, keepdims=True) * scale
    centred = values - centre
    spread = jnp.sum(centred * centred, axis=-1, keepdims=True) * scale
    inverse = lax.rsqrt(spread + NORM_EPS)
    return centred * inverse, inverse


def norm_back(unit, inverse, gain, grad):
    scale = 1.0 / unit.shape[-1]
    scaled = grad * gain
    mean = jnp.sum(scaled, axis=-1, keepdims=True) * scale
    along = jnp.sum(scaled * unit, axis=-1, keepdims=True) * scale
    return inverse * (scaled - mean - unit * along)


def tile_rows(count, size):
    return pl.ds(pl.multiple_of(count * size, size), size)


def plane_first(apart):
    return (apart & 3) * 4 + lax.shift_right_logical(apart, 2)


def line_first(apart):
    return apart


def spread_pieces(own, halves, out):
    for near in range(2):
        for slot in range(HALF):
            apart = near + 2 * ((slot // 4) + 4 * (slot % 4))
            out[own ^ apart] = halves[near][slot * out.shape[1] : (slot + 1) * out.shape[1], :]


def store_pieces(own, start, pieces, keep, send, at, step, order):
    count, size, _ = pieces.shape
    odd = (own & 1) == 1
    for e in range(0, count, 2):
        apart = lax.shift_right_logical(own, 1) ^ ((start + e) // 2)
        row = pl.multiple_of(order(apart) * step + at, 16)
        even_piece, odd_piece = pieces[e], pieces[e + 1]
        keep[pl.ds(row, size), :] = jnp.where(odd, odd_piece, even_piece)
        send[pl.ds(row, size), :] = jnp.where(odd, even_piece, odd_piece)


def split_low(values):
    high = values.astype(bf16)
    return high, (values - high.astype(f32)).astype(bf16)


def combine_body(parts, size, extra, count, *refs):
    own, received, outs = refs[0], refs[1 : 1 + count], refs[1 + count :]
    base = parts * size
    for part in range(parts):
        rows = slice(part * size, (part + 1) * size)
        total = own[rows, :].astype(f32)
        for other in received:
            total = total + other[rows, :].astype(f32)
        if part == 0:
            outs[0][:size, :] = total
        else:
            outs[part][:size, :] = total.astype(bf16)
    if extra:
        if own.dtype == bf16:
            sums = [own[base : base + extra, :].astype(f32) + own[base + extra :, :].astype(f32)]
        else:
            sums = [own[base:, :]]
        sums += [r[base : base + extra, :].astype(f32) + r[base + extra :, :].astype(f32) for r in received]
        while len(sums) > 1:
            sums = [sums[i] + sums[i + 1] for i in range(0, len(sums), 2)]
        high, low = split_low(sums[0])
        outs[0][size:, :] = high.astype(f32) + low.astype(f32) if parts > 1 else sums[0]
        for out in outs[1:]:
            out[size : size + extra, :] = high
            out[size + extra :, :] = low


def combine_call(own, received, parts, extra):
    size = (received[0].shape[0] - 2 * extra) // parts
    width = own.shape[1]
    outs = (S((size + extra, width), f32),) + (S((size + 2 * extra, width), bf16),) * (parts - 1)
    return kernel_call(
        functools.partial(combine_body, parts, size, extra, len(received)),
        [VM] * (1 + len(received)),
        outs,
        flops=own.size * len(received),
        micros=2,
        name="combine",
    )(own, *received)


def pieces_body(attn, ffn, bias, out, line):
    piece, width = attn.shape
    line[...] = jnp.zeros_like(line)
    line[0:1, :piece] = bias[...]
    out[:piece, :] = attn[...].astype(bf16)
    for k in range(2):
        out[(1 + k) * piece : (2 + k) * piece, :] = ffn[k].astype(bf16)
    out[3 * piece :, :] = line[...].astype(bf16)


def pieces_call(attn, ffn, bias):
    piece, width = attn.shape
    return kernel_call(
        pieces_body,
        [VM] * 3,
        (S((3 * piece + 16, width), bf16),),
        [pltpu.VMEM((16, width), f32)],
        name="pieces",
        mib=60,
    )(attn, ffn, bias)[0]


def over_core(values):
    return lax.ppermute(values, "mp", [(i, i ^ 1) for i in range(lax.axis_size("mp"))])


def over_plane(values, apart):
    devices = lax.axis_size("dp") * lax.axis_size("mp")
    return lax.ppermute(values, ("dp", "mp"), [(i, i ^ (2 * apart)) for i in range(devices)])


def over_line(values, apart):
    return lax.ppermute(values, "dp", [(i, i ^ (2 * apart)) for i in range(lax.axis_size("dp"))])


def tie(*values):
    return lax.optimization_barrier(values)


def gather_plane(pieces):
    return jnp.concatenate([pieces] + [over_plane(pieces, k) for k in (1, 2, 3)], axis=0)


def place_body(win, offs, images, keep, packed, acc, slots):
    images_here, length = keep.shape
    rows, width = packed.shape
    size = images.shape[0]
    step = pl.program_id(0)

    @pl.when(step == 0)
    def _():
        before = lax.broadcasted_iota(jnp.int32, (length, length), 0)
        after = lax.broadcasted_iota(jnp.int32, (length, length), 1)
        tri = jnp.where(before <= after, 1.0, 0.0).astype(bf16)
        kept = keep[...]
        ranks = dot(kept.astype(f32).astype(bf16), tri).astype(jnp.int32) - 1
        slots[...] = jnp.where(kept > 0, ranks, -4 * win)
        acc[0:8, :] = jnp.zeros((8, width), f32)

    place = lax.broadcasted_iota(jnp.int32, (win, length), 0)
    starts = [offs[step * size + k] for k in range(size)]
    bases = [pl.multiple_of((start // 8) * 8, 8) for start in starts]
    lines = [slots[pl.ds(step * size + k, 1), :] + (starts[k] - bases[k]) for k in range(size)]
    chosen = [jnp.where(place == line, 1.0, 0.0).astype(bf16) for line in lines]
    moved = [dot(chosen[k], images[k]) for k in range(size)]
    for base, part in zip(bases, moved):
        acc[pl.ds(base, 8), :] += part[0:8]
        acc[pl.ds(base + 8, win - 8), :] = part[8:]

    @pl.when(step == pl.num_programs(0) - 1)
    def _():
        packed[...] = acc[:rows, :].astype(bf16)


def place_call(images, keep, offs, rows):
    images_here, length, width = images.shape
    win = (length + 7 + 7) // 8 * 8
    size = 5
    return kernel_call(
        functools.partial(place_body, win),
        [SM, pl.BlockSpec((size, length, width), lambda i: (i, 0, 0)), whole(keep.shape)],
        (S((rows, width), bf16),),
        [pltpu.VMEM((rows + win, width), f32), pltpu.VMEM((images_here, length), jnp.int32)],
        flops=2 * images_here * win * length * width,
        micros=6,
        name="place",
        mib=60,
        grid=(images_here // size,),
        out_specs=(whole((rows, width)),),
    )(offs, images, keep)[0]


def norm_body(packed, seg_rows, vec, normed, normed_t, seg_cols):
    rows, width = packed.shape
    step = pl.program_id(0)
    sub = 128
    parts = [slice(k * sub, (k + 1) * sub) for k in range(rows // sub)]
    units = [norm_parts(packed[at, :].astype(f32))[0] for at in parts]
    lows = [(unit * vec[0:1, :] + vec[1:2, :]).astype(bf16) for unit in units]
    for at, low in zip(parts, lows):
        normed[at, :] = low
    for at, low in zip(parts, lows):
        normed_t[:, at] = low.T
    for k in range(rows // BLK):
        line = seg_rows[pl.ds(step * (rows // BLK) + k, 1), :]
        seg_cols[k * BLK : (k + 1) * BLK, :] = jnp.broadcast_to(line, (BLK, BLK)).T


def norm_call(packed, seg_rows, vec):
    rows, width = packed.shape
    size = 512
    return kernel_call(
        norm_body,
        [pl.BlockSpec((size, width), lambda i: (i, 0)), whole(seg_rows.shape), whole(vec.shape)],
        (S((rows, width), bf16), S((width, rows), bf16), S((rows, BLK), jnp.int32)),
        flops=rows * width * 12,
        micros=5,
        name="norm",
        mib=60,
        grid=(rows // size,),
        out_specs=(
            pl.BlockSpec((size, width), lambda i: (i, 0)),
            pl.BlockSpec((width, size), lambda i: (0, i)),
            pl.BlockSpec((size, BLK), lambda i: (i, 0)),
        ),
    )(packed, seg_rows, vec)


def window(seg, offs, counts, j, images_here, tiles, step):
    first = seg[j * BLK]
    last = seg[j * BLK + BLK - 1]
    used = last < images_here
    last_here = jnp.where(used, last, 0)
    end = jnp.where(used, offs[last_here] + counts[last_here], tiles * BLK)
    low = jnp.minimum(offs[first] // BLK, tiles - 2)
    return low, jnp.maximum((end + step - 1) // step - low * (BLK // step), 2 * BLK // step)


def masked_pair(pair):
    lane = lax.broadcasted_iota(jnp.int32, pair.shape, 1)
    none = jnp.zeros_like(pair)
    return jnp.concatenate([jnp.where(lane < HEAD, pair, none), jnp.where(lane >= HEAD, pair, none)], axis=0)


def limits(seg_rows, seg_cols, j, keys):
    same = seg_cols[keys, :] == seg_rows[pl.ds(j, 1), :]
    lim = jnp.where(same, INCLUDED, EXCLUDED)
    return jnp.concatenate([lim, lim], axis=1)


def over_windows(seg, offs, counts, tiles, base, first, blocks, block, step=BLK, before=None):
    def one(j, carry):
        if before is not None:
            before(j)
        low, size = window(seg, offs, counts, j, offs.shape[0], tiles, step)
        for n in range(2 * BLK // step, REACH * BLK // step + 1):

            @pl.when(size == n)
            def _():
                block(j, pl.ds(pl.multiple_of((low - base) * BLK, BLK), n * step))

        return carry

    lax.fori_loop(first, first + blocks, one, 0)


def attend_blocks(base, first, blocks, seg, offs, counts, qkv, value_t, seg_rows, seg_cols, mixed_t, stats):
    width = value_t.shape[0]
    tiles = seg.shape[0] // BLK

    def block(j, keys):
        here = tile_rows(j - base, BLK)
        there = tile_rows(j - first, BLK)
        lim = limits(seg_rows, seg_cols, j, keys)
        ats = [slice(p * PAIR, (p + 1) * PAIR) for p in range(PAIRS)]
        raws = [
            dot(qkv[keys, width + p * PAIR : width + (p + 1) * PAIR], masked_pair(qkv[here, ats[p]]), NT)
            for p in range(PAIRS)
        ]
        raws = [jnp.minimum(raw, lim) for raw in raws]
        tops = [jnp.max(raw, axis=0, keepdims=True) for raw in raws]
        expos = [jnp.exp2((raw - top) * SCORE_LOG2) for raw, top in zip(raws, tops)]
        totals = [jnp.sum(expo, axis=0, keepdims=True) for expo in expos]
        lows = [(expo * (1.0 / total)).astype(bf16) for expo, total in zip(expos, totals)]
        outs = [dot(value_t[at, keys], low) for at, low in zip(ats, lows)]
        for p in range(PAIRS):
            out = outs[p]
            mixed_t[p * PAIR : p * PAIR + HEAD, there] = out[:HEAD, :BLK].astype(bf16)
            mixed_t[p * PAIR + HEAD : (p + 1) * PAIR, there] = out[HEAD:, BLK:].astype(bf16)
            level = tops[p] * SCORE_LOG2 + jnp.log2(totals[p])
            stats[pl.ds(j - first, 1), p * 2 * BLK : (p + 1) * 2 * BLK] = level

    over_windows(seg, offs, counts, tiles, base, first, blocks, block)


def attend_first_body(
    own, seg, offs, counts, normed_in, mine, other, vec, seg_rows, cols_in,
    qkv_out, key_out, value_out, w_out, mixed_t, stats,
    qkv, key_t, value_t, w_t, normed, seg_cols, sems, in_sems,
):
    rows, width = normed.shape
    size = 512

    def reads(i):
        sl = tile_rows(i, size)
        return pltpu.make_async_copy(normed_in.at[sl, :], normed.at[sl, :], in_sems.at[i])

    cols = pltpu.make_async_copy(cols_in, seg_cols, in_sems.at[rows // size])
    for i in range(rows // size):
        reads(i).start()
    cols.start()
    spread_pieces(own[0], (mine, other), w_t)
    units = w_t.shape[0] * w_t.shape[1]
    weights = w_t[...].reshape(units, width)[: 3 * width]
    bias = jnp.concatenate([vec[2:3, :], jnp.zeros((1, width), f32), vec[3:4, :]], axis=1)
    last = pltpu.make_async_copy(w_t, w_out, sems.at[3, 0])
    last.start()

    def copies(i):
        sl = tile_rows(i, size)
        return [
            pltpu.make_async_copy(qkv.at[sl, :], qkv_out.at[sl, :], sems.at[0, i]),
            pltpu.make_async_copy(key_t.at[:, sl], key_out.at[:, sl], sems.at[1, i]),
            pltpu.make_async_copy(value_t.at[:, sl], value_out.at[:, sl], sems.at[2, i]),
        ]

    def project(i, carry):
        sl = tile_rows(i, size)
        reads(i).wait()
        low = (dot(normed[sl, :], weights, NT) + bias).astype(bf16)
        qkv[sl, :] = low
        key_t[:, sl] = low[:, width : 2 * width].T
        value_t[:, sl] = low[:, 2 * width :].T
        for copy in copies(i):
            copy.start()
        return carry

    lax.fori_loop(0, rows // size, project, 0)
    cols.wait()
    attend_blocks(
        0, 0, mixed_t.shape[1] // BLK, seg, offs, counts, qkv, value_t, seg_rows, seg_cols, mixed_t, stats
    )
    for i in range(rows // size):
        for copy in copies(i):
            copy.wait()
    last.wait()


def attend_first_call(blocks, own, seg, offs, counts, normed, mine, other, vec, seg_rows, seg_cols):
    rows, width = normed.shape
    piece = mine.shape[0] // HALF
    kept = ((rows, 3 * width), (width, rows), (width, rows), (CHUNKS, piece, width))
    return kernel_call(
        attend_first_body,
        [SM, SM, SM, SM, HB, VM, VM, VM, VM, HB],
        tuple(S(shape, bf16) for shape in kept)
        + (S((width, blocks * BLK), bf16), S((blocks, HEADS * BLK), f32)),
        [pltpu.VMEM(shape, bf16) for shape in kept]
        + [
            pltpu.VMEM(normed.shape, bf16),
            pltpu.VMEM(seg_cols.shape, jnp.int32),
            pltpu.SemaphoreType.DMA((4, rows // 512)),
            pltpu.SemaphoreType.DMA((rows // 512 + 1,)),
        ],
        flops=2 * rows * width * 3 * width,
        micros=20,
        name="attend_first",
        mib=60,
        out_specs=(HB, HB, HB, HB, VM, VM),
    )(own, seg, offs, counts, normed, mine, other, vec, seg_rows, seg_cols)


def attend_last_call(blocks, seg, offs, counts, qkv, value_t, seg_rows, seg_cols):
    width, rows = value_t.shape
    part = (blocks + REACH - 1) * BLK
    while rows % part:
        part += BLK
    at = rows // part - 1
    tiles = rows // BLK
    return kernel_call(
        functools.partial(attend_blocks, tiles - part // BLK, tiles - blocks, blocks),
        [
            SM,
            SM,
            SM,
            pl.BlockSpec((part, 3 * width), lambda i: (at, 0)),
            pl.BlockSpec((width, part), lambda i: (0, at)),
            whole(seg_rows.shape),
            pl.BlockSpec((part, BLK), lambda i: (at, 0)),
        ],
        (S((width, blocks * BLK), bf16), S((blocks, HEADS * BLK), f32)),
        grid=(1,),
        out_specs=(whole((width, blocks * BLK)), whole((blocks, HEADS * BLK))),
        flops=4 * blocks * BLK * 512 * width,
        micros=5,
        name="attend_last",
        mib=60,
    )(seg, offs, counts, qkv, value_t, seg_rows, seg_cols)


def attend_back(
    seg, offs, counts, qkv, key_t, mixed_grad, stats_a, stats_b, seg_rows, seg_cols, qkv_grad, key_grad, value_grad, stats, before
):
    rows, width = mixed_grad.shape
    key_grad[...] = jnp.zeros_like(key_grad)
    value_grad[...] = jnp.zeros_like(value_grad)
    stats[: stats_a.shape[0], :] = stats_a[...]
    stats[stats_a.shape[0] :, :] = stats_b[...]

    def block(j, keys):
        here = tile_rows(j, BLK)
        lim = limits(seg_rows, seg_cols, j, keys)
        ats = [slice(p * PAIR, (p + 1) * PAIR) for p in range(PAIRS)]
        levels = stats[pl.ds(j, 1), :]
        levels = [levels[:, p * 2 * BLK : (p + 1) * 2 * BLK] for p in range(PAIRS)]
        queries = [masked_pair(qkv[here, at]) for at in ats]
        outs = [masked_pair(mixed_grad[here, at]) for at in ats]
        raws = [
            dot(qkv[keys, width + p * PAIR : width + (p + 1) * PAIR], queries[p], NT) for p in range(PAIRS)
        ]
        grads = [
            dot(qkv[keys, 2 * width + p * PAIR : 2 * width + (p + 1) * PAIR], outs[p], NT) for p in range(PAIRS)
        ]
        probs = [jnp.exp2(jnp.minimum(raw, lim) * SCORE_LOG2 - level) for raw, level in zip(raws, levels)]
        inners = [jnp.sum(prob * grad, axis=0, keepdims=True) for prob, grad in zip(probs, grads)]
        lows = [prob.astype(bf16) for prob in probs]
        score_grads = [
            (prob * (grad - inner)).astype(bf16) for prob, grad, inner in zip(probs, grads, inners)
        ]
        for p in range(PAIRS):
            value_grad[keys, ats[p]] += dot(lows[p], outs[p])
        for p in range(PAIRS):
            key_grad[keys, ats[p]] += dot(score_grads[p], queries[p])
        for p in range(PAIRS):
            query_t = dot(key_t[ats[p], keys], score_grads[p]) * SCALE
            joined = jnp.concatenate([query_t[:HEAD, :BLK], query_t[HEAD:, BLK:]], axis=0)
            qkv_grad[here, ats[p]] = joined.T.astype(bf16)

    over_windows(seg, offs, counts, rows // BLK, 0, 0, rows // BLK, block, BLK // 2, before)


def bias_line(rows_of, units):
    chunks, size = rows_of.shape
    column = lax.broadcasted_iota(jnp.int32, (size, units), 1)
    within = lax.broadcasted_iota(jnp.int32, (size, units), 0)
    repeat = jnp.where(column % size == within, 1.0, 0.0).astype(bf16)
    wide = dot(rows_of, repeat)
    owner = lax.broadcasted_iota(jnp.int32, (chunks, units), 1) // size
    mine = owner == lax.broadcasted_iota(jnp.int32, (chunks, units), 0)
    return jnp.sum(jnp.where(mine, wide, 0.0), axis=0, keepdims=True)


def feed_body(
    sub, own, packed, mixed_a, mixed_b, cot, vec, w_t, mine, other,
    layer_out, middle_grad, mixed_grad, keep, send,
    all_s, up_s, down_s, hid_s, gi_s, n2t_s, glt_s, bias_s, sums, bias_sum, mixed,
):
    size, width = packed.shape
    step, steps = pl.program_id(0), pl.num_programs(0)
    me = own[0]
    units = up_s.shape[0]
    piece = units // CHUNKS

    @pl.when(step == 0)
    def _():
        spread_pieces(me, (mine, other), all_s)
        up_s[...] = all_s[:, :piece, :].reshape(units, width)
        down_s[...] = all_s[:, piece : 2 * piece, :].reshape(units, width)
        bias_s[...] = bias_line(all_s[:, 2 * piece, :piece], units)
        bias_sum[...] = jnp.zeros_like(bias_sum)
        sums[...] = jnp.zeros_like(sums)

    @pl.when(step < steps - 1)
    def _():
        mixed[...] = mixed_a[...]

    @pl.when(step == steps - 1)
    def _():
        mixed[...] = mixed_b[...]

    w_out_t = w_t[...].reshape(width, width)
    parts = [slice(k * sub, (k + 1) * sub) for k in range(size // sub)]
    rows = [pl.ds(pl.multiple_of(step * size + k * sub, sub), sub) for k in range(size // sub)]
    mids = [packed[at, :].astype(f32) + dot(mixed[:, at].T, w_out_t, NT) + vec[4:5, :] for at in parts]
    valids = [
        lax.broadcasted_iota(jnp.int32, (sub, 1), 0) + step * size + k * sub < steps * size - 1
        for k in range(size // sub)
    ]
    outs = [jnp.where(valid, cot[at, :].astype(f32), 0.0) for valid, at in zip(valids, parts)]
    out_lows = [out.astype(bf16) for out in outs]
    grads = [dot(out_low, down_s[...], NT) for out_low in out_lows]
    units_of = [norm_parts(middle) for middle in mids]
    lows = [(unit * vec[5:6, :] + vec[6:7, :]).astype(bf16) for unit, _ in units_of]
    us = [dot(low, up_s[...], NT) + bias_s[...] for low in lows]
    downs, backs = [], []
    for k in range(size // sub):
        n2t_s[:, rows[k]] = lows[k].T
        glt_s[:, rows[k]] = out_lows[k].T
        u = us[k]
        phi = 0.5 + 0.5 * lax.erf(u * (1.0 / math.sqrt(2.0)))
        hidden = (u * phi).astype(bf16)
        hid_s[rows[k], :] = hidden
        slope = phi + u * jnp.exp2(u * u * (-0.5 * LOG2E)) * (1.0 / math.sqrt(2.0 * math.pi))
        grad_in = grads[k] * slope
        bias_sum[...] += row_sums(grad_in)
        grad_in_low = grad_in.astype(bf16)
        gi_s[rows[k], :] = grad_in_low
        downs.append(dot(hidden, down_s[...]))
        backs.append(dot(grad_in_low, up_s[...]))
    totals = []
    for k, at in enumerate(parts):
        unit, inverse = units_of[k]
        layer_out[at, :] = jnp.where(valids[k], mids[k] + downs[k] + vec[7:8, :], 0.0).astype(bf16)
        n2_grad = backs[k]
        sums[8:16, :] += row_sums(n2_grad * unit)
        sums[16:24, :] += row_sums(n2_grad)
        total = outs[k] + norm_back(unit, inverse, vec[5:6, :], n2_grad)
        middle_grad[at, :] = total
        sums[0:8, :] += row_sums(total)
        sums[24:32, :] += row_sums(outs[k])
        totals.append(total.astype(bf16))
    for k, at in enumerate(parts):
        mixed_grad[at, :] = dot(totals[k], w_out_t).astype(bf16)

    @pl.when(step == steps - 1)
    def _():
        wide = 2 * width
        for lower in range(0, units, wide):
            hs = slice(lower, lower + wide)
            for index, (left, right) in enumerate(((n2t_s, gi_s), (glt_s, hid_s))):
                pieces = dot(left[...], right[:, hs]).T.astype(bf16).reshape(wide // piece, piece, width)
                store_pieces(me, lower // piece, pieces, keep, send, index * piece, 2 * piece, line_first)
        line = jnp.sum(bias_sum[...], axis=0, keepdims=True)
        lines = [jnp.sum(sums[8 * row : 8 * row + 8, :], axis=0, keepdims=True) for row in range(4)]
        lines += [line[:, row * width : (row + 1) * width] for row in range(units // width)]
        store_extra(lines, keep, send)


def store_extra(lines, keep, send):
    width = keep.shape[1]
    lines = jnp.concatenate(lines + [jnp.zeros((EXTRA - len(lines), width), f32)], axis=0)
    high, low = split_low(lines)
    base = keep.shape[0] - 2 * EXTRA
    for out in (keep, send):
        out[base : base + EXTRA, :] = high
        out[base + EXTRA :, :] = low


def feed_call(own, packed, mixed_a, mixed_b, cot, vec, w_t, mine, other):
    rows, width = packed.shape
    units = 4 * width
    size = mixed_b.shape[1]
    steps = rows // size
    row_block = pl.BlockSpec((size, width), lambda i: (i, 0))
    sent = (units + 2 * EXTRA, width)
    return kernel_call(
        functools.partial(feed_body, size),
        [
            SM,
            row_block,
            pl.BlockSpec((width, size), lambda i: (0, jnp.minimum(i, steps - 2))),
            whole(mixed_b.shape),
            row_block,
            whole((8, width)),
            pl.BlockSpec((CHUNKS // 4, units // CHUNKS, width), lambda i: (3, 0, 0)),
            whole(mine.shape),
            whole(other.shape),
        ],
        (S((rows, width), bf16), S((rows, width), f32), S((rows, width), bf16), S(sent, bf16), S(sent, bf16)),
        [
            pltpu.VMEM((CHUNKS, mine.shape[0] // HALF, width), bf16),
            pltpu.VMEM((units, width), bf16),
            pltpu.VMEM((units, width), bf16),
            pltpu.VMEM((rows, units), bf16),
            pltpu.VMEM((rows, units), bf16),
            pltpu.VMEM((width, rows), bf16),
            pltpu.VMEM((width, rows), bf16),
            pltpu.VMEM((1, units), f32),
            pltpu.VMEM((32, width), f32),
            pltpu.VMEM((8, units), f32),
            pltpu.VMEM((width, size), bf16),
        ],
        grid=(steps,),
        out_specs=(row_block, row_block, row_block, whole(sent), whole(sent)),
        flops=12 * rows * width * units + 6 * rows * width * width,
        micros=30,
        name="feed",
        mib=50,
    )(own, packed, mixed_a, mixed_b, cot, vec, w_t, mine, other)


def side_body(mixed_a, mixed_b, middle_grad, out_grad):
    first = mixed_a.shape[1]
    total = dot(mixed_a[...], middle_grad[:first, :].astype(bf16))
    total += dot(mixed_b[...], middle_grad[first:, :].astype(bf16))
    out_grad[...] = total.T.astype(bf16)


def side_call(mixed_a, mixed_b, middle_grad):
    rows, width = middle_grad.shape
    return kernel_call(
        side_body,
        [VM] * 3,
        (S((width, width), bf16),),
        flops=2 * rows * width * width,
        micros=4,
        name="side",
        mib=20,
    )(mixed_a, mixed_b, middle_grad)[0]


def back_body(
    own, seg, offs, counts, qkv_in, key_in, mixed_in, stats_a, stats_b, seg_rows, seg_cols,
    w_in, packed_in, normed_in, middle_in, out_grad, vec,
    input_out, keep, send,
    qkv, key_t, mixed_grad, w_t, packed, normed_t, middle_grad, input_grad,
    qkv_grad, key_grad, value_grad, stats, sums, sems, late_sems, out_sems,
):
    rows, width = packed.shape
    me = own[0]
    piece = w_t.shape[1]
    size = 512

    def early(i):
        sl = tile_rows(i, size)
        return [
            pltpu.make_async_copy(qkv_in.at[sl, :], qkv.at[sl, :], sems.at[0, i]),
            pltpu.make_async_copy(key_in.at[:, sl], key_t.at[:, sl], sems.at[1, i]),
            pltpu.make_async_copy(mixed_in.at[sl, :], mixed_grad.at[sl, :], sems.at[2, i]),
        ]

    late = [
        pltpu.make_async_copy(source, target, late_sems.at[k])
        for k, (source, target) in enumerate(
            ((w_in, w_t), (packed_in, packed), (middle_in, middle_grad), (normed_in, normed_t))
        )
    ]
    for i in range(rows // size):
        for copy in early(i):
            copy.start()
    for copy in late:
        copy.start()

    def before(j):
        step = size // BLK

        @pl.when(j == 0)
        def _():
            for copy in early(0):
                copy.wait()

        @pl.when(((j + 2) % step == 0) & ((j + 2) // step < rows // size))
        def _():
            for copy in early((j + 2) // step):
                copy.wait()

    attend_back(
        seg, offs, counts, qkv, key_t, mixed_grad, stats_a, stats_b, seg_rows, seg_cols,
        qkv_grad, key_grad, value_grad, stats, before,
    )
    for copy in late:
        copy.wait()
    weights = w_t[: 3 * HALF // 2].reshape(3 * width, width)
    sums[...] = jnp.zeros_like(sums)

    def result(i):
        sl = tile_rows(i, size)
        return pltpu.make_async_copy(input_grad.at[sl, :], input_out.at[sl, :], out_sems.at[i])

    tiles = [slice(i * size, (i + 1) * size) for i in range(rows // size)]
    for sl in tiles:
        qkv_grad[sl, width : 2 * width] = (key_grad[sl, :] * SCALE).astype(bf16)
        qkv_grad[sl, 2 * width :] = value_grad[sl, :].astype(bf16)

    def finish(i, normed_grad):
        sl = tiles[i]
        unit, inverse = norm_parts(packed[sl, :].astype(f32))
        sums[0:8, :] += row_sums(normed_grad * unit)
        sums[8:16, :] += row_sums(normed_grad)
        sums[16:24, :] += row_sums(qkv_grad[sl, :width].astype(f32))
        sums[24:32, :] += row_sums(qkv_grad[sl, 2 * width :].astype(f32))
        input_grad[sl, :] = middle_grad[sl, :] + norm_back(unit, inverse, vec[0:1, :], normed_grad)
        result(i).start()

    def weight_part(lower, wide):
        pieces = dot(normed_t[...], qkv_grad[:, lower : lower + wide]).T.astype(bf16)
        pieces = pieces.reshape(wide // piece, piece, width)
        store_pieces(me, lower // piece, pieces, keep, send, 0, piece, plane_first)

    grads = [dot(qkv_grad[sl, :], weights) for sl in tiles]
    for i in range(len(tiles)):
        if i == 0:
            weight_part(0, 2 * width)
        if i == 2:
            weight_part(2 * width, width)
        finish(i, grads[i])
    pieces = out_grad[...].reshape(width // piece, piece, width)
    store_pieces(me, 3 * width // piece, pieces, keep, send, 0, piece, plane_first)
    lines = [jnp.sum(sums[8 * row : 8 * row + 8, :], axis=0, keepdims=True) for row in range(4)]
    store_extra(lines, keep, send)
    for i in range(rows // size):
        result(i).wait()


def back_call(
    own, seg, offs, counts, qkv, key_t, mixed_grad, stats_a, stats_b, seg_rows, seg_cols,
    w_t, packed, normed_t, middle_grad, out_grad, vec,
):
    rows, width = packed.shape
    sent = S((HALF * w_t.shape[1] + 2 * EXTRA, width), bf16)
    moved = (qkv, key_t, mixed_grad, w_t, packed, normed_t, middle_grad)
    tiles = rows // 512
    return kernel_call(
        back_body,
        [SM] * 4 + [HB] * 3 + [VM] * 4 + [HB] * 4 + [VM] * 2,
        (S((rows, width), f32), sent, sent),
        [pltpu.VMEM(v.shape, v.dtype) for v in moved]
        + [
            pltpu.VMEM((rows, width), f32),
            pltpu.VMEM((rows, 3 * width), bf16),
            pltpu.VMEM((rows, width), f32),
            pltpu.VMEM((rows, width), f32),
            pltpu.VMEM((rows // BLK, HEADS * BLK), f32),
            pltpu.VMEM((32, width), f32),
            pltpu.SemaphoreType.DMA((3, tiles)),
            pltpu.SemaphoreType.DMA((4,)),
            pltpu.SemaphoreType.DMA((tiles,)),
        ],
        flops=22 * rows * width * width,
        micros=30,
        name="back",
        mib=50,
        out_specs=(HB, VM, VM),
    )(
        own, seg, offs, counts, qkv, key_t, mixed_grad, stats_a, stats_b, seg_rows, seg_cols,
        w_t, packed, normed_t, middle_grad, out_grad, vec,
    )


def unpack_body(win, offs, keep, input_grad, image_grads, slots):
    images_here, length = keep.shape
    rows, width = input_grad.shape
    before = lax.broadcasted_iota(jnp.int32, (length, length), 0)
    after = lax.broadcasted_iota(jnp.int32, (length, length), 1)
    tri = jnp.where(before <= after, 1.0, 0.0).astype(bf16)
    place = lax.broadcasted_iota(jnp.int32, (win, length), 0)

    @pl.when(pl.program_id(0) == 0)
    def _():
        kept = keep[...]
        ranks = dot(kept.astype(f32).astype(bf16), tri).astype(jnp.int32) - 1
        slots[...] = jnp.where(kept > 0, ranks, -4 * win)

    chosen, values = [], []
    for k in range(image_grads.shape[0]):
        i = pl.program_id(0) * image_grads.shape[0] + k
        base = pl.multiple_of(jnp.minimum((offs[i] // 8) * 8, rows - win), 8)
        shift = offs[i] - base
        chosen.append(jnp.where(place == slots[pl.ds(i, 1), :] + shift, 1.0, 0.0).astype(bf16))
        values.append(input_grad[pl.ds(base, win), :])
    highs = [value.astype(bf16) for value in values]
    rests = [(value - high.astype(f32)).astype(bf16) for value, high in zip(values, highs)]
    for k in range(image_grads.shape[0]):
        image_grads[k] = dot(chosen[k], highs[k], TN) + dot(chosen[k], rests[k], TN)


def unpack_call(offs, keep, input_grad):
    images_here, length = keep.shape
    rows, width = input_grad.shape
    win = (length + 7 + 7) // 8 * 8
    size = 5
    return kernel_call(
        functools.partial(unpack_body, win),
        [SM, whole(keep.shape), whole(input_grad.shape)],
        (S((images_here, length, width), f32),),
        [pltpu.VMEM((images_here, length), jnp.int32)],
        flops=4 * images_here * win * length * width,
        micros=9,
        name="unpack",
        mib=60,
        grid=(images_here // size,),
        out_specs=(pl.BlockSpec((size, length, width), lambda i: (i, 0, 0)),),
    )(offs, keep, input_grad)[0]


def to_halves(chunks):
    _, size, width = chunks.shape
    ordered = chunks.reshape(4, 4, 2, size, width).transpose(2, 1, 0, 3, 4).reshape(2, HALF * size, width)
    return ordered[0], ordered[1]


def from_halves(keep, send, parts, width, line_first):
    size = keep.shape[0] // HALF // parts
    both = jnp.stack([keep, send]).reshape(2, 4, 4, parts, size, width)
    both = both.transpose((1, 2, 0, 3, 4, 5) if line_first else (2, 1, 0, 3, 4, 5))
    return both.reshape(CHUNKS, parts, size, width)


def adamw(weight, grad, first, second, average, count, rate, decay):
    first_new = BETA_ONE * first + (1.0 - BETA_ONE) * grad
    second_new = BETA_TWO * second + (1.0 - BETA_TWO) * grad * grad
    first_hat = first_new / (1.0 - jnp.power(BETA_ONE, count))
    second_hat = second_new / (1.0 - jnp.power(BETA_TWO, count))
    weight_new = weight - rate * (first_hat / (jnp.sqrt(second_hat) + ADAM_EPS) + decay * weight)
    average_new = AVERAGE_DECAY * average + (1.0 - AVERAGE_DECAY) * weight_new
    return (weight_new, first_new, second_new, average_new)


def wide_of(ref, rows):
    return ref[rows, :].astype(f32)


def whole_extra(ref):
    return wide_of(ref, slice(-2 * EXTRA, -EXTRA)) + wide_of(ref, slice(-EXTRA, None))


def paired(values):
    while len(values) > 1:
        values = [values[i] + values[i + 1] for i in range(0, len(values), 2)]
    return values[0]


def put_extra(values, out, pieces):
    high, low = split_low(values)
    out[-EXTRA:, :] = high.astype(f32) + low.astype(f32)
    for piece in pieces:
        piece[-2 * EXTRA : -EXTRA, :] = high
        piece[-EXTRA:, :] = low


def merge_first_body(ffn_own, ffn_a, ffn_b, ffn_c, attn_own, attn_in, own, *pieces):
    ffn_size, attn_size = (ffn_own.shape[0] - EXTRA) // 4, (attn_own.shape[0] - 2 * EXTRA) // 4
    for part in range(4):
        rows = slice(part * ffn_size, (part + 1) * ffn_size)
        ffn = ffn_own[rows, :] + wide_of(ffn_a, rows) + wide_of(ffn_b, rows) + wide_of(ffn_c, rows)
        rows = slice(part * attn_size, (part + 1) * attn_size)
        attn = wide_of(attn_own, rows) + wide_of(attn_in, rows)
        out = own if part == 0 else pieces[part - 1]
        out[:ffn_size, :] = ffn.astype(out.dtype)
        out[ffn_size : ffn_size + attn_size, :] = attn.astype(out.dtype)
    known = paired([ffn_own[-EXTRA:, :]] + [whole_extra(r) for r in (ffn_a, ffn_b, ffn_c)])
    fresh = whole_extra(attn_own) + whole_extra(attn_in)
    put_extra(jnp.concatenate([fresh[:4], known[:8], fresh[12:]], axis=0), own, pieces)


def merge_first_call(ffn_own, ffn_in, attn_own, attn_in):
    width = ffn_own.shape[1]
    size = (ffn_own.shape[0] - EXTRA) // 4 + (attn_own.shape[0] - 2 * EXTRA) // 4
    out = kernel_call(
        merge_first_body,
        [VM] * 6,
        (S((size + EXTRA, width), f32),) + (S((size + 2 * EXTRA, width), bf16),) * 3,
        micros=3,
        name="merge_first",
    )(ffn_own, *ffn_in, attn_own, attn_in)
    return out[0], out[1:]


def merge_second_body(skip, own, in_a, in_b, in_c, out, *pieces):
    received = (in_a, in_b, in_c)
    size = out.shape[0] - EXTRA
    for part in range(4):
        rows = slice(skip + part * size, skip + (part + 1) * size)
        total = own[rows, :] + wide_of(in_a, rows) + wide_of(in_b, rows) + wide_of(in_c, rows)
        to = out if part == 0 else pieces[part - 1]
        to[:size, :] = total.astype(to.dtype)
    high, low = split_low(paired([own[-EXTRA:, :]] + [whole_extra(r) for r in received]))
    high, low = high.astype(f32), low.astype(f32)
    out[-EXTRA:, :] = high + low
    few = jnp.concatenate([high[: EXTRA // 2], low[: EXTRA // 2]], axis=0).astype(bf16)
    for piece in pieces:
        piece[-EXTRA:, :] = few


def merge_second_call(skip, own, received):
    width = own.shape[1]
    size = (own.shape[0] - EXTRA - skip) // 4
    out = kernel_call(
        functools.partial(merge_second_body, skip),
        [VM] * 4,
        (S((size + EXTRA, width), f32),) + (S((size + EXTRA, width), bf16),) * 3,
        micros=2,
        name="merge_second",
    )(own, *received)
    return out[0], out[1:]


def adamw_with(weight, grad, first, second, average, one, two, rate, decay):
    first_new = BETA_ONE * first + (1.0 - BETA_ONE) * grad
    second_new = BETA_TWO * second + (1.0 - BETA_TWO) * grad * grad
    weight_new = weight - rate * ((first_new / one) / (jnp.sqrt(second_new / two) + ADAM_EPS) + decay * weight)
    average_new = AVERAGE_DECAY * average + (1.0 - AVERAGE_DECAY) * weight_new
    return (weight_new, first_new, second_new, average_new)


def update(powers, states, grad, rate, decay, grad_out, outs, at=slice(None)):
    held = [ref[at] for ref in states]
    grad_out[at] = grad
    for ref, value in zip(outs, adamw_with(held[0], grad, *held[1:], powers[0], powers[1], rate, decay)):
        ref[at] = value


def finish_ffn_body(me, powers, own, in_a, in_b, in_c, *refs):
    states, outs = refs[:8], refs[8:]
    _, piece, width = states[0].shape
    received = (in_a, in_b, in_c)
    for k in range(2):
        rows = slice(k * piece, (k + 1) * piece)
        grad = own[rows, :] + wide_of(in_a, rows) + wide_of(in_b, rows) + wide_of(in_c, rows)
        update(powers, states[:4], grad, MATRIX_RATE, WEIGHT_DECAY, outs[0], outs[2:6], k)
    sums = paired([own[-EXTRA:, :]] + [whole_extra(r) for r in received])
    across = width // piece
    row = lax.broadcasted_iota(jnp.int32, (EXTRA, width), 0)
    line = jnp.sum(jnp.where(row == 8 + me[0] // across, sums, 0.0), axis=0, keepdims=True)
    line = jnp.broadcast_to(line, (8, width))
    shift = (me[0] % across) * piece
    line = jnp.where(shift == 0, line, pltpu.roll(line, width - shift, 1))
    update(powers, states[4:], line[:1, :piece], VECTOR_RATE, 0.0, outs[1], outs[6:])


def finish_ffn_call(me, powers, own, received, states):
    kinds = [S(states[k].shape, f32) for k in (0, 4)]
    out = kernel_call(
        finish_ffn_body,
        [SM, SM] + [VM] * 12,
        tuple(kinds) + tuple(kind for kind in kinds for _ in range(4)),
        micros=2,
        name="finish_ffn",
    )(me, powers, own, *received, *states)
    return out[0], out[1], out[2:6], out[6:]


def finish_attn_body(powers, own, in_a, in_b, in_c, *refs):
    states, outs = refs[:8], refs[8:]
    piece = states[0].shape[0]
    rows = slice(0, piece)
    grad = own[rows, :] + wide_of(in_a, rows) + wide_of(in_b, rows) + wide_of(in_c, rows)
    update(powers, states[:4], grad, MATRIX_RATE, WEIGHT_DECAY, outs[0], outs[2:6])
    few = [wide_of(r, slice(-EXTRA, None)) for r in (in_a, in_b, in_c)]
    sums = paired([own[-EXTRA : -EXTRA // 2, :]] + [v[: EXTRA // 2] + v[EXTRA // 2 :] for v in few])
    vec = jnp.concatenate([sums[:4], own[-EXTRA + 4 : -EXTRA + 8, :]], axis=0)
    update(powers, states[4:], vec, VECTOR_RATE, 0.0, outs[1], outs[6:])


def finish_attn_call(powers, own, received, states):
    kinds = [S(states[k].shape, f32) for k in (0, 4)]
    out = kernel_call(
        finish_attn_body,
        [SM] + [VM] * 12,
        tuple(kinds) + tuple(kind for kind in kinds for _ in range(4)),
        micros=2,
        name="finish_attn",
    )(powers, own, *received, *states)
    return out[0], out[1], out[2:6], out[6:]


def body(
    images, keep_mask, kept_counts, pack_offsets, segment_ids, cotangent,
    attn_weight, ffn_weight, up_bias, vectors,
    attn_first, ffn_first, bias_first, vec_first,
    attn_second, ffn_second, bias_second, vec_second,
    attn_average, ffn_average, bias_average, vec_average, step,
):
    width = images.shape[2]
    rows = segment_ids.shape[0]
    both = ("dp", "mp")
    piece = attn_weight.shape[1]
    tree = lax.axis_size("dp") == 8 and lax.axis_size("mp") == 4
    seg_rows = segment_ids.reshape(rows // BLK, BLK)
    placed = place_call(images, keep_mask, pack_offsets, rows)
    count = step[0].astype(f32)
    powers = jnp.stack([1.0 - jnp.power(BETA_ONE, count), 1.0 - jnp.power(BETA_TWO, count)])
    if tree:
        own = (lax.axis_index("dp") * 4 + lax.axis_index("mp")).astype(jnp.int32)[None]
        pieces = pieces_call(attn_weight.T, jnp.swapaxes(ffn_weight, 1, 2), up_bias[None, :])
        lines = [pieces] + [over_line(pieces, k) for k in (1, 2, 3)]
        placed, *lines = tie(placed, *lines)
        attn_line = jnp.concatenate([line[:piece] for line in lines], axis=0)
        ffn_line = jnp.concatenate([line[piece:] for line in lines], axis=0)
        attn_mine = gather_plane(attn_line)
        normed, normed_t, seg_cols = norm_call(placed, seg_rows, vectors)
        attn_mine, normed, ffn_line = tie(attn_mine, normed, ffn_line)
        attn_other = over_core(attn_mine)
        ffn_lines = [ffn_line] + [over_plane(ffn_line, k) for k in (1, 2, 3)]
    else:
        own = jnp.zeros((1,), jnp.int32)
        attn_all = lax.all_gather(attn_weight.astype(bf16).T, both, axis=0, tiled=True)
        ffn_all = lax.all_gather(jnp.swapaxes(ffn_weight.astype(bf16), 1, 2), both, axis=1, tiled=True)
        bias_all = lax.all_gather(up_bias.astype(bf16), both, axis=0, tiled=True)
        size = 4 * width // CHUNKS
        ffn_all = jnp.concatenate(
            [
                ffn_all[0].reshape(CHUNKS, size, width),
                ffn_all[1].reshape(CHUNKS, size, width),
                jnp.pad(bias_all.reshape(CHUNKS, 1, size), ((0, 0), (0, 15), (0, width - size))),
            ],
            axis=1,
        )
        attn_mine, attn_other = to_halves(attn_all.reshape(CHUNKS, size, width))
        ffn_mine, ffn_other = to_halves(ffn_all)
        normed, normed_t, seg_cols = norm_call(placed, seg_rows, vectors)
    where = (segment_ids, pack_offsets, kept_counts)
    blocks = rows // BLK
    late = blocks // 4
    qkv, key_t, value_t, w_t, mixed_a, stats_a = attend_first_call(
        blocks - late, own, *where, normed, attn_mine, attn_other, vectors, seg_rows, seg_cols
    )
    if tree:
        qkv, mixed_a, *ffn_lines = tie(qkv, mixed_a, *ffn_lines)
        ffn_mine = jnp.concatenate(ffn_lines, axis=0)
        ffn_other = over_core(ffn_mine)
    mixed_b, stats_b = attend_last_call(late, *where, qkv, value_t, seg_rows, seg_cols)
    if tree:
        mixed_b, ffn_mine, ffn_other = tie(mixed_b, ffn_mine, ffn_other)
    layer_out, middle_grad, mixed_grad, ffn_keep, ffn_send = feed_call(
        own, placed, mixed_a, mixed_b, cotangent, vectors, w_t, ffn_mine, ffn_other
    )
    if tree:
        ffn_in = over_core(ffn_send)
    out_grad = side_call(mixed_a, mixed_b, middle_grad)
    if tree:
        out_grad, ffn_in = tie(out_grad, ffn_in)
        ffn_own, *ffn_out = combine_call(ffn_keep, [ffn_in], 4, EXTRA)
        out_grad, ffn_own, *ffn_out = tie(out_grad, ffn_own, *ffn_out)
        ffn_in = [over_line(p, k + 1) for k, p in enumerate(ffn_out)]
    input_grad, attn_keep, attn_send = back_call(
        own, *where, qkv, key_t, mixed_grad, stats_a, stats_b, seg_rows, seg_cols,
        w_t, placed, normed_t, middle_grad, out_grad, vectors,
    )
    index = lax.axis_index("dp") * lax.axis_size("mp") + lax.axis_index("mp")
    if tree:
        input_grad, attn_send, *ffn_in = tie(input_grad, attn_send, *ffn_in)
        attn_in = over_core(attn_send)
        states = [v.T for v in (attn_weight, attn_first, attn_second, attn_average)]
        states += [vectors, vec_first, vec_second, vec_average]
        ffn_states = [jnp.swapaxes(v, 1, 2) for v in (ffn_weight, ffn_first, ffn_second, ffn_average)]
        ffn_states += [v[None, :] for v in (up_bias, bias_first, bias_second, bias_average)]
        merged, pieces = merge_first_call(ffn_own, ffn_in, attn_keep, attn_in)
        input_grad, *pieces = tie(input_grad, *pieces)
        received = [over_plane(p, k + 1) for k, p in enumerate(pieces)]
        image_grads = unpack_call(pack_offsets, keep_mask, input_grad)
        image_grads, *received = tie(image_grads, *received)
        attn_own, pieces = merge_second_call(2 * piece, merged, received)
        image_grads, merged, *pieces = tie(image_grads, merged, *pieces)
        last = [over_line(p, k + 1) for k, p in enumerate(pieces)]
        ffn_grad, bias_grad, ffn_up, bias_up = finish_ffn_call(own, powers, merged, received, ffn_states)
        image_grads, ffn_grad, *last = tie(image_grads, ffn_grad, *last)
        attn_grad, vec_grad, attn_up, vec_up = finish_attn_call(powers, attn_own, last, states)
        attn_grad, ffn_grad, bias_grad = attn_grad.T, jnp.swapaxes(ffn_grad, 1, 2), bias_grad[0]
        attn_up, ffn_up = [v.T for v in attn_up], [jnp.swapaxes(v, 1, 2) for v in ffn_up]
        bias_up = [v[0] for v in bias_up]
    else:
        image_grads = unpack_call(pack_offsets, keep_mask, input_grad)
        base = ffn_keep.shape[0] - 2 * EXTRA
        ffn_t = from_halves(ffn_keep[:base], ffn_send[:base], 2, width, True)
        ffn_t = jnp.swapaxes(ffn_t, 0, 1).reshape(2, 4 * width, width)
        ffn_t = lax.psum_scatter(ffn_t.astype(f32), both, scatter_dimension=1, tiled=True)
        ffn_grad = jnp.swapaxes(ffn_t, 1, 2)
        known = ffn_keep[base : base + EXTRA].astype(f32) + ffn_keep[base + EXTRA :].astype(f32)
        base = attn_keep.shape[0] - 2 * EXTRA
        attn_t = from_halves(attn_keep[:base], attn_send[:base], 1, width, False).reshape(4 * width, width)
        attn_grad = lax.psum_scatter(attn_t.astype(f32), both, scatter_dimension=0, tiled=True).T
        sums = attn_keep[base : base + EXTRA].astype(f32) + attn_keep[base + EXTRA :].astype(f32)
        sums = lax.psum(jnp.concatenate([sums[:4], known[:8]], axis=0), both)
        vec_grad, bias_sums = sums[:8], sums[8:]
        bias_grad = lax.dynamic_slice_in_dim(bias_sums.reshape(4 * width), index * piece, piece, 0)
        attn_up = adamw(attn_weight, attn_grad, attn_first, attn_second, attn_average, count, MATRIX_RATE, WEIGHT_DECAY)
        vec_up = adamw(vectors, vec_grad, vec_first, vec_second, vec_average, count, VECTOR_RATE, 0.0)
        ffn_up = adamw(ffn_weight, ffn_grad, ffn_first, ffn_second, ffn_average, count, MATRIX_RATE, WEIGHT_DECAY)
        bias_up = adamw(up_bias, bias_grad, bias_first, bias_second, bias_average, count, VECTOR_RATE, 0.0)
    news = [part[k] for k in range(4) for part in (attn_up, ffn_up, bias_up, vec_up)]
    return (layer_out, image_grads, attn_grad, ffn_grad, bias_grad, vec_grad, *news)


def solution(mesh):
    both = ("dp", "mp")
    matrix, slab, line = P(None, both), P(None, None, both), P(both)
    states = (matrix, slab, line, P())
    return jax.shard_map(
        body,
        mesh=mesh,
        in_specs=(P(both, None, None), P(both, None), line, line, line, P(both, None), *states * 4, P()),
        out_specs=(P(both, None), P(both, None, None), *states, *states * 4),
        check_vma=False,
    )
```
